32 devices in a mesh: dp: 16 (over z, x, core), tensor: 2 (over y).
Axes of the slice: x: 2, y: 2, z: 4, core: 2. Of those that a mesh axis runs over, the one named last changes fastest.
Arguments:
- tokens: bfloat16 [12288, 2048], P(('dp', 'tensor')), may hold values from -6 to 6
- segments: int32 [16, 768], P('dp'), may hold values from 0 to 6, as said below
- q_weight: bfloat16 [2048, 2048], P('dp', 'tensor'), may hold values from -0.125 to 0.125
- k_weight: bfloat16 [2048, 256], P('dp', 'tensor'), may hold values from -0.125 to 0.125
- v_weight: bfloat16 [2048, 256], P('dp', 'tensor'), may hold values from -0.125 to 0.125
- o_weight: bfloat16 [2048, 2048], P('dp', 'tensor'), may hold values from -0.375 to 0.375
- attention_gain: float32 [2048], replicated, may hold values from 0.5 to 1.5
- gate_weight: bfloat16 [2048, 5632], P('dp', 'tensor'), may hold values from -0.125 to 0.125
- up_weight: bfloat16 [2048, 5632], P('dp', 'tensor'), may hold values from -0.125 to 0.125
- down_weight: bfloat16 [2048, 5632], P('dp', 'tensor'), may hold values from -0.109375 to 0.109375
- feed_gain: float32 [2048], replicated, may hold values from 0.5 to 1.5
- out_grad: bfloat16 [12288, 2048], P(('dp', 'tensor')), may hold values from -6 to 6
Outputs:
- block_out: bfloat16 [12288, 2048], P(('dp', 'tensor'))
- input_grad: bfloat16 [12288, 2048], P(('dp', 'tensor'))
- q_weight_grad: float32 [2048, 2048], P('dp', 'tensor')
- k_weight_grad: float32 [2048, 256], P('dp', 'tensor')
- v_weight_grad: float32 [2048, 256], P('dp', 'tensor')
- o_weight_grad: float32 [2048, 2048], P('dp', 'tensor')
- attention_gain_grad: float32 [2048], replicated
- gate_weight_grad: float32 [2048, 5632], P('dp', 'tensor')
- up_weight_grad: float32 [2048, 5632], P('dp', 'tensor')
- down_weight_grad: float32 [2048, 5632], P('dp', 'tensor')
- feed_gain_grad: float32 [2048], replicated
The draws below stay inside these ranges and needn't reach their ends.
Inputs may be any that keep to these rules, and one draw needn't show every extreme that they name: `segments`: along each row the numbers never fall, begin at 0 and end at 6; the document holding places 768 / 2 - 1 and 384 of a row runs over more than 2 * (96) tokens.
All inputs are finite; a program needn't handle non-finite values.
Results may differ from the reference program's by a relative error of at most 0.015.
Values may be sent and summed in bfloat16 or wider, within the bound.
No kernel may reach another device: no remote copies, remote signals or barrier semaphores. Data moves between devices by JAX's collectives and lax.ppermute only.
A program may use at most 160 MiB of HBM per device.

```python
import jax
import jax.numpy as jnp
from jax import lax

D = 2048
HEADS = 32
KV_HEADS = 4
HEAD_DIM = 64
FF = 5632
SEQ = 768
GROUPS = 16
TOKENS = 12288
QD = 2048
KVD = 256


def draw_segments(key, part):
    key = jax.random.fold_in(key, 11)
    margin = SEQ // 8
    cut_points = jax.random.randint(key, (GROUPS, 6), 1, SEQ - 2 * margin - 1)
    cut_points = jnp.where(cut_points >= SEQ // 2 - margin, cut_points + 2 * margin + 1, cut_points)
    places = jnp.arange(SEQ, dtype=jnp.int32)
    return jnp.sum((cut_points[:, None, :] <= places[None, :, None]).astype(jnp.int32), axis=2)


def block_scale(key, extent, split, least, high):
    def one(axis_at, blocks):
        draws = jax.random.uniform(jax.random.fold_in(jax.random.fold_in(key, 6), axis_at), (blocks,), jnp.float32, least / len(split), high / len(split))
        return jnp.repeat(jnp.exp(draws), extent[axis_at] // blocks).reshape((-1,) + (1,) * (len(extent) - axis_at - 1))

    loudness = one(*split[0])
    for cut in split[1:]:
        loudness = loudness * one(*cut)
    return loudness


def bell_draw(rng, shape, scale, limit, shards=(), held_as=jnp.bfloat16):
    values = jax.random.normal(rng, shape, jnp.float32) * scale
    if len(shards) > 0:
        values = block_scale(rng, shape, shards, -0.22, 0.18) * values
    return jnp.clip(values, min=-limit, max=limit).astype(held_as)


def setup_inputs(seed: int = 0) -> dict:
    seeds = jax.random.split(jax.random.key(seed), 13)
    return {
        "tokens": bell_draw(seeds[0], (TOKENS, D), 1.0, 6.0, ((0, 32),)),
        "segments": draw_segments(jax.random.fold_in(seeds[12], 71), 0),
        "q_weight": bell_draw(seeds[2], (D, QD), D ** -0.5, 0.125, ((0, 16), (1, 2))),
        "k_weight": bell_draw(seeds[3], (D, KVD), D ** -0.5, 0.125, ((0, 16), (1, 2))),
        "v_weight": bell_draw(seeds[4], (D, KVD), D ** -0.5, 0.125, ((0, 16), (1, 2))),
        "o_weight": bell_draw(seeds[5], (D, QD), (QD // 8) ** -0.5, 0.375, ((0, 16), (1, 2))),
        "attention_gain": jnp.clip(1.0 + 0.1 * jax.random.normal(seeds[6], (D,), jnp.float32), 0.5, 1.5),
        "gate_weight": bell_draw(seeds[7], (D, FF), D ** -0.5, 0.125, ((0, 16), (1, 2))),
        "up_weight": bell_draw(seeds[8], (D, FF), D ** -0.5, 0.125, ((0, 16), (1, 2))),
        "down_weight": bell_draw(seeds[9], (D, FF), (FF // 2) ** -0.5, 0.109375, ((0, 16), (1, 2))),
        "feed_gain": jnp.clip(1.0 + 0.1 * jax.random.normal(seeds[10], (D,), jnp.float32), 0.5, 1.5),
        "out_grad": bell_draw(seeds[11], (TOKENS, D), 1.0, 6.0, ((0, 32),)),
    }


@jax.custom_vjp
def low(v):
    return lax.optimization_barrier(v.astype(jnp.bfloat16)).astype(jnp.float32)

@jax.custom_vjp
def low_back(v):
    return v

def low_keep(v):
    return (low(v), None)

def low_pass(kept, grad):
    return (grad,)

def back_keep(v):
    return (v, None)

def back_low(kept, grad):
    return (low(grad),)
low.defvjp(low_keep, low_pass)
low_back.defvjp(back_keep, back_low)
epsilon = 1e-05
rope_base = 10000.0
highest = lax.Precision.HIGHEST

def product(left_side, right_side):
    return jnp.dot(left_side, right_side, precision=highest)

def product_trans(left_side, right_side):
    return jnp.dot(left_side, right_side.T, precision=highest)

def rotary_tables(segment_row):
    length = segment_row.shape[0]
    before = lax.optimization_barrier(jnp.sum((segment_row[None, :] < segment_row[:, None]).astype(jnp.int32), axis=1))
    places = (jnp.arange(length, dtype=jnp.int32) - before).astype(jnp.float32)
    half_dim = HEAD_DIM // 2
    frequency = rope_base ** (-2.0 * jnp.arange(half_dim).astype(jnp.float32) / HEAD_DIM)
    angles = places[:, None] * frequency[None, :]
    return (jnp.cos(angles)[:, None, :], jnp.sin(angles)[:, None, :])

def rotate(vectors, cosine_table, sine_table):
    half_dim = vectors.shape[-1] // 2
    first_half = vectors[..., :half_dim]
    second = vectors[..., half_dim:]
    return jnp.concatenate([first_half * cosine_table - second * sine_table, second * cosine_table + first_half * sine_table], axis=-1)

def rms_norm(activity, gain_vec):
    inverse = lax.rsqrt(lax.optimization_barrier(jnp.mean(activity * activity, axis=-1, keepdims=True)) + epsilon)
    return activity * inverse * gain_vec

def forward(inputs, q_weight, k_weight, v_weight, o_weight, attention_gain, gate_weight, up_weight, down_weight, feed_gain, segment_row):
    length = inputs.shape[0]
    group_size = HEADS // KV_HEADS
    cosine_table, sine_table = rotary_tables(segment_row)
    normed = low(rms_norm(inputs, attention_gain))
    query_lin = low_back(product(normed, q_weight)).reshape(length, HEADS, HEAD_DIM)
    key_lin = low_back(product(normed, k_weight)).reshape(length, KV_HEADS, HEAD_DIM)
    values = low(low_back(product(normed, v_weight))).reshape(length, KV_HEADS, HEAD_DIM)
    queries = low(rotate(query_lin, cosine_table, sine_table)).reshape(length, KV_HEADS, group_size, HEAD_DIM)
    key_rot = low(rotate(key_lin, cosine_table, sine_table))
    places = jnp.arange(length)
    allowed = (segment_row[:, None] == segment_row[None, :]) & (places[:, None] >= places[None, :])
    raw_scores = jnp.einsum('qkgd,skd->kgqs', queries, key_rot, precision=highest)
    scores = jnp.where(allowed, low_back(raw_scores) * HEAD_DIM ** (-0.5), -1e+30)
    row_max = lax.optimization_barrier(jnp.max(scores, axis=-1, keepdims=True))
    powers = jnp.exp(scores - row_max)
    attend_prob = low(powers / lax.optimization_barrier(jnp.sum(powers, axis=-1, keepdims=True)))
    heads_out = jnp.einsum('kgqs,skd->qkgd', attend_prob, values, precision=highest).reshape(length, HEADS * HEAD_DIM)
    mixed_heads = low(low_back(heads_out))
    middle = inputs + low_back(product_trans(mixed_heads, o_weight))
    normed_feed = low(rms_norm(middle, feed_gain))
    gate_value = low_back(product(normed_feed, gate_weight))
    up_value = low_back(product(normed_feed, up_weight))
    hidden = low(jax.nn.silu(gate_value) * up_value)
    return middle + product_trans(hidden, down_weight)

def reference(tokens, segments, q_weight, k_weight, v_weight, o_weight, attention_gain, gate_weight, up_weight, down_weight, feed_gain, out_grad):
    params = (q_weight.astype(jnp.float32), k_weight.astype(jnp.float32), v_weight.astype(jnp.float32), o_weight.astype(jnp.float32), attention_gain.astype(jnp.float32), gate_weight.astype(jnp.float32), up_weight.astype(jnp.float32), down_weight.astype(jnp.float32), feed_gain.astype(jnp.float32))
    inputs_all = tokens.astype(jnp.float32).reshape(GROUPS, SEQ, D)
    grads_all = out_grad.astype(jnp.float32).reshape(GROUPS, SEQ, D)

    def one_sequence(running, sequence_item):
        inputs, segment_row, cotangent = sequence_item

        def local_forward(activity, *weights):
            return forward(activity, *weights, segment_row)
        result, pullback = jax.vjp(local_forward, inputs, *params)
        pulled = pullback(cotangent)
        running = tuple((summed_grad + fresh_grad for summed_grad, fresh_grad in zip(running, pulled[1:])))
        return (running, (result, pulled[0]))
    initial = tuple((jnp.zeros(weight_arr.shape, jnp.float32) for weight_arr in params))
    totals, (results, input_grads) = lax.scan(one_sequence, initial, (inputs_all, segments, grads_all))
    query_grad, key_grad, value_grad, output_grad, attention_gain_grad, gate_grad, up_grad, down_grad, feed_gain_grad = totals
    return (results.reshape(TOKENS, D).astype(jnp.bfloat16), input_grads.reshape(TOKENS, D).astype(jnp.bfloat16), query_grad, key_grad, value_grad, output_grad, attention_gain_grad, gate_grad, up_grad, down_grad, feed_gain_grad)
```

```python
import functools

import jax
import jax.numpy as jnp
from jax import lax
from jax.experimental import pallas as pl
from jax.experimental.pallas import tpu as pltpu
from jax.sharding import Mesh, PartitionSpec as P

HEAD_DIM = 64
SWAP = ((0, 1), (1, 0))
QUERIES = 256
VMEM = 40 * 2**20
epsilon = 1e-05
rope_base = 10000.0
bf16 = jnp.bfloat16
f32 = jnp.float32


def dot_plain(left, right):
    return jnp.dot(left, right, preferred_element_type=f32)


def dot_trans(left, right):
    return lax.dot_general(left, right, (((1,), (1,)), ((), ())), preferred_element_type=f32)


def dot_inner(left, right):
    return lax.dot_general(left, right, (((0,), (0,)), ((), ())), preferred_element_type=f32)


def rotary_tables(segment_row):
    length = segment_row.shape[0]
    before = jnp.sum((segment_row[None, :] < segment_row[:, None]).astype(jnp.int32), axis=1)
    places = (jnp.arange(length, dtype=jnp.int32) - before).astype(f32)
    half_dim = HEAD_DIM // 2
    frequency = rope_base ** (-2.0 * jnp.arange(half_dim).astype(f32) / HEAD_DIM)
    angles = places[:, None] * frequency[None, :]
    cosine, sine = jnp.cos(angles), jnp.sin(angles)
    return (jnp.concatenate([cosine] * 4, axis=1), jnp.concatenate([-sine, sine] * 2, axis=1))


def first_blocks(segment_row):
    starts, ends = segment_row[::QUERIES], segment_row[QUERIES - 1 :: QUERIES]
    return jnp.sum((ends[None, :] < starts[:, None]).astype(jnp.int32), axis=1)


def inverse_rms(activity):
    return lax.rsqrt(jnp.mean(activity * activity, axis=-1, keepdims=True) + epsilon)


def norm_back(activity, inverse, gain_vec, incoming):
    scaled = incoming * gain_vec
    return inverse * scaled - activity * (inverse * inverse * inverse) * jnp.mean(
        scaled * activity, axis=-1, keepdims=True
    )


def lanes_of(shape):
    return lax.broadcasted_iota(jnp.int32, shape, len(shape) - 1)


def turn(block, cosine, sine):
    low_half = lanes_of(block.shape) % HEAD_DIM < HEAD_DIM // 2
    other = jnp.where(low_half, pltpu.roll(block, 96, 1), pltpu.roll(block, 32, 1))
    return block * cosine + other * sine


def rope_kernel(rotated, qkv_ref, cos_ref, sin_ref, out_ref):
    block = qkv_ref[...]

    @pl.when(pl.program_id(0) < rotated)
    def _():
        out_ref[...] = turn(block, cos_ref[...], sin_ref[...]).astype(bf16)

    @pl.when(pl.program_id(0) >= rotated)
    def _():
        out_ref[...] = block.astype(bf16)


def rope(qkv, cosine, sine, rotated):
    length, width = qkv.shape
    block = pl.BlockSpec((length, 128), lambda j: (0, j))
    table = pl.BlockSpec((length, 128), lambda j: (0, 0))
    return pl.pallas_call(
        functools.partial(rope_kernel, rotated),
        grid=(width // 128,),
        in_specs=[block, table, table],
        out_specs=block,
        out_shape=jax.ShapeDtypeStruct((length, width), bf16),
        compiler_params=pltpu.CompilerParams(vmem_limit_bytes=VMEM),
        cost_estimate=pl.CostEstimate(
            flops=4 * length * width, bytes_accessed=6 * length * width, transcendentals=0
        ),
    )(qkv, cosine, sine)


def widen(pair_ref, wide_ref, group):
    pair = pair_ref[...]
    keep = (lanes_of(pair.shape) < HEAD_DIM) == (group == 0)
    half = jnp.where(keep, pair, pltpu.roll(pair.astype(f32), HEAD_DIM, 1).astype(bf16))
    wide_ref[:, :128] = half
    wide_ref[:, 128:] = half


def seen_bias(col_ref, row_ref, start, keys, step):
    queries = col_ref.shape[0]
    same = col_ref[...] == row_ref[:, pl.ds(start, keys)]
    q_at = lax.broadcasted_iota(jnp.int32, (queries, keys), 0) + step * queries
    k_at = lax.broadcasted_iota(jnp.int32, (queries, keys), 1) + start
    return jnp.where(same & (q_at >= k_at), 0.0, -1e30).astype(f32)


def forward_kernel(scale, low_ref, q_ref, k_ref, v_ref, col_ref, row_ref, o_ref, lse_ref, kw_ref, vw_ref):
    group, step = pl.program_id(0), pl.program_id(1)
    queries = q_ref.shape[0]

    @pl.when(step == 0)
    def _():
        widen(k_ref, kw_ref, group)
        widen(v_ref, vw_ref, group)

    def run(blocks):
        keys = blocks * queries
        start = pl.multiple_of(low_ref[step] * queries, queries)
        bias = seen_bias(col_ref, row_ref, start, keys, step)
        key = kw_ref[pl.ds(start, keys), :]
        value = vw_ref[pl.ds(start, keys), :]
        head_of = lanes_of((queries, 256)) // HEAD_DIM
        lse = jnp.zeros((queries, 128), f32)
        for quad in range(q_ref.shape[1] // 256):
            wide = q_ref[:, quad * 256 : quad * 256 + 256]
            out = jnp.zeros((queries, 256), f32)
            for j in range(4):
                one = jnp.where(head_of == j, wide, jnp.zeros_like(wide))
                scores = dot_trans(one, key) * scale + bias
                top = jnp.max(scores, axis=1, keepdims=True)
                powers = jnp.exp(scores - top)
                sums = jnp.sum(powers, axis=1, keepdims=True)
                prob = (powers * (1.0 / sums)).astype(bf16)
                out = jnp.where(head_of == j, dot_plain(prob, value), out)
                lse = jnp.where(lanes_of(lse.shape) == quad * 4 + j, top + jnp.log(sums), lse)
            o_ref[:, quad * 256 : quad * 256 + 256] = out.astype(bf16)
        lse_ref[...] = lse

    for blocks in range(1, row_ref.shape[1] // queries + 1):
        pl.when(step + 1 - low_ref[step] == blocks)(functools.partial(run, blocks))


def backward_kernel(
    scale, low_ref, q_ref, k_ref, v_ref, g_ref, lse_ref, col_ref, row_ref, cos_ref, sin_ref, kcos_ref, ksin_ref,
    dq_ref, dk_ref, dv_ref, kw_ref, vw_ref, dkw_ref, dvw_ref,
):
    group, step = pl.program_id(0), pl.program_id(1)
    queries = q_ref.shape[0]

    @pl.when(step == 0)
    def _():
        widen(k_ref, kw_ref, group)
        widen(v_ref, vw_ref, group)
        dkw_ref[...] = jnp.zeros_like(dkw_ref)
        dvw_ref[...] = jnp.zeros_like(dvw_ref)

    def run(blocks):
        keys = blocks * queries
        start = pl.multiple_of(low_ref[step] * queries, queries)
        bias = seen_bias(col_ref, row_ref, start, keys, step)
        key = kw_ref[pl.ds(start, keys), :]
        value = vw_ref[pl.ds(start, keys), :]
        head_of = lanes_of((queries, 256)) // HEAD_DIM
        cosine, sine = cos_ref[...], sin_ref[...]
        for quad in range(q_ref.shape[1] // 256):
            wide = q_ref[:, quad * 256 : quad * 256 + 256]
            grads = g_ref[:, quad * 256 : quad * 256 + 256]
            out = jnp.zeros((queries, 256), f32)
            for j in range(4):
                at = quad * 4 + j
                one = jnp.where(head_of == j, wide, jnp.zeros_like(wide))
                grad = jnp.where(head_of == j, grads, jnp.zeros_like(grads))
                prob = jnp.exp(dot_trans(one, key) * scale + bias - lse_ref[:, at : at + 1])
                prob_grad = dot_trans(grad, value)
                centre = jnp.sum(prob * prob_grad, axis=1, keepdims=True)
                score_grad = (prob * (prob_grad - centre) * scale).astype(bf16)
                dvw_ref[pl.ds(start, keys), :] += dot_inner(prob.astype(bf16), grad)
                dkw_ref[pl.ds(start, keys), :] += dot_inner(score_grad, one)
                out = jnp.where(head_of == j, dot_plain(score_grad, key), out)
            for half in range(2):
                piece = turn(out[:, half * 128 : half * 128 + 128], cosine, -sine)
                dq_ref[:, quad * 256 + half * 128 : quad * 256 + half * 128 + 128] = piece.astype(bf16)

    for blocks in range(1, row_ref.shape[1] // queries + 1):
        pl.when(step + 1 - low_ref[step] == blocks)(functools.partial(run, blocks))

    @pl.when(step == pl.num_programs(1) - 1)
    def _():
        mine = (lanes_of(dk_ref.shape) < HEAD_DIM) == (group == 0)

        def fold(ref):
            pair = ref[:, :128] + ref[:, 128:]
            return pair + pltpu.roll(pair, HEAD_DIM, 1)

        dk = turn(fold(dkw_ref), kcos_ref[...], -ksin_ref[...]).astype(bf16)
        dk_ref[...] = jnp.where(mine, dk, dk_ref[...])
        dv_ref[...] = jnp.where(mine, fold(dvw_ref).astype(bf16), dv_ref[...])


def attention_specs(length, queries, wide):
    at = lambda g, i, low: (i, g)
    pair = lambda first: pl.BlockSpec((length, 128), lambda g, i, low: (0, first))
    col = pl.BlockSpec((queries, 1), lambda g, i, low: (i, 0))
    row = pl.BlockSpec((1, length), lambda g, i, low: (0, 0))
    return pl.BlockSpec((queries, wide), at), pair, col, row


def attend(rotated, query_width, first_seen, segment_row, scale):
    length = rotated.shape[0]
    queries = length // first_seen.shape[0]
    groups = 2
    wide = query_width // groups
    heads, pair, col, row = attention_specs(length, queries, wide)
    first = query_width // 128
    return pl.pallas_call(
        functools.partial(forward_kernel, scale),
        grid_spec=pltpu.PrefetchScalarGridSpec(
            num_scalar_prefetch=1,
            grid=(groups, length // queries),
            in_specs=[heads, pair(first), pair(first + 1), col, row],
            out_specs=[heads, pl.BlockSpec((queries, 128), lambda g, i, low: (i, g))],
            scratch_shapes=[pltpu.VMEM((length, 256), bf16), pltpu.VMEM((length, 256), bf16)],
        ),
        out_shape=[
            jax.ShapeDtypeStruct((length, query_width), bf16),
            jax.ShapeDtypeStruct((length, groups * 128), f32),
        ],
        compiler_params=pltpu.CompilerParams(vmem_limit_bytes=VMEM),
        cost_estimate=pl.CostEstimate(
            flops=10 * length * length * query_width, bytes_accessed=4 * length * query_width,
            transcendentals=0,
        ),
    )(first_seen, rotated, rotated, rotated, segment_row.reshape(length, 1), segment_row.reshape(1, length))


def attend_back(rotated, grads, lse, query_width, first_seen, segment_row, cosine, sine, scale):
    length = rotated.shape[0]
    queries = length // first_seen.shape[0]
    groups = 2
    wide = query_width // groups
    heads, pair, col, row = attention_specs(length, queries, wide)
    first = query_width // 128
    table = pl.BlockSpec((queries, 128), lambda g, i, low: (i, 0))
    return pl.pallas_call(
        functools.partial(backward_kernel, scale),
        grid_spec=pltpu.PrefetchScalarGridSpec(
            num_scalar_prefetch=1,
            grid=(groups, length // queries),
            in_specs=[
                heads, pair(first), pair(first + 1), heads,
                pl.BlockSpec((queries, 128), lambda g, i, low: (i, g)),
                col, row, table, table, pair(0), pair(0),
            ],
            out_specs=[heads, pair(0), pair(0)],
            scratch_shapes=[
                pltpu.VMEM((length, 256), bf16), pltpu.VMEM((length, 256), bf16),
                pltpu.VMEM((length, 256), f32), pltpu.VMEM((length, 256), f32),
            ],
        ),
        out_shape=[
            jax.ShapeDtypeStruct((length, query_width), bf16),
            jax.ShapeDtypeStruct((length, 128), bf16),
            jax.ShapeDtypeStruct((length, 128), bf16),
        ],
        compiler_params=pltpu.CompilerParams(vmem_limit_bytes=VMEM),
        cost_estimate=pl.CostEstimate(
            flops=30 * length * length * query_width, bytes_accessed=8 * length * query_width,
            transcendentals=0,
        ),
    )(
        first_seen, rotated, rotated, rotated, grads, lse,
        segment_row.reshape(length, 1), segment_row.reshape(1, length), cosine, sine, cosine, sine,
    )


def make_shards(outer):
    def relative(array):
        rows, width = array.shape
        blocks = array.reshape(rows, outer, 2, 2, width // (4 * outer))
        blocks = jnp.where(lax.axis_index("x") == 0, blocks, blocks[:, :, ::-1])
        blocks = jnp.where(lax.axis_index("core") == 0, blocks, blocks[:, :, :, ::-1])
        return blocks.transpose(0, 3, 2, 1, 4).reshape(rows, width)

    def natural(array):
        rows, width = array.shape
        blocks = array.reshape(rows, 2, 2, outer, width // (4 * outer)).transpose(0, 3, 2, 1, 4)
        blocks = jnp.where(lax.axis_index("x") == 0, blocks, blocks[:, :, ::-1])
        blocks = jnp.where(lax.axis_index("core") == 0, blocks, blocks[:, :, :, ::-1])
        return blocks.reshape(rows, width)

    def gather(weight):
        along = lax.all_gather(weight, "z", axis=0, tiled=True)
        across = lax.ppermute(along, "x", SWAP)
        return jnp.concatenate(
            [along, across, lax.ppermute(along, "core", SWAP), lax.ppermute(across, "core", SWAP)],
            axis=0,
        )

    def scatter(left, right):
        half = left.shape[1] // 2
        quarter = half // 2
        for_core = dot_inner(left[:, half:], right).astype(bf16)
        from_core = lax.ppermute(for_core, "core", SWAP)
        for_x = (dot_inner(left[:, quarter:half], right) + from_core[quarter:].astype(f32)).astype(bf16)
        from_x = lax.ppermute(for_x, "x", SWAP)
        kept = (
            dot_inner(left[:, :quarter], right)
            + from_core[:quarter].astype(f32)
            + from_x.astype(f32)
        ).astype(bf16)
        return lax.psum_scatter(kept, "z", scatter_dimension=0, tiled=True).astype(f32)

    def total(vector):
        for axis in ("core", "x", "tensor"):
            vector = vector + lax.ppermute(vector, axis, SWAP)
        step = 1
        while step < outer:
            vector = vector + lax.ppermute(vector, "z", [(i, i ^ step) for i in range(outer)])
            step *= 2
        return vector

    def both_halves(own):
        other = lax.ppermute(own, "tensor", SWAP)
        return jnp.where(
            lax.axis_index("tensor") == 0,
            jnp.concatenate([own, other], axis=0),
            jnp.concatenate([other, own], axis=0),
        )

    def reduce_halves(product, *operands):
        rows = operands[0].shape[0] // 2
        place = lax.axis_index("tensor")

        def cut(at):
            return [lax.dynamic_slice_in_dim(o, at * rows, rows, axis=0) for o in operands]

        sent = lax.ppermute(product(*cut(1 - place)).astype(bf16), "tensor", SWAP)
        return product(*cut(place)) + sent.astype(f32)

    def shards(
        tokens,
        segments,
        q_weight,
        k_weight,
        v_weight,
        o_weight,
        attention_gain,
        gate_weight,
        up_weight,
        down_weight,
        feed_gain,
        out_grad,
    ):
        query_width = q_weight.shape[1]
        key_width = k_weight.shape[1]
        score_scale = HEAD_DIM ** (-0.5)
        qkv_full = gather(jnp.concatenate([q_weight, k_weight, v_weight], axis=1))
        output_full = gather(o_weight)
        gate_full = gather(gate_weight)
        up_full = gather(up_weight)
        down_full = gather(down_weight)

        attention_gain = relative(attention_gain[None])
        feed_gain = relative(feed_gain[None])
        tokens = relative(tokens)
        out_grad = relative(out_grad)

        segment_row = segments[0]
        cosine, sine = rotary_tables(segment_row)
        first_seen = first_blocks(segment_row)
        inputs = tokens.astype(f32)
        inverse_first = inverse_rms(inputs)
        normed_first = (inputs * inverse_first * attention_gain).astype(bf16)
        normed_seq = both_halves(normed_first)
        grad_seq = both_halves(out_grad)
        qkv = dot_plain(normed_seq, qkv_full)
        rotated = rope(qkv, cosine, sine, (query_width + key_width) // 128)
        mixed, log_totals = attend(rotated, query_width, first_seen, segment_row, score_scale)
        middle = inputs + reduce_halves(lambda m: dot_trans(m, output_full), mixed)
        inverse_second = inverse_rms(middle)
        normed_second = (middle * inverse_second * feed_gain).astype(bf16)
        normed_feed = both_halves(normed_second)
        gate_value = dot_plain(normed_feed, gate_full).astype(bf16)
        up_value = dot_plain(normed_feed, up_full).astype(bf16)
        hidden = (jax.nn.silu(gate_value.astype(f32)) * up_value.astype(f32)).astype(bf16)
        down_weight_grad = scatter(grad_seq, hidden)
        hidden_grad = dot_plain(grad_seq, down_full)
        gate_value, up_value = gate_value.astype(f32), up_value.astype(f32)
        sigmoid_gate = jax.nn.sigmoid(gate_value)
        gate_grad = (
            hidden_grad * up_value * sigmoid_gate * (1.0 + gate_value * (1.0 - sigmoid_gate))
        ).astype(bf16)
        up_grad = (hidden_grad * gate_value * sigmoid_gate).astype(bf16)
        block_out = (middle + reduce_halves(lambda h: dot_trans(h, down_full), hidden)).astype(bf16)
        feed_normed_grad = reduce_halves(
            lambda g, u: dot_trans(g, gate_full) + dot_trans(u, up_full), gate_grad, up_grad
        )
        gate_weight_grad = scatter(normed_feed, gate_grad)
        up_weight_grad = scatter(normed_feed, up_grad)
        middle_grad = out_grad.astype(f32) + norm_back(
            middle, inverse_second, feed_gain, feed_normed_grad
        )
        feed_gain_part = jnp.sum(feed_normed_grad * middle * inverse_second, axis=0)
        attn_out_grad = middle_grad.astype(bf16)
        attn_grad_seq = both_halves(attn_out_grad)
        output_weight_grad = scatter(attn_grad_seq, mixed)
        mixed_grad = dot_plain(attn_grad_seq, output_full).astype(bf16)
        qkv_grad = jnp.concatenate(
            attend_back(
                rotated,
                mixed_grad,
                log_totals,
                query_width,
                first_seen,
                segment_row,
                cosine,
                sine,
                score_scale,
            ),
            axis=1,
        )
        qkv_weight_grad = scatter(normed_seq, qkv_grad)
        normed_grad = reduce_halves(lambda g: dot_trans(g, qkv_full), qkv_grad)
        input_grad = (
            middle_grad + norm_back(inputs, inverse_first, attention_gain, normed_grad)
        ).astype(bf16)
        attention_gain_part = jnp.sum(normed_grad * inputs * inverse_first, axis=0)
        feed_gain_grad = total(natural(feed_gain_part[None]))[0]
        attention_gain_grad = total(natural(attention_gain_part[None]))[0]
        return (
            natural(block_out),
            natural(input_grad),
            qkv_weight_grad[:, :query_width],
            qkv_weight_grad[:, query_width : query_width + key_width],
            qkv_weight_grad[:, query_width + key_width :],
            output_weight_grad,
            attention_gain_grad,
            gate_weight_grad,
            up_weight_grad,
            down_weight_grad,
            feed_gain_grad,
        )

    return shards


def solution(mesh):
    outer = mesh.shape["dp"] // 4
    fine = Mesh(
        mesh.devices.reshape(outer, 2, 2, mesh.shape["tensor"]), ("z", "x", "core", "tensor")
    )
    dp = ("z", "x", "core")
    every = P(dp + ("tensor",), None)
    weight = P(dp, "tensor")
    return jax.shard_map(
        make_shards(outer),
        mesh=fine,
        in_specs=(
            every,
            P(dp, None),
            weight,
            weight,
            weight,
            weight,
            P(),
            weight,
            weight,
            weight,
            P(),
            every,
        ),
        out_specs=(every, every, weight, weight, weight, weight, P(), weight, weight, weight, P()),
        check_vma=False,
    )
```

```python
import functools

import jax
import jax.numpy as jnp
from jax import lax
from jax.experimental import pallas as pl
from jax.experimental.pallas import tpu as pltpu
from jax.sharding import Mesh, PartitionSpec as P

HEAD_DIM = 64
SWAP = ((0, 1), (1, 0))
QUERIES = 256
CHUNKS = 2
VMEM = 40 * 2**20
epsilon = 1e-05
rope_base = 10000.0
bf16 = jnp.bfloat16
f32 = jnp.float32


def dot_plain(left, right):
    return jnp.dot(left, right, preferred_element_type=f32)


def dot_trans(left, right):
    return lax.dot_general(left, right, (((1,), (1,)), ((), ())), preferred_element_type=f32)


def dot_inner(left, right):
    return lax.dot_general(left, right, (((0,), (0,)), ((), ())), preferred_element_type=f32)


def rotary_tables(segment_row):
    length = segment_row.shape[0]
    before = jnp.sum((segment_row[None, :] < segment_row[:, None]).astype(jnp.int32), axis=1)
    places = (jnp.arange(length, dtype=jnp.int32) - before).astype(f32)
    half_dim = HEAD_DIM // 2
    frequency = rope_base ** (-2.0 * jnp.arange(half_dim).astype(f32) / HEAD_DIM)
    angles = places[:, None] * frequency[None, :]
    cosine, sine = jnp.cos(angles), jnp.sin(angles)
    return (jnp.concatenate([cosine] * 4, axis=1), jnp.concatenate([-sine, sine] * 2, axis=1))


def first_blocks(segment_row):
    starts, ends = segment_row[::QUERIES], segment_row[QUERIES - 1 :: QUERIES]
    return jnp.sum((ends[None, :] < starts[:, None]).astype(jnp.int32), axis=1)


def inverse_rms(activity):
    return lax.rsqrt(jnp.mean(activity * activity, axis=-1, keepdims=True) + epsilon)


def norm_back(activity, inverse, gain_vec, incoming):
    scaled = incoming * gain_vec
    return inverse * scaled - activity * (inverse * inverse * inverse) * jnp.mean(
        scaled * activity, axis=-1, keepdims=True
    )


def lanes_of(shape):
    return lax.broadcasted_iota(jnp.int32, shape, len(shape) - 1)


def turn(block, cosine, sine):
    low_half = lanes_of(block.shape) % HEAD_DIM < HEAD_DIM // 2
    other = jnp.where(low_half, pltpu.roll(block, 96, 1), pltpu.roll(block, 32, 1))
    return block * cosine + other * sine


def rope_kernel(rotated, qkv_ref, cos_ref, sin_ref, out_ref):
    block = qkv_ref[...]

    @pl.when(pl.program_id(0) < rotated)
    def _():
        out_ref[...] = turn(block, cos_ref[...], sin_ref[...]).astype(bf16)

    @pl.when(pl.program_id(0) >= rotated)
    def _():
        out_ref[...] = block.astype(bf16)


def rope(qkv, cosine, sine, rotated):
    length, width = qkv.shape
    block = pl.BlockSpec((length, 128), lambda j: (0, j))
    table = pl.BlockSpec((length, 128), lambda j: (0, 0))
    return pl.pallas_call(
        functools.partial(rope_kernel, rotated),
        grid=(width // 128,),
        in_specs=[block, table, table],
        out_specs=block,
        out_shape=jax.ShapeDtypeStruct((length, width), bf16),
        compiler_params=pltpu.CompilerParams(vmem_limit_bytes=VMEM),
        cost_estimate=pl.CostEstimate(
            flops=4 * length * width, bytes_accessed=6 * length * width, transcendentals=0
        ),
    )(qkv, cosine, sine)


def widen(pair_ref, wide_ref, group):
    pair = pair_ref[...]
    keep = (lanes_of(pair.shape) < HEAD_DIM) == (group == 0)
    half = jnp.where(keep, pair, pltpu.roll(pair.astype(f32), HEAD_DIM, 1).astype(bf16))
    wide_ref[:, :128] = half
    wide_ref[:, 128:] = half


def seen_bias(col_ref, row_ref, start, keys, step):
    queries = col_ref.shape[0]
    same = col_ref[...] == row_ref[:, pl.ds(start, keys)]
    q_at = lax.broadcasted_iota(jnp.int32, (queries, keys), 0) + step * queries
    k_at = lax.broadcasted_iota(jnp.int32, (queries, keys), 1) + start
    return jnp.where(same & (q_at >= k_at), 0.0, -1e30).astype(f32)


def forward_kernel(scale, low_ref, q_ref, k_ref, v_ref, col_ref, row_ref, o_ref, lse_ref, kw_ref, vw_ref):
    group, step = pl.program_id(0), pl.program_id(1)
    queries = q_ref.shape[0]

    @pl.when(step == 0)
    def _():
        widen(k_ref, kw_ref, group)
        widen(v_ref, vw_ref, group)

    def run(blocks):
        keys = blocks * queries
        start = pl.multiple_of(low_ref[step] * queries, queries)
        bias = seen_bias(col_ref, row_ref, start, keys, step)
        key = kw_ref[pl.ds(start, keys), :]
        value = vw_ref[pl.ds(start, keys), :]
        head_of = lanes_of((queries, 256)) // HEAD_DIM
        lse = jnp.zeros((queries, 128), f32)
        for quad in range(q_ref.shape[1] // 256):
            wide = q_ref[:, quad * 256 : quad * 256 + 256]
            out = jnp.zeros((queries, 256), f32)
            for j in range(4):
                one = jnp.where(head_of == j, wide, jnp.zeros_like(wide))
                scores = dot_trans(one, key) * scale + bias
                top = jnp.max(scores, axis=1, keepdims=True)
                powers = jnp.exp(scores - top)
                sums = jnp.sum(powers, axis=1, keepdims=True)
                prob = (powers * (1.0 / sums)).astype(bf16)
                out = jnp.where(head_of == j, dot_plain(prob, value), out)
                lse = jnp.where(lanes_of(lse.shape) == quad * 4 + j, top + jnp.log(sums), lse)
            o_ref[:, quad * 256 : quad * 256 + 256] = out.astype(bf16)
        lse_ref[...] = lse

    for blocks in range(1, row_ref.shape[1] // queries + 1):
        pl.when(step + 1 - low_ref[step] == blocks)(functools.partial(run, blocks))


def backward_kernel(
    scale, low_ref, q_ref, k_ref, v_ref, g_ref, lse_ref, col_ref, row_ref, cos_ref, sin_ref, kcos_ref, ksin_ref,
    dq_ref, dk_ref, dv_ref, kw_ref, vw_ref, dkw_ref, dvw_ref,
):
    group, step = pl.program_id(0), pl.program_id(1)
    queries = q_ref.shape[0]

    @pl.when(step == 0)
    def _():
        widen(k_ref, kw_ref, group)
        widen(v_ref, vw_ref, group)
        dkw_ref[...] = jnp.zeros_like(dkw_ref)
        dvw_ref[...] = jnp.zeros_like(dvw_ref)

    def run(blocks):
        keys = blocks * queries
        start = pl.multiple_of(low_ref[step] * queries, queries)
        bias = seen_bias(col_ref, row_ref, start, keys, step)
        key = kw_ref[pl.ds(start, keys), :]
        value = vw_ref[pl.ds(start, keys), :]
        head_of = lanes_of((queries, 256)) // HEAD_DIM
        cosine, sine = cos_ref[...], sin_ref[...]
        for quad in range(q_ref.shape[1] // 256):
            wide = q_ref[:, quad * 256 : quad * 256 + 256]
            grads = g_ref[:, quad * 256 : quad * 256 + 256]
            out = jnp.zeros((queries, 256), f32)
            for j in range(4):
                at = quad * 4 + j
                one = jnp.where(head_of == j, wide, jnp.zeros_like(wide))
                grad = jnp.where(head_of == j, grads, jnp.zeros_like(grads))
                prob = jnp.exp(dot_trans(one, key) * scale + bias - lse_ref[:, at : at + 1])
                prob_grad = dot_trans(grad, value)
                centre = jnp.sum(prob * prob_grad, axis=1, keepdims=True)
                score_grad = (prob * (prob_grad - centre) * scale).astype(bf16)
                dvw_ref[pl.ds(start, keys), :] += dot_inner(prob.astype(bf16), grad)
                dkw_ref[pl.ds(start, keys), :] += dot_inner(score_grad, one)
                out = jnp.where(head_of == j, dot_plain(score_grad, key), out)
            for half in range(2):
                piece = turn(out[:, half * 128 : half * 128 + 128], cosine, -sine)
                dq_ref[:, quad * 256 + half * 128 : quad * 256 + half * 128 + 128] = piece.astype(bf16)

    for blocks in range(1, row_ref.shape[1] // queries + 1):
        pl.when(step + 1 - low_ref[step] == blocks)(functools.partial(run, blocks))

    @pl.when(step == pl.num_programs(1) - 1)
    def _():
        mine = (lanes_of(dk_ref.shape) < HEAD_DIM) == (group == 0)

        def fold(ref):
            pair = ref[:, :128] + ref[:, 128:]
            return pair + pltpu.roll(pair, HEAD_DIM, 1)

        dk = turn(fold(dkw_ref), kcos_ref[...], -ksin_ref[...]).astype(bf16)
        dk_ref[...] = jnp.where(mine, dk, dk_ref[...])
        dv_ref[...] = jnp.where(mine, fold(dvw_ref).astype(bf16), dv_ref[...])


def attention_specs(length, queries, wide):
    at = lambda g, i, low: (i, g)
    pair = lambda first: pl.BlockSpec((length, 128), lambda g, i, low: (0, first))
    col = pl.BlockSpec((queries, 1), lambda g, i, low: (i, 0))
    row = pl.BlockSpec((1, length), lambda g, i, low: (0, 0))
    return pl.BlockSpec((queries, wide), at), pair, col, row


def attend(rotated, query_width, first_seen, segment_row, scale):
    length = rotated.shape[0]
    queries = length // first_seen.shape[0]
    groups = 2
    wide = query_width // groups
    heads, pair, col, row = attention_specs(length, queries, wide)
    first = query_width // 128
    return pl.pallas_call(
        functools.partial(forward_kernel, scale),
        grid_spec=pltpu.PrefetchScalarGridSpec(
            num_scalar_prefetch=1,
            grid=(groups, length // queries),
            in_specs=[heads, pair(first), pair(first + 1), col, row],
            out_specs=[heads, pl.BlockSpec((queries, 128), lambda g, i, low: (i, g))],
            scratch_shapes=[pltpu.VMEM((length, 256), bf16), pltpu.VMEM((length, 256), bf16)],
        ),
        out_shape=[
            jax.ShapeDtypeStruct((length, query_width), bf16),
            jax.ShapeDtypeStruct((length, groups * 128), f32),
        ],
        compiler_params=pltpu.CompilerParams(vmem_limit_bytes=VMEM),
        cost_estimate=pl.CostEstimate(
            flops=10 * length * length * query_width, bytes_accessed=4 * length * query_width,
            transcendentals=0,
        ),
    )(first_seen, rotated, rotated, rotated, segment_row.reshape(length, 1), segment_row.reshape(1, length))


def attend_back(rotated, grads, lse, query_width, first_seen, segment_row, cosine, sine, scale):
    length = rotated.shape[0]
    queries = length // first_seen.shape[0]
    groups = 2
    wide = query_width // groups
    heads, pair, col, row = attention_specs(length, queries, wide)
    first = query_width // 128
    table = pl.BlockSpec((queries, 128), lambda g, i, low: (i, 0))
    return pl.pallas_call(
        functools.partial(backward_kernel, scale),
        grid_spec=pltpu.PrefetchScalarGridSpec(
            num_scalar_prefetch=1,
            grid=(groups, length // queries),
            in_specs=[
                heads, pair(first), pair(first + 1), heads,
                pl.BlockSpec((queries, 128), lambda g, i, low: (i, g)),
                col, row, table, table, pair(0), pair(0),
            ],
            out_specs=[heads, pair(0), pair(0)],
            scratch_shapes=[
                pltpu.VMEM((length, 256), bf16), pltpu.VMEM((length, 256), bf16),
                pltpu.VMEM((length, 256), f32), pltpu.VMEM((length, 256), f32),
            ],
        ),
        out_shape=[
            jax.ShapeDtypeStruct((length, query_width), bf16),
            jax.ShapeDtypeStruct((length, 128), bf16),
            jax.ShapeDtypeStruct((length, 128), bf16),
        ],
        compiler_params=pltpu.CompilerParams(vmem_limit_bytes=VMEM),
        cost_estimate=pl.CostEstimate(
            flops=30 * length * length * query_width, bytes_accessed=8 * length * query_width,
            transcendentals=0,
        ),
    )(
        first_seen, rotated, rotated, rotated, grads, lse,
        segment_row.reshape(length, 1), segment_row.reshape(1, length), cosine, sine, cosine, sine,
    )


def tie(array, *earlier):
    return lax.optimization_barrier((array,) + earlier)[0]


class Order:
    def __init__(self):
        self.last = None

    def __call__(self, compute, *operands):
        if self.last is not None:
            operands = lax.optimization_barrier((*operands, self.last))[:-1]
        result = compute(*operands)
        self.last = result[0] if isinstance(result, tuple) else result
        return result


def make_shards(outer):
    def relative(array):
        rows, width = array.shape
        blocks = array.reshape(rows, outer, 2, 2, width // (4 * outer))
        blocks = jnp.where(lax.axis_index("x") == 0, blocks, blocks[:, :, ::-1])
        blocks = jnp.where(lax.axis_index("core") == 0, blocks, blocks[:, :, :, ::-1])
        return blocks.transpose(0, 3, 2, 1, 4).reshape(rows, width)

    def natural(array):
        rows, width = array.shape
        blocks = array.reshape(rows, 2, 2, outer, width // (4 * outer)).transpose(0, 3, 2, 1, 4)
        blocks = jnp.where(lax.axis_index("x") == 0, blocks, blocks[:, :, ::-1])
        blocks = jnp.where(lax.axis_index("core") == 0, blocks, blocks[:, :, :, ::-1])
        return blocks.reshape(rows, width)

    def gather(along):
        across = lax.ppermute(along, "x", SWAP)
        return jnp.concatenate(
            [along, across, lax.ppermute(along, "core", SWAP), lax.ppermute(across, "core", SWAP)],
            axis=0,
        )

    def total(vector):
        for axis in ("core", "x", "tensor"):
            vector = vector + lax.ppermute(vector, axis, SWAP)
        step = 1
        while step < outer:
            vector = vector + lax.ppermute(vector, "z", [(i, i ^ step) for i in range(outer)])
            step *= 2
        return vector

    def join(own, other):
        first = lax.axis_index("tensor") == 0
        return jnp.concatenate([jnp.where(first, own, other), jnp.where(first, other, own)], axis=0)

    def swap(own):
        return lax.ppermute(own, "tensor", SWAP)

    def shards(
        tokens,
        segments,
        q_weight,
        k_weight,
        v_weight,
        o_weight,
        attention_gain,
        gate_weight,
        up_weight,
        down_weight,
        feed_gain,
        out_grad,
    ):
        query_width = q_weight.shape[1]
        key_width = k_weight.shape[1]
        hidden_width = gate_weight.shape[1]
        score_scale = HEAD_DIM ** (-0.5)
        place = lax.axis_index("tensor")
        order = Order()

        def cut(weight):
            width = hidden_width // CHUNKS
            return [weight[:, i * width : i * width + width] for i in range(CHUNKS)]

        names = ["qkv", "o"]
        shard = {"qkv": jnp.concatenate([q_weight, k_weight, v_weight], axis=1), "o": o_weight}
        for i, (gate, up) in enumerate(zip(cut(gate_weight), cut(up_weight))):
            names += [("gate", i), ("up", i)]
            shard["gate", i], shard["up", i] = gate, up
        for i, down in enumerate(cut(down_weight)):
            names.append(("down", i))
            shard["down", i] = down
        along = {}
        for at, name in enumerate(names):
            operand = shard[name]
            if at > 1:
                operand = tie(operand, along[names[at - 2]])
            along[name] = lax.all_gather(operand, "z", axis=0, tiled=True)
        full = {name: gather(along[name]) for name in names}

        attention_gain = relative(attention_gain[None])
        feed_gain = relative(feed_gain[None])
        tokens = relative(tokens)
        out_grad = relative(out_grad)
        half = tokens.shape[1] // 2
        quarter = half // 2
        rows = tokens.shape[0]

        def mine(array):
            return lax.dynamic_slice_in_dim(array, place * rows, rows, axis=0)

        def theirs(array):
            return lax.dynamic_slice_in_dim(array, (1 - place) * rows, rows, axis=0)

        from_core, from_x, summed = {}, {}, {}

        def for_core(name, left, right):
            part = order(lambda l, r: dot_inner(l[:, half:], r).astype(bf16), left, right)
            from_core[name] = lax.ppermute(part, "core", SWAP)

        def for_x(name, left, right):
            part = order(
                lambda l, r, c: (dot_inner(l[:, quarter:half], r) + c[quarter:].astype(f32)).astype(bf16),
                left, right, from_core[name],
            )
            from_x[name] = lax.ppermute(part, "x", SWAP)

        def keep(name, left, right):
            part = order(
                lambda l, r, c, x: (
                    dot_inner(l[:, :quarter], r) + c[:quarter].astype(f32) + x.astype(f32)
                ).astype(bf16),
                left, right, from_core[name], from_x[name],
            )
            summed[name] = lax.psum_scatter(part, "z", scatter_dimension=0, tiled=True)

        segment_row = segments[0]
        cosine, sine = rotary_tables(segment_row)
        first_seen = first_blocks(segment_row)
        inputs = tokens.astype(f32)
        inverse_first = inverse_rms(inputs)
        normed_first = (inputs * inverse_first * attention_gain).astype(bf16)
        normed_seq = join(normed_first, swap(normed_first))
        grad_seq = join(out_grad, swap(out_grad))

        qkv = order(dot_plain, normed_seq, full["qkv"])
        rotated = order(lambda a: rope(a, cosine, sine, (query_width + key_width) // 128), qkv)
        mixed, log_totals = order(
            lambda a: attend(a, query_width, first_seen, segment_row, score_scale), rotated
        )
        sent = swap(order(lambda m, w: dot_trans(theirs(m), w).astype(bf16), mixed, full["o"]))
        own = order(lambda m, w: dot_trans(mine(m), w), mixed, full["o"])
        middle = inputs + own + sent.astype(f32)
        inverse_second = inverse_rms(middle)
        normed_second = (middle * inverse_second * feed_gain).astype(bf16)
        normed_feed = join(normed_second, swap(normed_second))

        gates, ups, hiddens = [], [], []
        for i in range(CHUNKS):
            gate = order(lambda n, w: dot_plain(n, w).astype(bf16), normed_feed, full["gate", i])

            def up_step(n, w, g):
                u = dot_plain(n, w)
                return u.astype(bf16), (jax.nn.silu(g.astype(f32)) * u).astype(bf16)

            up, hidden = order(up_step, normed_feed, full["up", i], gate)
            gates.append(gate)
            ups.append(up)
            hiddens.append(hidden)
            for_core(("down", i), grad_seq, hidden)
            if i > 0:
                for_x(("down", i - 1), grad_seq, hiddens[i - 1])
        for_x(("down", CHUNKS - 1), grad_seq, hiddens[-1])

        gate_grads, up_grads = [], []
        for i in range(CHUNKS):

            def back_step(g, w, gate, up):
                grad = dot_plain(g, w)
                gate, up = gate.astype(f32), up.astype(f32)
                sigmoid = jax.nn.sigmoid(gate)
                return (
                    (grad * up * sigmoid * (1.0 + gate * (1.0 - sigmoid))).astype(bf16),
                    (grad * gate * sigmoid).astype(bf16),
                )

            gate_grad, up_grad = order(back_step, grad_seq, full["down", i], gates[i], ups[i])
            gate_grads.append(gate_grad)
            up_grads.append(up_grad)
            if i < CHUNKS - 1:
                for_core(("gate", i), normed_feed, gate_grad)
                for_core(("up", i), normed_feed, up_grad)

        def feed_back(pick):
            total_grad = None
            for i in range(CHUNKS):
                for grad, name in ((gate_grads[i], "gate"), (up_grads[i], "up")):
                    one = lambda g, w, t=None: dot_trans(pick(g), w) + (0.0 if t is None else t)
                    more = () if total_grad is None else (total_grad,)
                    total_grad = order(one, grad, full[name, i], *more)
            return total_grad

        sent = swap(feed_back(theirs).astype(bf16))
        keep(("down", 0), grad_seq, hiddens[0])
        for i in range(CHUNKS - 1):
            for_x(("gate", i), normed_feed, gate_grads[i])
            for_x(("up", i), normed_feed, up_grads[i])
        for_core(("gate", CHUNKS - 1), normed_feed, gate_grads[-1])
        for_core(("up", CHUNKS - 1), normed_feed, up_grads[-1])
        own = feed_back(mine)
        for_x(("gate", CHUNKS - 1), normed_feed, gate_grads[-1])
        for_x(("up", CHUNKS - 1), normed_feed, up_grads[-1])
        for i in range(1, CHUNKS):
            keep(("down", i), grad_seq, hiddens[i])
        own, sent = order(lambda a, b: (a, b), own, sent)
        feed_normed_grad = own + sent.astype(f32)
        middle_grad = out_grad.astype(f32) + norm_back(
            middle, inverse_second, feed_gain, feed_normed_grad
        )
        feed_gain_part = jnp.sum(feed_normed_grad * middle * inverse_second, axis=0)
        attn_out_grad = middle_grad.astype(bf16)
        attn_out_grad, middle_grad, feed_gain_part = order(
            lambda *a: a, attn_out_grad, middle_grad, feed_gain_part
        )
        attn_grad_other = swap(attn_out_grad)

        def block(pick):
            return lambda *a: sum(
                dot_trans(pick(h), w) for h, w in zip(a[:CHUNKS], a[CHUNKS:])
            )

        downs = [full["down", i] for i in range(CHUNKS)]
        sent = swap(order(lambda *a: block(theirs)(*a).astype(bf16), *hiddens, *downs))
        keep(("gate", 0), normed_feed, gate_grads[0])
        own = order(block(mine), *hiddens, *downs)
        keep(("up", 0), normed_feed, up_grads[0])
        attn_grad_seq = join(attn_out_grad, attn_grad_other)
        mixed_grad = order(lambda g, w: dot_plain(g, w).astype(bf16), attn_grad_seq, full["o"])
        for_core("o", attn_grad_seq, mixed)
        block_out = order(lambda m, a, b: (m + a + b.astype(f32)).astype(bf16), middle, own, sent)
        for_x("o", attn_grad_seq, mixed)
        qkv_grad = order(
            lambda r, g, l: jnp.concatenate(
                attend_back(
                    r, g, l, query_width, first_seen, segment_row, cosine, sine, score_scale
                ),
                axis=1,
            ),
            rotated, mixed_grad, log_totals,
        )
        for_core("qkv", normed_seq, qkv_grad)
        for i in range(1, CHUNKS):
            keep(("gate", i), normed_feed, gate_grads[i])
        sent = swap(order(lambda g, w: dot_trans(theirs(g), w).astype(bf16), qkv_grad, full["qkv"]))
        for_x("qkv", normed_seq, qkv_grad)
        for i in range(1, CHUNKS):
            keep(("up", i), normed_feed, up_grads[i])
        own = order(lambda g, w: dot_trans(mine(g), w), qkv_grad, full["qkv"])
        keep("o", attn_grad_seq, mixed)
        feed_gain_grad = total(natural(feed_gain_part[None]))[0]
        normed_grad = own + sent.astype(f32)
        input_grad = (
            middle_grad + norm_back(inputs, inverse_first, attention_gain, normed_grad)
        ).astype(bf16)
        attention_gain_part = jnp.sum(normed_grad * inputs * inverse_first, axis=0)
        input_grad, attention_gain_part = order(lambda *a: a, input_grad, attention_gain_part)
        keep("qkv", normed_seq, qkv_grad)
        attention_gain_grad = total(natural(attention_gain_part[None]))[0]
        qkv_weight_grad = summed["qkv"].astype(f32)

        def whole(name):
            return jnp.concatenate([summed[name, i] for i in range(CHUNKS)], axis=1).astype(f32)

        return (
            natural(block_out),
            natural(input_grad),
            qkv_weight_grad[:, :query_width],
            qkv_weight_grad[:, query_width : query_width + key_width],
            qkv_weight_grad[:, query_width + key_width :],
            summed["o"].astype(f32),
            attention_gain_grad,
            whole("gate"),
            whole("up"),
            whole("down"),
            feed_gain_grad,
        )

    return shards


def solution(mesh):
    outer = mesh.shape["dp"] // 4
    fine = Mesh(
        mesh.devices.reshape(outer, 2, 2, mesh.shape["tensor"]), ("z", "x", "core", "tensor")
    )
    dp = ("z", "x", "core")
    every = P(dp + ("tensor",), None)
    weight = P(dp, "tensor")
    return jax.shard_map(
        make_shards(outer),
        mesh=fine,
        in_specs=(
            every,
            P(dp, None),
            weight,
            weight,
            weight,
            weight,
            P(),
            weight,
            weight,
            weight,
            P(),
            every,
        ),
        out_specs=(every, every, weight, weight, weight, weight, P(), weight, weight, weight, P()),
        check_vma=False,
    )
```

```python
import functools

import jax
import jax.numpy as jnp
from jax import lax
from jax.experimental import pallas as pl
from jax.experimental.pallas import tpu as pltpu
from jax.sharding import Mesh, PartitionSpec as P

HEAD_DIM = 64
SWAP = ((0, 1), (1, 0))
QUERIES = 256
CHUNKS = 2
BLOCK = 256
VMEM = 48 * 2**20
epsilon = 1e-05
rope_base = 10000.0
bf16 = jnp.bfloat16
f32 = jnp.float32


def dot_plain(left, right):
    return jnp.dot(left, right, preferred_element_type=f32)


def dot_trans(left, right):
    return lax.dot_general(left, right, (((1,), (1,)), ((), ())), preferred_element_type=f32)


def dot_inner(left, right):
    return lax.dot_general(left, right, (((0,), (0,)), ((), ())), preferred_element_type=f32)


def rotary_tables(segment_row):
    length = segment_row.shape[0]
    before = jnp.sum((segment_row[None, :] < segment_row[:, None]).astype(jnp.int32), axis=1)
    places = (jnp.arange(length, dtype=jnp.int32) - before).astype(f32)
    half_dim = HEAD_DIM // 2
    frequency = rope_base ** (-2.0 * jnp.arange(half_dim).astype(f32) / HEAD_DIM)
    angles = places[:, None] * frequency[None, :]
    cosine, sine = jnp.cos(angles), jnp.sin(angles)
    return (jnp.concatenate([cosine] * 4, axis=1), jnp.concatenate([-sine, sine] * 2, axis=1))


def first_blocks(segment_row):
    starts, ends = segment_row[::QUERIES], segment_row[QUERIES - 1 :: QUERIES]
    return jnp.sum((ends[None, :] < starts[:, None]).astype(jnp.int32), axis=1)


def inverse_rms(activity):
    return lax.rsqrt(jnp.mean(activity * activity, axis=-1, keepdims=True) + epsilon)


def norm_back(activity, inverse, gain_vec, incoming):
    scaled = incoming * gain_vec
    return inverse * scaled - activity * (inverse * inverse * inverse) * jnp.mean(
        scaled * activity, axis=-1, keepdims=True
    )


def lanes_of(shape):
    return lax.broadcasted_iota(jnp.int32, shape, len(shape) - 1)


def turn(block, cosine, sine):
    low_half = lanes_of(block.shape) % HEAD_DIM < HEAD_DIM // 2
    other = jnp.where(low_half, pltpu.roll(block, 96, 1), pltpu.roll(block, 32, 1))
    return block * cosine + other * sine


def widen(pair_ref, wide_ref, group):
    pair = pair_ref[...]
    keep = (lanes_of(pair.shape) < HEAD_DIM) == (group == 0)
    half = jnp.where(keep, pair, pltpu.roll(pair.astype(f32), HEAD_DIM, 1).astype(bf16))
    wide_ref[:, :128] = half
    wide_ref[:, 128:] = half


def seen_bias(col_ref, row_ref, start, keys, step):
    queries = col_ref.shape[0]
    same = col_ref[...] == row_ref[:, pl.ds(start, keys)]
    q_at = lax.broadcasted_iota(jnp.int32, (queries, keys), 0) + step * queries
    k_at = lax.broadcasted_iota(jnp.int32, (queries, keys), 1) + start
    return jnp.where(same & (q_at >= k_at), 0.0, -1e30).astype(f32)


def forward_kernel(scale, low_ref, q_ref, k_ref, v_ref, col_ref, row_ref, o_ref, lse_ref, kw_ref, vw_ref):
    group, step = pl.program_id(0), pl.program_id(1)
    queries = q_ref.shape[0]

    @pl.when(step == 0)
    def _():
        widen(k_ref, kw_ref, group)
        widen(v_ref, vw_ref, group)

    def run(blocks):
        keys = blocks * queries
        start = pl.multiple_of(low_ref[step] * queries, queries)
        bias = seen_bias(col_ref, row_ref, start, keys, step)
        key = kw_ref[pl.ds(start, keys), :]
        value = vw_ref[pl.ds(start, keys), :]
        head_of = lanes_of((queries, 256)) // HEAD_DIM
        lse = jnp.zeros((queries, 128), f32)
        for quad in range(q_ref.shape[1] // 256):
            wide = q_ref[:, quad * 256 : quad * 256 + 256]
            out = jnp.zeros((queries, 256), f32)
            for j in range(4):
                one = jnp.where(head_of == j, wide, jnp.zeros_like(wide))
                scores = dot_trans(one, key) * scale + bias
                top = jnp.max(scores, axis=1, keepdims=True)
                powers = jnp.exp(scores - top)
                sums = jnp.sum(powers, axis=1, keepdims=True)
                prob = (powers * (1.0 / sums)).astype(bf16)
                out = jnp.where(head_of == j, dot_plain(prob, value), out)
                lse = jnp.where(lanes_of(lse.shape) == quad * 4 + j, top + jnp.log(sums), lse)
            o_ref[:, quad * 256 : quad * 256 + 256] = out.astype(bf16)
        lse_ref[...] = lse

    for blocks in range(1, row_ref.shape[1] // queries + 1):
        pl.when(step + 1 - low_ref[step] == blocks)(functools.partial(run, blocks))


def backward_kernel(
    scale, low_ref, q_ref, k_ref, v_ref, g_ref, lse_ref, col_ref, row_ref, cos_ref, sin_ref, kcos_ref, ksin_ref,
    dq_ref, dk_ref, dv_ref, kw_ref, vw_ref, dkw_ref, dvw_ref,
):
    group, step = pl.program_id(0), pl.program_id(1)
    queries = q_ref.shape[0]

    @pl.when(step == 0)
    def _():
        widen(k_ref, kw_ref, group)
        widen(v_ref, vw_ref, group)
        dkw_ref[...] = jnp.zeros_like(dkw_ref)
        dvw_ref[...] = jnp.zeros_like(dvw_ref)

    def run(blocks):
        keys = blocks * queries
        start = pl.multiple_of(low_ref[step] * queries, queries)
        bias = seen_bias(col_ref, row_ref, start, keys, step)
        key = kw_ref[pl.ds(start, keys), :]
        value = vw_ref[pl.ds(start, keys), :]
        head_of = lanes_of((queries, 256)) // HEAD_DIM
        cosine, sine = cos_ref[...], sin_ref[...]
        for quad in range(q_ref.shape[1] // 256):
            wide = q_ref[:, quad * 256 : quad * 256 + 256]
            grads = g_ref[:, quad * 256 : quad * 256 + 256]
            out = jnp.zeros((queries, 256), f32)
            for j in range(4):
                at = quad * 4 + j
                one = jnp.where(head_of == j, wide, jnp.zeros_like(wide))
                grad = jnp.where(head_of == j, grads, jnp.zeros_like(grads))
                prob = jnp.exp(dot_trans(one, key) * scale + bias - lse_ref[:, at : at + 1])
                prob_grad = dot_trans(grad, value)
                centre = jnp.sum(prob * prob_grad, axis=1, keepdims=True)
                score_grad = (prob * (prob_grad - centre) * scale).astype(bf16)
                dvw_ref[pl.ds(start, keys), :] += dot_inner(prob.astype(bf16), grad)
                dkw_ref[pl.ds(start, keys), :] += dot_inner(score_grad, one)
                out = jnp.where(head_of == j, dot_plain(score_grad, key), out)
            for half in range(2):
                piece = turn(out[:, half * 128 : half * 128 + 128], cosine, -sine)
                dq_ref[:, quad * 256 + half * 128 : quad * 256 + half * 128 + 128] = piece.astype(bf16)

    for blocks in range(1, row_ref.shape[1] // queries + 1):
        pl.when(step + 1 - low_ref[step] == blocks)(functools.partial(run, blocks))

    @pl.when(step == pl.num_programs(1) - 1)
    def _():
        mine = (lanes_of(dk_ref.shape) < HEAD_DIM) == (group == 0)

        def fold(ref):
            pair = ref[:, :128] + ref[:, 128:]
            return pair + pltpu.roll(pair, HEAD_DIM, 1)

        dk = turn(fold(dkw_ref), kcos_ref[...], -ksin_ref[...]).astype(bf16)
        dk_ref[...] = jnp.where(mine, dk, dk_ref[...])
        dv_ref[...] = jnp.where(mine, fold(dvw_ref).astype(bf16), dv_ref[...])


def attention_specs(length, queries, wide):
    at = lambda g, i, low: (i, g)
    pair = lambda first: pl.BlockSpec((length, 128), lambda g, i, low: (0, first))
    col = pl.BlockSpec((queries, 1), lambda g, i, low: (i, 0))
    row = pl.BlockSpec((1, length), lambda g, i, low: (0, 0))
    return pl.BlockSpec((queries, wide), at), pair, col, row


def attend(rotated, query_width, first_seen, segment_row, scale):
    length = rotated.shape[0]
    queries = length // first_seen.shape[0]
    groups = 2
    wide = query_width // groups
    heads, pair, col, row = attention_specs(length, queries, wide)
    first = query_width // 128
    return pl.pallas_call(
        functools.partial(forward_kernel, scale),
        grid_spec=pltpu.PrefetchScalarGridSpec(
            num_scalar_prefetch=1,
            grid=(groups, length // queries),
            in_specs=[heads, pair(first), pair(first + 1), col, row],
            out_specs=[heads, pl.BlockSpec((queries, 128), lambda g, i, low: (i, g))],
            scratch_shapes=[pltpu.VMEM((length, 256), bf16), pltpu.VMEM((length, 256), bf16)],
        ),
        out_shape=[
            jax.ShapeDtypeStruct((length, query_width), bf16),
            jax.ShapeDtypeStruct((length, groups * 128), f32),
        ],
        compiler_params=pltpu.CompilerParams(vmem_limit_bytes=VMEM),
        cost_estimate=pl.CostEstimate(
            flops=10 * length * length * query_width, bytes_accessed=4 * length * query_width,
            transcendentals=0,
        ),
    )(first_seen, rotated, rotated, rotated, segment_row.reshape(length, 1), segment_row.reshape(1, length))


def attend_back(rotated, grads, lse, query_width, first_seen, segment_row, cosine, sine, scale):
    length = rotated.shape[0]
    queries = length // first_seen.shape[0]
    groups = 2
    wide = query_width // groups
    heads, pair, col, row = attention_specs(length, queries, wide)
    first = query_width // 128
    table = pl.BlockSpec((queries, 128), lambda g, i, low: (i, 0))
    return pl.pallas_call(
        functools.partial(backward_kernel, scale),
        grid_spec=pltpu.PrefetchScalarGridSpec(
            num_scalar_prefetch=1,
            grid=(groups, length // queries),
            in_specs=[
                heads, pair(first), pair(first + 1), heads,
                pl.BlockSpec((queries, 128), lambda g, i, low: (i, g)),
                col, row, table, table, pair(0), pair(0),
            ],
            out_specs=[heads, pair(0), pair(0)],
            scratch_shapes=[
                pltpu.VMEM((length, 256), bf16), pltpu.VMEM((length, 256), bf16),
                pltpu.VMEM((length, 256), f32), pltpu.VMEM((length, 256), f32),
            ],
        ),
        out_shape=[
            jax.ShapeDtypeStruct((length, query_width), bf16),
            jax.ShapeDtypeStruct((length, 128), bf16),
            jax.ShapeDtypeStruct((length, 128), bf16),
        ],
        compiler_params=pltpu.CompilerParams(vmem_limit_bytes=VMEM),
        cost_estimate=pl.CostEstimate(
            flops=30 * length * length * query_width, bytes_accessed=8 * length * query_width,
            transcendentals=0,
        ),
    )(
        first_seen, rotated, rotated, rotated, grads, lse,
        segment_row.reshape(length, 1), segment_row.reshape(1, length), cosine, sine, cosine, sine,
    )


def feed_kernel(x_ref, g_ref, *refs):
    pieces, (h_ref, gg_ref, ug_ref) = refs[:12], refs[12:]
    depth = pieces[0].shape[0]

    def product(act_ref, parts):
        return sum(
            dot_plain(act_ref[:, i * depth : i * depth + depth], part[...]) for i, part in enumerate(parts)
        )

    gate = product(x_ref, pieces[:4])
    up = product(x_ref, pieces[4:8])
    sigmoid = jax.nn.sigmoid(gate)
    silu = gate * sigmoid
    h_ref[...] = (silu * up).astype(bf16)
    grad = product(g_ref, pieces[8:])
    gg_ref[...] = (grad * up * (sigmoid * (1.0 + gate * (1.0 - sigmoid)))).astype(bf16)
    ug_ref[...] = (grad * silu).astype(bf16)


def feed(normed, grads, gate, up, down):
    rows, width = normed.shape
    units = gate[0].shape[1]
    depth = width // 4
    act = pl.BlockSpec((rows, width), lambda j: (0, 0))
    part = pl.BlockSpec((depth, BLOCK), lambda j: (0, j))
    out = pl.BlockSpec((rows, BLOCK), lambda j: (0, j))
    return pl.pallas_call(
        feed_kernel,
        grid=(units // BLOCK,),
        in_specs=[act, act] + [part] * 12,
        out_specs=[out] * 3,
        out_shape=[jax.ShapeDtypeStruct((rows, units), bf16)] * 3,
        compiler_params=pltpu.CompilerParams(vmem_limit_bytes=VMEM),
        cost_estimate=pl.CostEstimate(
            flops=6 * rows * width * units, bytes_accessed=6 * width * units, transcendentals=0
        ),
    )(normed, grads, *gate, *up, *down)


def project_kernel(rotated, place_ref, own_ref, other_ref, *refs):
    parts, out_ref = refs[:4], refs[-1]
    depth = parts[0].shape[0]
    rows = own_ref.shape[0]
    for act_ref, place in ((own_ref, place_ref[0]), (other_ref, 1 - place_ref[0])):
        at = pl.ds(pl.multiple_of(place * rows, rows), rows)
        total = sum(
            dot_plain(act_ref[:, i * depth : i * depth + depth], part[...]) for i, part in enumerate(parts)
        )
        if rotated is None:
            out_ref[at, :] = total.astype(bf16)
        else:
            cosine, sine = refs[4][at, :], refs[5][at, :]
            for half in range(2):
                piece = total[:, half * 128 : half * 128 + 128]
                keep = 2 * pl.program_id(0) + half >= rotated
                piece = jnp.where(keep, piece, turn(piece, cosine, sine))
                out_ref[at, half * 128 : half * 128 + 128] = piece.astype(bf16)


def project(place, own, other, weight, tables=(), rotated=None):
    rows, width = own.shape
    units = weight[0].shape[1]
    act = pl.BlockSpec((rows, width), lambda j, s: (0, 0))
    table = pl.BlockSpec((2 * rows, 128), lambda j, s: (0, 0))
    part = pl.BlockSpec((width // 4, BLOCK), lambda j, s: (0, j))
    return pl.pallas_call(
        functools.partial(project_kernel, rotated),
        grid_spec=pltpu.PrefetchScalarGridSpec(
            num_scalar_prefetch=1,
            grid=(units // BLOCK,),
            in_specs=[act, act] + [part] * 4 + [table] * len(tables),
            out_specs=pl.BlockSpec((2 * rows, BLOCK), lambda j, s: (0, j)),
        ),
        out_shape=jax.ShapeDtypeStruct((2 * rows, units), bf16),
        compiler_params=pltpu.CompilerParams(vmem_limit_bytes=VMEM),
        cost_estimate=pl.CostEstimate(
            flops=4 * rows * width * units, bytes_accessed=2 * width * units, transcendentals=0
        ),
    )(place, own, other, *weight, *tables)


def back_kernel(count, started, place_ref, *refs):
    step = pl.program_id(0)
    acts = refs[:count]
    weights = refs[count : 5 * count]
    starts = refs[5 * count : 5 * count + 2] if started else None
    mine_ref, theirs_ref = refs[-2:]
    rows = mine_ref.shape[0]

    def run(part):
        total = sum(dot_trans(a[...], weights[4 * i + part][...]) for i, a in enumerate(acts))
        first = place_ref[0] == 0
        mine = jnp.where(first, total[:rows], total[rows:])
        theirs = jnp.where(first, total[rows:], total[:rows])
        if started:
            mine = mine + starts[0][...].astype(f32)
            theirs = theirs + starts[1][...].astype(f32)
        mine_ref[...] = mine.astype(mine_ref.dtype)
        theirs_ref[...] = theirs.astype(theirs_ref.dtype)

    for part in range(4):
        pl.when(step // (pl.num_programs(0) // 4) == part)(functools.partial(run, part))


def back(place, acts, weights, starts=None, kinds=(f32, bf16)):
    rows = acts[0].shape[0]
    depth = weights[0][0].shape[0]
    width = 4 * depth
    block = min(BLOCK, depth)
    per = depth // block
    half = pl.BlockSpec((rows // 2, block), lambda j, s: (0, j))
    specs = [pl.BlockSpec(a.shape, lambda j, s: (0, 0)) for a in acts]
    for weight in weights:
        for p in range(4):
            specs.append(
                pl.BlockSpec(
                    (block, weight[p].shape[1]),
                    lambda j, s, p=p: (jnp.clip(j - p * per, 0, per - 1), 0),
                )
            )
    operands = [*acts, *(piece for weight in weights for piece in weight)]
    if starts is not None:
        specs += [half, half]
        operands += starts
    units = sum(a.shape[1] for a in acts)
    return pl.pallas_call(
        functools.partial(back_kernel, len(acts), starts is not None),
        grid_spec=pltpu.PrefetchScalarGridSpec(
            num_scalar_prefetch=1, grid=(4 * per,), in_specs=specs, out_specs=[half, half]
        ),
        out_shape=[jax.ShapeDtypeStruct((rows // 2, width), kind) for kind in kinds],
        compiler_params=pltpu.CompilerParams(vmem_limit_bytes=VMEM),
        cost_estimate=pl.CostEstimate(
            flops=2 * rows * width * units, bytes_accessed=2 * width * units, transcendentals=0
        ),
    )(place, *operands)


def grad_kernel(which, added, *refs):
    step, steps = pl.program_id(0), pl.num_programs(0)
    acts = refs[: max(which) + 1]
    count = len(which)
    grads = refs[len(acts) : len(acts) + count]
    others = refs[len(acts) + count : len(acts) + 2 * count]
    for i in range(count):
        total = dot_inner(acts[which[i]][...], grads[i][...])
        if not added:
            refs[i - count][...] = total.astype(bf16)
            continue
        total = (total + others[i][...].astype(f32)).astype(bf16)
        sent_ref, kept_ref = refs[i - 2 * count], refs[i - count]

        @pl.when(step < steps // 2)
        def _():
            sent_ref[...] = total

        @pl.when(step >= steps // 2)
        def _():
            kept_ref[...] = total


def grad(acts, which, grads, added=None):
    tokens, width = acts[0].shape
    block = min(BLOCK, width // 4)
    steps = width // 2 // block
    half = steps // 2
    if added is None:
        row = lambda j: j + steps
    else:
        row = lambda j: (j + half) % steps
    specs = [pl.BlockSpec((tokens, block), lambda j: (0, row(j))) for _ in acts]
    specs += [pl.BlockSpec(g.shape, lambda j: (0, 0)) for g in grads]
    operands = [*acts, *grads]
    if added is None:
        outs = [pl.BlockSpec((block, g.shape[1]), lambda j: (j, 0)) for g in grads]
        shapes = [jax.ShapeDtypeStruct((width // 2, g.shape[1]), bf16) for g in grads]
    else:
        specs += [pl.BlockSpec((block, g.shape[1]), lambda j: (row(j), 0)) for g in grads]
        operands += added
        outs = [pl.BlockSpec((block, g.shape[1]), lambda j: (jnp.minimum(j, half - 1), 0)) for g in grads]
        outs += [pl.BlockSpec((block, g.shape[1]), lambda j: (jnp.maximum(j - half, 0), 0)) for g in grads]
        shapes = [jax.ShapeDtypeStruct((width // 4, g.shape[1]), bf16) for g in grads] * 2
    units = sum(g.shape[1] for g in grads)
    return pl.pallas_call(
        functools.partial(grad_kernel, which, added is not None),
        grid=(steps,),
        in_specs=specs,
        out_specs=outs,
        out_shape=shapes,
        compiler_params=pltpu.CompilerParams(vmem_limit_bytes=VMEM),
        cost_estimate=pl.CostEstimate(
            flops=tokens * width * units, bytes_accessed=width * units, transcendentals=0
        ),
    )(*operands)


def tie(array, *earlier):
    return lax.optimization_barrier((array,) + earlier)[0]


class Order:
    def __init__(self, last):
        self.last = last

    def after(self, array):
        return tie(array, self.last)

    def __call__(self, compute, *operands):
        operands = lax.optimization_barrier((*operands, self.last))[:-1]
        result = compute(*operands)
        self.last = result[0] if isinstance(result, (tuple, list)) else result
        return result


def chunk_edges(width):
    blocks = width // BLOCK
    return [width * 0] + [BLOCK * (blocks * (i + 1) // CHUNKS) for i in range(CHUNKS)]


def make_shards(outer):
    def relative(array):
        rows, width = array.shape
        blocks = array.reshape(rows, outer, 2, 2, width // (4 * outer))
        blocks = jnp.where(lax.axis_index("x") == 0, blocks, blocks[:, :, ::-1])
        blocks = jnp.where(lax.axis_index("core") == 0, blocks, blocks[:, :, :, ::-1])
        return blocks.transpose(0, 3, 2, 1, 4).reshape(rows, width)

    def natural(array):
        rows, width = array.shape
        blocks = array.reshape(rows, 2, 2, outer, width // (4 * outer)).transpose(0, 3, 2, 1, 4)
        blocks = jnp.where(lax.axis_index("x") == 0, blocks, blocks[:, :, ::-1])
        blocks = jnp.where(lax.axis_index("core") == 0, blocks, blocks[:, :, :, ::-1])
        return blocks.reshape(rows, width)

    def spread(along):
        across = lax.ppermute(along, "x", SWAP)
        return [along, across, lax.ppermute(along, "core", SWAP), lax.ppermute(across, "core", SWAP)]

    def total(vector):
        for axis in ("core", "x", "tensor"):
            vector = vector + lax.ppermute(vector, axis, SWAP)
        step = 1
        while step < outer:
            vector = vector + lax.ppermute(vector, "z", [(i, i ^ step) for i in range(outer)])
            step *= 2
        return vector

    def join(own, other):
        first = lax.axis_index("tensor") == 0
        return jnp.concatenate([jnp.where(first, own, other), jnp.where(first, other, own)], axis=0)

    def swap(own):
        return lax.ppermute(own, "tensor", SWAP)

    def shards(
        tokens,
        segments,
        q_weight,
        k_weight,
        v_weight,
        o_weight,
        attention_gain,
        gate_weight,
        up_weight,
        down_weight,
        feed_gain,
        out_grad,
    ):
        query_width = q_weight.shape[1]
        key_width = k_weight.shape[1]
        score_scale = HEAD_DIM ** (-0.5)
        place = lax.axis_index("tensor").astype(jnp.int32).reshape(1)
        here = jnp.zeros((1,), jnp.int32)
        edges = chunk_edges(gate_weight.shape[1])

        def gathered(operand):
            return lax.all_gather(operand, "z", axis=0, tiled=True)

        def chunk(weight, i):
            return weight[:, edges[i] : edges[i + 1]]

        along = {}
        along["qkv"] = gathered(jnp.concatenate([q_weight, k_weight, v_weight], axis=1))

        attention_gain = relative(attention_gain[None])
        feed_gain = relative(feed_gain[None])
        inputs = relative(tokens).astype(f32)
        inverse_first = inverse_rms(inputs)
        normed_first = (inputs * inverse_first * attention_gain).astype(bf16)
        along["o"] = gathered(o_weight)
        normed_other = swap(normed_first)
        along["gate", 0] = gathered(tie(chunk(gate_weight, 0), normed_first))
        out_grad = relative(tie(out_grad, normed_first))
        grad_other = swap(out_grad)
        along["up", 0] = gathered(tie(chunk(up_weight, 0), out_grad))
        segment_row = segments[0]
        cosine, sine = rotary_tables(segment_row)
        first_seen = first_blocks(segment_row)

        full = {"qkv": spread(along["qkv"])}
        order = Order(out_grad)
        rotated = order(
            lambda a, b, *w: project(
                place, a, b, w[:4], (cosine, sine), (query_width + key_width) // 128
            ),
            normed_first, normed_other, *full["qkv"],
        )
        along["down", 0] = gathered(order.after(chunk(down_weight, 0)))
        full["o"] = spread(order.after(along["o"]))
        mixed, log_totals = order(
            lambda a: attend(a, query_width, first_seen, segment_row, score_scale), rotated
        )
        along["gate", 1] = gathered(order.after(chunk(gate_weight, 1)))
        full["gate", 0] = spread(order.after(along["gate", 0]))
        own, sent = order(lambda m, *w: back(place, (m,), (w,)), mixed, *full["o"])
        other = swap(sent)
        along["up", 1] = gathered(order.after(chunk(up_weight, 1)))
        full["up", 0] = spread(order.after(along["up", 0]))

        def feed_norm(inputs, own, other):
            middle = inputs + own + other.astype(f32)
            inverse = inverse_rms(middle)
            return (middle * inverse * feed_gain).astype(bf16), middle, inverse

        normed_second, middle, inverse_second = order(feed_norm, inputs, own, other)
        along["down", 1] = gathered(order.after(chunk(down_weight, 1)))
        normed_other_second = swap(normed_second)
        full["down", 0] = spread(order.after(along["down", 0]))
        grad_seq = order(lambda a, b: jnp.concatenate([a, b], axis=0), out_grad, grad_other)
        normed_feed = order(
            lambda a, b: jnp.concatenate([a, b], axis=0), normed_second, normed_other_second
        )
        names = ("gate", "up", "down")
        hidden, gate_grad, up_grad = {}, {}, {}
        from_core, from_x, kept, summed = {}, {}, {}, {}

        def run_feed(i):
            pieces = [piece for name in names for piece in full[name, i]]
            hidden[i], gate_grad[i], up_grad[i] = order(
                lambda n, g, *w: feed(n, g, w[:4], w[4:8], w[8:]), normed_feed, grad_seq, *pieces
            )

        def chunk_grads(i):
            return gate_grad[i], up_grad[i], hidden[i]

        def core_part(i):
            parts = order(
                lambda n, g, *d: grad((n, g), (0, 0, 1), d), normed_feed, grad_seq, *chunk_grads(i)
            )
            from_core[i] = [lax.ppermute(part, "core", SWAP) for part in parts]

        def x_part(i):
            parts = order(
                lambda n, g, *d: grad((n, g), (0, 0, 1), d[:3], d[3:]),
                normed_feed, grad_seq, *chunk_grads(i), *from_core[i],
            )
            from_x[i] = [lax.ppermute(part, "x", SWAP) for part in parts[:3]]
            kept[i] = parts[3:]

        def add(a, b):
            return (a.astype(f32) + b.astype(f32)).astype(bf16)

        def scattered(part):
            return lax.psum_scatter(part, "z", scatter_dimension=0, tiled=True)

        def finish(i, at):
            summed[names[at], i] = scattered(order(add, kept[i][at], from_x[i][at]))

        def feed_back(i, starts):
            return order(
                lambda a, b, *w: back(here, (a, b), (w[:4], w[4:8]), w[8:] or None, (f32, starts and bf16 or f32)),
                gate_grad[i], up_grad[i], *full["gate", i], *full["up", i], *starts,
            )

        def block_back(i, starts):
            return order(
                lambda a, *w: back(here, (a,), (w[:4],), w[4:] or None, (f32, starts and bf16 or f32)),
                hidden[i], *full["down", i], *starts,
            )

        run_feed(0)
        full["gate", 1] = spread(order.after(along["gate", 1]))
        core_part(0)
        starts = feed_back(0, [])
        full["up", 1] = spread(order.after(along["up", 1]))
        x_part(0)
        block_starts = block_back(0, [])
        full["down", 1] = spread(order.after(along["down", 1]))
        run_feed(1)
        own, sent = feed_back(1, starts)
        other = swap(sent)
        core_part(1)
        finish(0, 0)
        finish(0, 1)
        x_part(1)
        finish(0, 2)

        def middle_back(own, other, middle, out_grad):
            feed_normed_grad = own + other.astype(f32)
            middle_grad = out_grad.astype(f32) + norm_back(
                middle, inverse_second, feed_gain, feed_normed_grad
            )
            gain_part = jnp.sum(feed_normed_grad * middle * inverse_second, axis=0)
            return middle_grad.astype(bf16), middle_grad, gain_part

        attn_out_grad, middle_grad, feed_gain_part = order(middle_back, own, other, middle, out_grad)
        attn_other = swap(attn_out_grad)
        block_own, block_sent = block_back(1, block_starts)
        block_other = swap(block_sent)
        finish(1, 0)
        mixed_grad = order(lambda a, b, *w: project(place, a, b, w), attn_out_grad, attn_other, *full["o"])
        attn_grad_seq = order(join, attn_out_grad, attn_other)
        (part,) = order(lambda a, m: grad((a,), (0,), (m,)), attn_grad_seq, mixed)
        from_core["o"] = lax.ppermute(part, "core", SWAP)
        finish(1, 1)
        part, kept["o"] = order(
            lambda a, m, c: grad((a,), (0,), (m,), (c,)), attn_grad_seq, mixed, from_core["o"]
        )
        from_x["o"] = lax.ppermute(part, "x", SWAP)
        qkv_grad = order(
            lambda r, g, l: jnp.concatenate(
                attend_back(
                    r, g, l, query_width, first_seen, segment_row, cosine, sine, score_scale
                ),
                axis=1,
            ),
            rotated, mixed_grad, log_totals,
        )
        normed_seq = order(join, normed_first, normed_other)
        (part,) = order(lambda a, m: grad((a,), (0,), (m,)), normed_seq, qkv_grad)
        from_core["qkv"] = lax.ppermute(part, "core", SWAP)
        own, sent = order(lambda g, *w: back(place, (g,), (w,)), qkv_grad, *full["qkv"])
        other = swap(sent)
        finish(1, 2)
        part, kept["qkv"] = order(
            lambda a, m, c: grad((a,), (0,), (m,), (c,)), normed_seq, qkv_grad, from_core["qkv"]
        )
        from_x["qkv"] = lax.ppermute(part, "x", SWAP)
        summed["o"] = scattered(order(add, kept["o"], from_x["o"]))
        block_out = order(
            lambda m, a, b: natural((m + a + b.astype(f32)).astype(bf16)), middle, block_own, block_other
        )

        def input_back(own, other, inputs, middle_grad):
            normed_grad = own + other.astype(f32)
            input_grad = middle_grad + norm_back(inputs, inverse_first, attention_gain, normed_grad)
            gain_part = jnp.sum(normed_grad * inputs * inverse_first, axis=0)
            return input_grad.astype(bf16), gain_part

        input_grad, attention_gain_part = order(input_back, own, other, inputs, middle_grad)
        summed["qkv"] = scattered(order(add, kept["qkv"], from_x["qkv"]))
        gains = total(natural(jnp.stack([attention_gain_part, feed_gain_part])))
        qkv_weight_grad = summed["qkv"].astype(f32)

        def whole(name):
            return jnp.concatenate([summed[name, i] for i in range(CHUNKS)], axis=1).astype(f32)

        return (
            block_out,
            natural(input_grad),
            qkv_weight_grad[:, :query_width],
            qkv_weight_grad[:, query_width : query_width + key_width],
            qkv_weight_grad[:, query_width + key_width :],
            summed["o"].astype(f32),
            gains[0],
            whole("gate"),
            whole("up"),
            whole("down"),
            gains[1],
        )

    return shards


def solution(mesh):
    outer = mesh.shape["dp"] // 4
    fine = Mesh(
        mesh.devices.reshape(outer, 2, 2, mesh.shape["tensor"]), ("z", "x", "core", "tensor")
    )
    dp = ("z", "x", "core")
    every = P(dp + ("tensor",), None)
    weight = P(dp, "tensor")
    return jax.shard_map(
        make_shards(outer),
        mesh=fine,
        in_specs=(
            every,
            P(dp, None),
            weight,
            weight,
            weight,
            weight,
            P(),
            weight,
            weight,
            weight,
            P(),
            every,
        ),
        out_specs=(every, every, weight, weight, weight, weight, P(), weight, weight, weight, P()),
        check_vma=False,
    )
```

```python
import functools

import jax
import jax.numpy as jnp
from jax import lax
from jax.experimental import pallas as pl
from jax.experimental.pallas import tpu as pltpu
from jax.sharding import Mesh, PartitionSpec as P

HEAD_DIM = 64
SWAP = ((0, 1), (1, 0))
QUERIES = 256
CHUNKS = 4
BLOCK = 256
ROW_STEPS = 3
COST = 10**11
VMEM = 48 * 2**20
epsilon = 1e-05
rope_base = 10000.0
bf16 = jnp.bfloat16
f32 = jnp.float32


def dot_plain(left, right):
    return jnp.dot(left, right, preferred_element_type=f32)


def dot_trans(left, right):
    return lax.dot_general(left, right, (((1,), (1,)), ((), ())), preferred_element_type=f32)


def dot_inner(left, right):
    return lax.dot_general(left, right, (((0,), (0,)), ((), ())), preferred_element_type=f32)


def rotary_tables(segment_row):
    length = segment_row.shape[0]
    before = jnp.sum((segment_row[None, :] < segment_row[:, None]).astype(jnp.int32), axis=1)
    places = (jnp.arange(length, dtype=jnp.int32) - before).astype(f32)
    half_dim = HEAD_DIM // 2
    frequency = rope_base ** (-2.0 * jnp.arange(half_dim).astype(f32) / HEAD_DIM)
    angles = places[:, None] * frequency[None, :]
    cosine, sine = jnp.cos(angles), jnp.sin(angles)
    return (jnp.concatenate([cosine] * 4, axis=1), jnp.concatenate([-sine, sine] * 2, axis=1))


def first_blocks(segment_row):
    starts, ends = segment_row[::QUERIES], segment_row[QUERIES - 1 :: QUERIES]
    return jnp.sum((ends[None, :] < starts[:, None]).astype(jnp.int32), axis=1)


def lanes_of(shape):
    return lax.broadcasted_iota(jnp.int32, shape, len(shape) - 1)


def turn(block, cosine, sine):
    low_half = lanes_of(block.shape) % HEAD_DIM < HEAD_DIM // 2
    other = jnp.where(low_half, pltpu.roll(block, 96, 1), pltpu.roll(block, 32, 1))
    return block * cosine + other * sine


def widen(pair_ref, wide_ref, group):
    pair = pair_ref[...]
    keep = (lanes_of(pair.shape) < HEAD_DIM) == (group == 0)
    half = jnp.where(keep, pair, pltpu.roll(pair.astype(f32), HEAD_DIM, 1).astype(bf16))
    wide_ref[:, :128] = half
    wide_ref[:, 128:] = half


def seen_bias(col_ref, row_ref, start, keys, step):
    queries = col_ref.shape[0]
    same = col_ref[...] == row_ref[:, pl.ds(start, keys)]
    q_at = lax.broadcasted_iota(jnp.int32, (queries, keys), 0) + step * queries
    k_at = lax.broadcasted_iota(jnp.int32, (queries, keys), 1) + start
    return jnp.where(same & (q_at >= k_at), 0.0, -1e30).astype(f32)


def forward_kernel(scale, low_ref, q_ref, k_ref, v_ref, col_ref, row_ref, o_ref, lse_ref, kw_ref, vw_ref):
    group, step = pl.program_id(0), pl.program_id(1)
    queries = q_ref.shape[0]

    @pl.when(step == 0)
    def _():
        widen(k_ref, kw_ref, group)
        widen(v_ref, vw_ref, group)

    def run(blocks):
        keys = blocks * queries
        start = pl.multiple_of(low_ref[step] * queries, queries)
        bias = seen_bias(col_ref, row_ref, start, keys, step)
        key = kw_ref[pl.ds(start, keys), :]
        value = vw_ref[pl.ds(start, keys), :]
        head_of = lanes_of((queries, 256)) // HEAD_DIM
        lse = jnp.zeros((queries, 128), f32)
        for quad in range(q_ref.shape[1] // 256):
            wide = q_ref[:, quad * 256 : quad * 256 + 256]
            out = jnp.zeros((queries, 256), f32)
            for j in range(4):
                one = jnp.where(head_of == j, wide, jnp.zeros_like(wide))
                scores = dot_trans(one, key) * scale + bias
                top = jnp.max(scores, axis=1, keepdims=True)
                powers = jnp.exp(scores - top)
                sums = jnp.sum(powers, axis=1, keepdims=True)
                prob = (powers * (1.0 / sums)).astype(bf16)
                out = jnp.where(head_of == j, dot_plain(prob, value), out)
                lse = jnp.where(lanes_of(lse.shape) == quad * 4 + j, top + jnp.log(sums), lse)
            o_ref[:, quad * 256 : quad * 256 + 256] = out.astype(bf16)
        lse_ref[...] = lse

    for blocks in range(1, row_ref.shape[1] // queries + 1):
        pl.when(step + 1 - low_ref[step] == blocks)(functools.partial(run, blocks))


def backward_kernel(
    scale, low_ref, q_ref, k_ref, v_ref, g_ref, lse_ref, col_ref, row_ref, cos_ref, sin_ref, kcos_ref, ksin_ref,
    dq_ref, dk_ref, dv_ref, kw_ref, vw_ref, dkw_ref, dvw_ref,
):
    group, step = pl.program_id(0), pl.program_id(1)
    queries = q_ref.shape[0]

    @pl.when(step == 0)
    def _():
        widen(k_ref, kw_ref, group)
        widen(v_ref, vw_ref, group)
        dkw_ref[...] = jnp.zeros_like(dkw_ref)
        dvw_ref[...] = jnp.zeros_like(dvw_ref)

    def run(blocks):
        keys = blocks * queries
        start = pl.multiple_of(low_ref[step] * queries, queries)
        bias = seen_bias(col_ref, row_ref, start, keys, step)
        key = kw_ref[pl.ds(start, keys), :]
        value = vw_ref[pl.ds(start, keys), :]
        head_of = lanes_of((queries, 256)) // HEAD_DIM
        cosine, sine = cos_ref[...], sin_ref[...]
        for quad in range(q_ref.shape[1] // 256):
            wide = q_ref[:, quad * 256 : quad * 256 + 256]
            grads = g_ref[:, quad * 256 : quad * 256 + 256]
            out = jnp.zeros((queries, 256), f32)
            for j in range(4):
                at = quad * 4 + j
                one = jnp.where(head_of == j, wide, jnp.zeros_like(wide))
                grad = jnp.where(head_of == j, grads, jnp.zeros_like(grads))
                prob = jnp.exp(dot_trans(one, key) * scale + bias - lse_ref[:, at : at + 1])
                prob_grad = dot_trans(grad, value)
                centre = jnp.sum(prob * prob_grad, axis=1, keepdims=True)
                score_grad = (prob * (prob_grad - centre) * scale).astype(bf16)
                dvw_ref[pl.ds(start, keys), :] += dot_inner(prob.astype(bf16), grad)
                dkw_ref[pl.ds(start, keys), :] += dot_inner(score_grad, one)
                out = jnp.where(head_of == j, dot_plain(score_grad, key), out)
            for half in range(2):
                piece = turn(out[:, half * 128 : half * 128 + 128], cosine, -sine)
                dq_ref[:, quad * 256 + half * 128 : quad * 256 + half * 128 + 128] = piece.astype(bf16)

    for blocks in range(1, row_ref.shape[1] // queries + 1):
        pl.when(step + 1 - low_ref[step] == blocks)(functools.partial(run, blocks))

    @pl.when(step == pl.num_programs(1) - 1)
    def _():
        mine = (lanes_of(dk_ref.shape) < HEAD_DIM) == (group == 0)

        def fold(ref):
            pair = ref[:, :128] + ref[:, 128:]
            return pair + pltpu.roll(pair, HEAD_DIM, 1)

        dk = turn(fold(dkw_ref), kcos_ref[...], -ksin_ref[...]).astype(bf16)
        dk_ref[...] = jnp.where(mine, dk, dk_ref[...])
        dv_ref[...] = jnp.where(mine, fold(dvw_ref).astype(bf16), dv_ref[...])


def launch(kernel, scalars, operands, deps, grid, in_specs, out_specs, out_shape, scratch=(), aliases=()):
    count = len(scalars) + len(operands)

    def body(*refs):
        kernel(*refs[:count], *refs[count + len(deps) :])

    return pl.pallas_call(
        body,
        grid_spec=pltpu.PrefetchScalarGridSpec(
            num_scalar_prefetch=len(scalars),
            grid=grid,
            in_specs=[*in_specs, *([pl.BlockSpec(memory_space=pl.ANY)] * len(deps))],
            out_specs=out_specs,
            scratch_shapes=scratch,
        ),
        out_shape=out_shape,
        compiler_params=pltpu.CompilerParams(vmem_limit_bytes=VMEM),
        cost_estimate=pl.CostEstimate(flops=COST, bytes_accessed=1024, transcendentals=0),
        input_output_aliases=dict(aliases),
    )(*scalars, *operands, *deps)


def whole_block(array):
    return pl.BlockSpec(array.shape, lambda *at: (0,) * array.ndim)


def weight_columns(weight, column):
    both, across, across_core = weight
    depth = across.shape[0]
    specs = [
        pl.BlockSpec((depth, BLOCK), lambda j, s: (s[1], column(j))),
        pl.BlockSpec((depth, BLOCK), lambda j, s: (0, column(j))),
        pl.BlockSpec((depth, BLOCK), lambda j, s: (1 - s[1], column(j))),
        pl.BlockSpec((depth, BLOCK), lambda j, s: (0, column(j))),
    ]
    return specs, [both, across, both, across_core]


def weight_rows(weight, block, units, at):
    both, across, across_core = weight
    per = across.shape[0] // block

    def spec(quarter):
        def index(j, s):
            row = jnp.clip(j - quarter * per, 0, per - 1)
            if quarter % 2 == 0:
                row = row + per * (s[1] if quarter == 0 else 1 - s[1])
            return row, at

        return pl.BlockSpec((block, units), index)

    return [spec(quarter) for quarter in range(4)], [both, across, both, across_core]


def stack_kernel(*refs):
    first = 0
    for ref in refs[:-1]:
        refs[-1][:, first : first + ref.shape[1]] = ref[...]
        first += ref.shape[1]


def stack(parts, deps):
    shape = (parts[0].shape[0], sum(p.shape[1] for p in parts))
    return launch(
        stack_kernel,
        [],
        parts,
        deps,
        (1,),
        [whole_block(p) for p in parts],
        pl.BlockSpec(shape, lambda j: (0, 0)),
        jax.ShapeDtypeStruct(shape, bf16),
    )


def own_kernel(spot_ref, both_ref, out_ref):
    out_ref[...] = both_ref[...]


def own_rows(spot, both, deps):
    rows, width = both.shape
    steps = 4
    block = rows // 2 // steps
    return launch(
        own_kernel,
        [spot],
        [both],
        deps,
        (steps,),
        [pl.BlockSpec((block, width), lambda j, s: (s[1] * steps + j, 0))],
        pl.BlockSpec((block, width), lambda j, s: (j, 0)),
        jax.ShapeDtypeStruct((rows // 2, width), bf16),
    )


def gate_kernel(in_ref, out_ref):
    pass


def gate(array, deps):
    anywhere = pl.BlockSpec(memory_space=pl.ANY)
    return launch(
        gate_kernel,
        [],
        [array],
        deps,
        (1,),
        [anywhere],
        anywhere,
        jax.ShapeDtypeStruct(array.shape, array.dtype),
        aliases=((0, 0),),
    )


def product(act_ref, parts):
    depth = parts[0].shape[0]
    return sum(
        dot_plain(act_ref[:, i * depth : i * depth + depth], part[...]) for i, part in enumerate(parts)
    )


def feed_kernel(spot_ref, x_ref, g_ref, *refs):
    pieces, (h_ref, gg_ref, ug_ref) = refs[:12], refs[12:]
    gate = product(x_ref, pieces[:4])
    up = product(x_ref, pieces[4:8])
    sigmoid = jax.nn.sigmoid(gate)
    silu = gate * sigmoid
    h_ref[...] = (silu * up).astype(bf16)
    grad = product(g_ref, pieces[8:])
    gg_ref[...] = (grad * up * (sigmoid * (1.0 + gate * (1.0 - sigmoid)))).astype(bf16)
    ug_ref[...] = (grad * silu).astype(bf16)


def feed(spot, normed, grads, weight, deps):
    rows, width = normed.shape
    units = weight[0].shape[1] // 3
    blocks = units // BLOCK
    specs, operands = [whole_block(normed), whole_block(grads)], [normed, grads]
    for at in range(3):
        more = weight_columns(weight, lambda j, at=at: j + at * blocks)
        specs += more[0]
        operands += more[1]
    return launch(
        feed_kernel,
        [spot],
        operands,
        deps,
        (blocks,),
        specs,
        [pl.BlockSpec((rows, BLOCK), lambda j, s: (0, j))] * 3,
        [jax.ShapeDtypeStruct((rows, units), bf16)] * 3,
    )


def project_kernel(rotated, spot_ref, own_ref, other_ref, *refs):
    parts, out_ref = refs[:4], refs[-1]
    rows = own_ref.shape[0]
    for act_ref, place in ((own_ref, spot_ref[0]), (other_ref, 1 - spot_ref[0])):
        at = pl.ds(pl.multiple_of(place * rows, rows), rows)
        total = product(act_ref, parts)
        if rotated is None:
            out_ref[at, :] = total.astype(bf16)
        else:
            cosine, sine = refs[4][at, :], refs[5][at, :]
            for half in range(2):
                piece = total[:, half * 128 : half * 128 + 128]
                keep = 2 * pl.program_id(0) + half >= rotated
                piece = jnp.where(keep, piece, turn(piece, cosine, sine))
                out_ref[at, half * 128 : half * 128 + 128] = piece.astype(bf16)


def project(spot, own, other, weight, deps, tables=(), rotated=None):
    rows, width = own.shape
    units = weight[0].shape[1]
    specs, operands = weight_columns(weight, lambda j: j)
    return launch(
        functools.partial(project_kernel, rotated),
        [spot],
        [own, other, *operands, *tables],
        deps,
        (units // BLOCK,),
        [whole_block(own), whole_block(other), *specs, *(whole_block(t) for t in tables)],
        pl.BlockSpec((2 * rows, BLOCK), lambda j, s: (0, j)),
        jax.ShapeDtypeStruct((2 * rows, units), bf16),
    )


def back_kernel(count, started, placed, spot_ref, *refs):
    step = pl.program_id(0)
    acts = refs[:count]
    weights = refs[count : 5 * count]
    starts = refs[5 * count : 5 * count + 2] if started else None
    mine_ref, theirs_ref = refs[-2:]
    rows = mine_ref.shape[0]

    def run(part):
        total = sum(dot_trans(a[...], weights[4 * i + part][...]) for i, a in enumerate(acts))
        mine, theirs = total[:rows], total[rows:]
        if placed:
            first = spot_ref[0] == 0
            mine, theirs = jnp.where(first, mine, theirs), jnp.where(first, theirs, mine)
        if started:
            mine = mine + starts[0][...].astype(f32)
            theirs = theirs + starts[1][...].astype(f32)
        mine_ref[...] = mine.astype(mine_ref.dtype)
        theirs_ref[...] = theirs.astype(theirs_ref.dtype)

    for part in range(4):
        pl.when(step // (pl.num_programs(0) // 4) == part)(functools.partial(run, part))


def back(spot, acts, weights, deps, placed=False, starts=(), kinds=(f32, bf16)):
    rows = acts[0].shape[0]
    depth = weights[0][0][1].shape[0]
    width = 4 * depth
    block = min(BLOCK, depth)
    half = pl.BlockSpec((rows // 2, block), lambda j, s: (0, j))
    specs, operands = [whole_block(a) for a in acts], list(acts)
    for act, (weight, at) in zip(acts, weights):
        more = weight_rows(weight, block, act.shape[1], at)
        specs += more[0]
        operands += more[1]
    return launch(
        functools.partial(back_kernel, len(acts), len(starts) > 0, placed),
        [spot],
        [*operands, *starts],
        deps,
        (width // block,),
        [*specs, *([half] * len(starts))],
        [half, half],
        [jax.ShapeDtypeStruct((rows // 2, width), kind) for kind in kinds],
    )


def grad_kernel(which, added, *refs):
    step, steps = pl.program_id(0), pl.num_programs(0)
    acts = refs[: max(which) + 1]
    count = len(which)
    grads = refs[len(acts) : len(acts) + count]
    first = 0
    for i in range(count):
        at = slice(first, first + grads[i].shape[1])
        first = at.stop
        total = dot_inner(acts[which[i]][...], grads[i][...])
        if not added:
            refs[-1][:, at] = total.astype(bf16)
            continue
        total = (total + refs[-3][:, at].astype(f32)).astype(bf16)

        @pl.when(step < steps // 2)
        def _():
            refs[-2][:, at] = total

        @pl.when(step >= steps // 2)
        def _():
            refs[-1][:, at] = total


def grad(acts, which, grads, deps, added=None):
    tokens, width = acts[0].shape
    block = min(BLOCK, width // 4)
    steps = width // 2 // block
    half = steps // 2
    units = sum(g.shape[1] for g in grads)
    if added is None:
        row = lambda j: j + steps
        outs = pl.BlockSpec((block, units), lambda j: (j, 0))
        shapes = jax.ShapeDtypeStruct((width // 2, units), bf16)
    else:
        row = lambda j: (j + half) % steps
        outs = [
            pl.BlockSpec((block, units), lambda j: (jnp.minimum(j, half - 1), 0)),
            pl.BlockSpec((block, units), lambda j: (jnp.maximum(j - half, 0), 0)),
        ]
        shapes = [jax.ShapeDtypeStruct((width // 4, units), bf16)] * 2
    specs = [pl.BlockSpec((tokens, block), lambda j: (0, row(j))) for _ in acts]
    specs += [whole_block(g) for g in grads]
    operands = [*acts, *grads]
    if added is not None:
        specs.append(pl.BlockSpec((block, units), lambda j: (row(j), 0)))
        operands.append(added)
    return launch(
        functools.partial(grad_kernel, which, added is not None),
        [],
        operands,
        deps,
        (steps,),
        specs,
        outs,
        shapes,
    )


def attention_specs(length, queries, wide):
    pair = lambda first: pl.BlockSpec((length, 128), lambda g, i, low: (0, first))
    col = pl.BlockSpec((queries, 1), lambda g, i, low: (i, 0))
    row = pl.BlockSpec((1, length), lambda g, i, low: (0, 0))
    return pl.BlockSpec((queries, wide), lambda g, i, low: (i, g)), pair, col, row


def attend(rotated, query_width, first_seen, segment_row, scale, deps):
    length = rotated.shape[0]
    queries = length // first_seen.shape[0]
    groups = 2
    heads, pair, col, row = attention_specs(length, queries, query_width // groups)
    first = query_width // 128
    return launch(
        functools.partial(forward_kernel, scale),
        [first_seen],
        [rotated, rotated, rotated, segment_row.reshape(length, 1), segment_row.reshape(1, length)],
        deps,
        (groups, length // queries),
        [heads, pair(first), pair(first + 1), col, row],
        [heads, pl.BlockSpec((queries, 128), lambda g, i, low: (i, g))],
        [
            jax.ShapeDtypeStruct((length, query_width), bf16),
            jax.ShapeDtypeStruct((length, groups * 128), f32),
        ],
        [pltpu.VMEM((length, 256), bf16)] * 2,
    )


def attend_back(rotated, grads, lse, query_width, first_seen, segment_row, cosine, sine, scale, deps):
    length = rotated.shape[0]
    queries = length // first_seen.shape[0]
    groups = 2
    heads, pair, col, row = attention_specs(length, queries, query_width // groups)
    first = query_width // 128
    table = pl.BlockSpec((queries, 128), lambda g, i, low: (i, 0))
    return launch(
        functools.partial(backward_kernel, scale),
        [first_seen],
        [
            rotated, rotated, rotated, grads, lse, segment_row.reshape(length, 1),
            segment_row.reshape(1, length), cosine, sine, cosine, sine,
        ],
        deps,
        (groups, length // queries),
        [
            heads, pair(first), pair(first + 1), heads,
            pl.BlockSpec((queries, 128), lambda g, i, low: (i, g)), col, row, table, table, pair(0), pair(0),
        ],
        [heads, pair(0), pair(0)],
        [
            jax.ShapeDtypeStruct((length, query_width), bf16),
            jax.ShapeDtypeStruct((length, 128), bf16),
            jax.ShapeDtypeStruct((length, 128), bf16),
        ],
        [pltpu.VMEM((length, 256), bf16)] * 2 + [pltpu.VMEM((length, 256), f32)] * 2,
    )


def join_kernel(spot_ref, own_ref, other_ref, out_ref):
    rows = own_ref.shape[0]
    for ref, place in ((own_ref, spot_ref[0]), (other_ref, 1 - spot_ref[0])):
        out_ref[pl.ds(pl.multiple_of(place * rows, rows), rows), :] = ref[...]


def join(spot, own, other, deps):
    rows, width = own.shape
    block = width // 4
    half = pl.BlockSpec((rows, block), lambda j, s: (0, j))
    return launch(
        join_kernel,
        [spot],
        [own, other],
        deps,
        (4,),
        [half, half],
        pl.BlockSpec((2 * rows, block), lambda j, s: (0, j)),
        jax.ShapeDtypeStruct((2 * rows, width), bf16),
    )


def add_kernel(a_ref, b_ref, out_ref):
    out_ref[...] = (a_ref[...].astype(f32) + b_ref[...].astype(f32)).astype(bf16)


def add(a, b, deps):
    rows, width = a.shape
    block = pl.BlockSpec((rows // 4, width), lambda j: (j, 0))
    return launch(
        add_kernel, [], [a, b], deps, (4,), [block, block], block, jax.ShapeDtypeStruct(a.shape, bf16)
    )


def natural_block(spot_ref, outer, core, x, z):
    x = 1 - spot_ref[2] if x else spot_ref[2]
    core = 1 - spot_ref[1] if core else spot_ref[1]
    return (z * 2 + x) * 2 + core


def reorder(spot_ref, outer, width):
    size = width // (4 * outer)
    for core in range(2):
        for x in range(2):
            for z in range(outer):
                at = ((core * 2 + x) * outer + z) * size
                there = natural_block(spot_ref, outer, core, x, z) * size
                yield slice(at, at + size), pl.ds(pl.multiple_of(there, size), size)


def inverse_rms(activity):
    return lax.rsqrt(jnp.mean(activity * activity, axis=-1, keepdims=True) + epsilon)


def norm_back(activity, inverse, gain_vec, incoming):
    scaled = incoming * gain_vec
    return inverse * scaled - activity * (inverse * inverse * inverse) * jnp.mean(
        scaled * activity, axis=-1, keepdims=True
    )


def enter_kernel(outer, spot_ref, tokens_ref, gain_ref, out_ref, normed_ref):
    if outer:
        for here, there in reorder(spot_ref, outer, tokens_ref.shape[1]):
            out_ref[:, here] = tokens_ref[:, there]
    else:
        out_ref[...] = tokens_ref[...]
    inputs = out_ref[...].astype(f32)
    normed_ref[...] = (inputs * inverse_rms(inputs) * gain_ref[...]).astype(bf16)


def turn_kernel(outer, spot_ref, array_ref, out_ref):
    for here, there in reorder(spot_ref, outer, array_ref.shape[1]):
        out_ref[:, here] = array_ref[:, there]


def rows_spec(rows, width):
    return pl.BlockSpec((rows // ROW_STEPS, width), lambda j, *s: (j, 0))


def enter(spot, outer, tokens, gain, deps):
    spec = rows_spec(*tokens.shape)
    return launch(
        functools.partial(enter_kernel, outer),
        [spot],
        [tokens, gain],
        deps,
        (ROW_STEPS,),
        [spec, whole_block(gain)],
        [spec, spec],
        [jax.ShapeDtypeStruct(tokens.shape, bf16)] * 2,
    )


def to_order(spot, outer, array, deps):
    spec = rows_spec(*array.shape)
    return launch(
        functools.partial(turn_kernel, outer),
        [spot],
        [array],
        deps,
        (ROW_STEPS,),
        [spec],
        spec,
        jax.ShapeDtypeStruct(array.shape, bf16),
    )


def middle_kernel(tokens_ref, own_ref, other_ref, gain_ref, normed_ref, middle_ref):
    middle = tokens_ref[...].astype(f32) + own_ref[...] + other_ref[...].astype(f32)
    middle_ref[...] = middle
    normed_ref[...] = (middle * inverse_rms(middle) * gain_ref[...]).astype(bf16)


def middle_forward(tokens, own, other, gain, deps):
    spec = rows_spec(*tokens.shape)
    return launch(
        middle_kernel,
        [],
        [tokens, own, other, gain],
        deps,
        (ROW_STEPS,),
        [spec, spec, spec, whole_block(gain)],
        [spec, spec],
        [jax.ShapeDtypeStruct(tokens.shape, bf16), jax.ShapeDtypeStruct(tokens.shape, f32)],
    )


def gain_part(part_ref, product):
    @pl.when(pl.program_id(0) == 0)
    def _():
        part_ref[...] = jnp.zeros_like(part_ref)

    part_ref[...] += jnp.sum(product, axis=0, keepdims=True)


def middle_back_kernel(own_ref, other_ref, middle_ref, grad_ref, gain_ref, low_ref, out_ref, part_ref):
    incoming = own_ref[...] + other_ref[...].astype(f32)
    middle = middle_ref[...]
    inverse = inverse_rms(middle)
    out = grad_ref[...].astype(f32) + norm_back(middle, inverse, gain_ref[...], incoming)
    out_ref[...] = out
    low_ref[...] = out.astype(bf16)
    gain_part(part_ref, incoming * middle * inverse)


def middle_backward(own, other, middle, out_grad, gain, deps):
    spec = rows_spec(*own.shape)
    part = jax.ShapeDtypeStruct(gain.shape, f32)
    return launch(
        middle_back_kernel,
        [],
        [own, other, middle, out_grad, gain],
        deps,
        (ROW_STEPS,),
        [spec, spec, spec, spec, whole_block(gain)],
        [spec, spec, whole_block(gain)],
        [jax.ShapeDtypeStruct(own.shape, bf16), jax.ShapeDtypeStruct(own.shape, f32), part],
    )


def leave(outer, spot_ref, out_ref, value):
    value = value.astype(bf16)
    if outer:
        for here, there in reorder(spot_ref, outer, value.shape[1]):
            out_ref[:, there] = value[:, here]
    else:
        out_ref[...] = value


def block_out_kernel(outer, spot_ref, middle_ref, own_ref, other_ref, out_ref):
    leave(outer, spot_ref, out_ref, middle_ref[...] + own_ref[...] + other_ref[...].astype(f32))


def block_result(spot, outer, middle, own, other, deps):
    spec = rows_spec(*own.shape)
    return launch(
        functools.partial(block_out_kernel, outer),
        [spot],
        [middle, own, other],
        deps,
        (ROW_STEPS,),
        [spec, spec, spec],
        spec,
        jax.ShapeDtypeStruct(own.shape, bf16),
    )


def input_back_kernel(outer, spot_ref, own_ref, other_ref, tokens_ref, grad_ref, gain_ref, out_ref, part_ref):
    incoming = own_ref[...] + other_ref[...].astype(f32)
    inputs = tokens_ref[...].astype(f32)
    inverse = inverse_rms(inputs)
    leave(outer, spot_ref, out_ref, grad_ref[...] + norm_back(inputs, inverse, gain_ref[...], incoming))
    gain_part(part_ref, incoming * inputs * inverse)


def input_backward(spot, outer, own, other, tokens, middle_grad, gain, deps):
    spec = rows_spec(*own.shape)
    return launch(
        functools.partial(input_back_kernel, outer),
        [spot],
        [own, other, tokens, middle_grad, gain],
        deps,
        (ROW_STEPS,),
        [spec, spec, spec, spec, whole_block(gain)],
        [spec, whole_block(gain)],
        [jax.ShapeDtypeStruct(own.shape, bf16), jax.ShapeDtypeStruct(gain.shape, f32)],
    )


class Order:
    def __init__(self):
        self.before = []

    def wait(self, *arrays):
        self.before += arrays

    def __call__(self, compute, *operands, **options):
        result = compute(*operands, deps=self.before, **options)
        self.before = [result[0] if isinstance(result, (tuple, list)) else result]
        return result


def chunk_edges(width):
    blocks = width // BLOCK
    return [BLOCK * (-(-blocks * i // CHUNKS)) for i in range(CHUNKS + 1)]


def make_shards(outer):
    def relative(array):
        rows, width = array.shape
        blocks = array.reshape(rows, outer, 2, 2, width // (4 * outer))
        blocks = jnp.where(lax.axis_index("x") == 0, blocks, blocks[:, :, ::-1])
        blocks = jnp.where(lax.axis_index("core") == 0, blocks, blocks[:, :, :, ::-1])
        return blocks.transpose(0, 3, 2, 1, 4).reshape(rows, width)

    def natural(array):
        rows, width = array.shape
        blocks = array.reshape(rows, 2, 2, outer, width // (4 * outer)).transpose(0, 3, 2, 1, 4)
        blocks = jnp.where(lax.axis_index("x") == 0, blocks, blocks[:, :, ::-1])
        blocks = jnp.where(lax.axis_index("core") == 0, blocks, blocks[:, :, :, ::-1])
        return blocks.reshape(rows, width)

    def over_x(array):
        return lax.ppermute(array, "x", SWAP)

    def over_core(array):
        return lax.ppermute(array, "core", SWAP)

    def gather(operand):
        return lax.all_gather(operand, ("core", "z"), axis=0, tiled=True)

    def scatter(operand):
        return lax.psum_scatter(operand, "z", scatter_dimension=0, tiled=True)

    def total(vector):
        for axis in ("core", "x", "tensor"):
            vector = vector + lax.ppermute(vector, axis, SWAP)
        step = 1
        while step < outer:
            vector = vector + lax.ppermute(vector, "z", [(i, i ^ step) for i in range(outer)])
            step *= 2
        return vector

    def swap(own):
        return lax.ppermute(own, "tensor", SWAP)

    def shards(
        tokens,
        segments,
        q_weight,
        k_weight,
        v_weight,
        o_weight,
        attention_gain,
        gate_weight,
        up_weight,
        down_weight,
        feed_gain,
        out_grad,
    ):
        query_width = q_weight.shape[1]
        key_width = k_weight.shape[1]
        score_scale = HEAD_DIM ** (-0.5)
        place, core, cross = (lax.axis_index(axis) for axis in ("tensor", "core", "x"))
        spot = jnp.stack([place, core, cross]).astype(jnp.int32)
        here = jnp.zeros_like(spot)
        edges = chunk_edges(gate_weight.shape[1])
        order = Order()
        along, full = {}, {}

        def spread(name):
            full[name] = over_x(order(lambda deps: own_rows(spot, along[name], deps)))

        def land(name):
            across = order(lambda deps: gate(full[name], deps))
            full[name] = (along[name], across, over_core(across))

        def chunk(i):
            columns = slice(edges[i], edges[i + 1])
            parts = [w[:, columns] for w in (gate_weight, up_weight, down_weight)]
            along[i] = gather(order(lambda deps: stack(parts, deps)))

        tiles = outer if tokens.shape[1] // (4 * outer) % 128 == 0 else 0
        along["o"] = gather(o_weight)
        along["qkv"] = gather(order(lambda deps: stack([q_weight, k_weight, v_weight], deps)))
        for i in range(CHUNKS):
            chunk(i)
        attention_gain = relative(attention_gain[None])
        feed_gain = relative(feed_gain[None])
        if not tiles:
            tokens, out_grad = relative(tokens), relative(out_grad)
        tokens, normed_first = order(lambda deps: enter(spot, tiles, tokens, attention_gain, deps))
        normed_other = swap(normed_first)
        if tiles:
            out_grad = order(lambda deps: to_order(spot, tiles, out_grad, deps))
        grad_other = swap(out_grad)
        segment_row = segments[0]
        cosine, sine = rotary_tables(segment_row)
        first_seen = first_blocks(segment_row)
        spread("o")
        spread("qkv")
        land("o")
        grad_seq = order(lambda deps: join(here, out_grad, grad_other, deps))
        normed_seq = order(lambda deps: join(spot, normed_first, normed_other, deps))
        land("qkv")
        rotated = order(
            lambda deps: project(
                spot, normed_first, normed_other, full["qkv"], deps, (cosine, sine),
                (query_width + key_width) // 128,
            )
        )
        spread(0)
        mixed, log_totals = order(
            lambda deps: attend(rotated, query_width, first_seen, segment_row, score_scale, deps)
        )
        own, sent = order(lambda deps: back(spot, (mixed,), ((full["o"], 0),), deps, True))
        other = swap(sent)
        spread(1)
        land(0)
        normed_second, middle = order(lambda deps: middle_forward(tokens, own, other, feed_gain, deps))
        normed_third = swap(normed_second)
        spread(2)
        normed_feed = order(lambda deps: join(here, normed_second, normed_third, deps))
        land(1)
        hidden, gate_grad, up_grad = {}, {}, {}
        from_core, to_x, from_x, kept, summed = {}, {}, {}, {}, {}

        def run_feed(i):
            hidden[i], gate_grad[i], up_grad[i] = order(
                lambda deps: feed(spot, normed_feed, grad_seq, full[i], deps)
            )

        def core_part(i):
            grads = (gate_grad[i], up_grad[i], hidden[i])
            part = order(lambda deps: grad((normed_feed, grad_seq), (0, 0, 1), grads, deps))
            from_core[i] = over_core(part)

        def x_part(i):
            grads = (gate_grad[i], up_grad[i], hidden[i])
            to_x[i], kept[i] = order(
                lambda deps: grad((normed_feed, grad_seq), (0, 0, 1), grads, deps, from_core[i])
            )

        def send_x(i):
            from_x[i] = over_x(to_x[i])

        def finish(i):
            summed[i] = scatter(order(lambda deps: add(kept[i], from_x[i], deps))).astype(f32)

        def feed_back(chunks, starts, kinds):
            acts = [a[i] for i in chunks for a in (gate_grad, up_grad)]
            weights = [(full[i], at) for i in chunks for at in (0, 1)]
            return order(
                lambda deps: back(spot, acts, weights, deps, starts=starts, kinds=kinds)
            )

        run_feed(0)
        core_part(0)
        run_feed(1)
        spread(3)
        x_part(0)
        kept_along, sent_along = scatter(kept[0]), scatter(to_x[0])
        core_part(1)
        land(2)
        x_part(1)
        send_x(1)
        run_feed(2)
        core_part(2)
        starts = feed_back((0, 1, 2), (), (f32, f32))
        land(3)
        run_feed(3)
        own, sent = feed_back((3,), starts, (f32, bf16))
        other = swap(sent)
        x_part(2)
        send_x(2)
        core_part(3)
        from_along = over_x(sent_along)
        finish(1)
        x_part(3)
        send_x(3)
        attn_out_grad, middle_grad, feed_gain_part = order(
            lambda deps: middle_backward(own, other, middle, out_grad, feed_gain, deps)
        )
        attn_other = swap(attn_out_grad)
        order.wait(from_along)
        block_own, block_sent = order(
            lambda deps: back(
                spot, [hidden[i] for i in range(CHUNKS)], [(full[i], 2) for i in range(CHUNKS)], deps
            )
        )
        block_other = swap(block_sent)
        finish(2)
        attn_grad_seq = order(lambda deps: join(spot, attn_out_grad, attn_other, deps))
        from_core["o"] = over_core(order(lambda deps: grad((attn_grad_seq,), (0,), (mixed,), deps)))
        mixed_grad = order(lambda deps: project(spot, attn_out_grad, attn_other, full["o"], deps))
        to_x["o"], kept["o"] = order(
            lambda deps: grad((attn_grad_seq,), (0,), (mixed,), deps, from_core["o"])
        )
        send_x("o")
        qkv_grad = order(
            lambda deps: attend_back(
                rotated, mixed_grad, log_totals, query_width, first_seen, segment_row, cosine, sine,
                score_scale, deps,
            )
        )
        from_core["qkv"] = over_core(
            order(lambda deps: grad((normed_seq,), (0,) * 3, qkv_grad, deps))
        )
        order.wait(block_other)
        finish(3)
        finish("o")
        to_x["qkv"], kept["qkv"] = order(
            lambda deps: grad((normed_seq,), (0,) * 3, qkv_grad, deps, from_core["qkv"])
        )
        send_x("qkv")
        places = (0, query_width // key_width, query_width // key_width + 1)
        own, sent = order(
            lambda deps: back(spot, qkv_grad, [(full["qkv"], at) for at in places], deps, True)
        )
        other = swap(sent)
        block_out = order(lambda deps: block_result(spot, tiles, middle, block_own, block_other, deps))
        finish("qkv")
        input_grad, attention_gain_part = order(
            lambda deps: input_backward(spot, tiles, own, other, tokens, middle_grad, attention_gain, deps)
        )
        gains = total(natural(jnp.concatenate([attention_gain_part, feed_gain_part], axis=0)))
        if not tiles:
            block_out, input_grad = natural(block_out), natural(input_grad)
        summed[0] = kept_along.astype(f32) + from_along.astype(f32)
        qkv_weight_grad = summed["qkv"]

        def whole(at):
            parts = []
            for i in range(CHUNKS):
                units = edges[i + 1] - edges[i]
                parts.append(summed[i][:, at * units : at * units + units])
            return jnp.concatenate(parts, axis=1)

        return (
            block_out,
            input_grad,
            qkv_weight_grad[:, :query_width],
            qkv_weight_grad[:, query_width : query_width + key_width],
            qkv_weight_grad[:, query_width + key_width :],
            summed["o"],
            gains[0],
            whole(0),
            whole(1),
            whole(2),
            gains[1],
        )

    return shards


def solution(mesh):
    outer = mesh.shape["dp"] // 4
    fine = Mesh(
        mesh.devices.reshape(outer, 2, 2, mesh.shape["tensor"]), ("z", "x", "core", "tensor")
    )
    dp = ("z", "x", "core")
    every = P(dp + ("tensor",), None)
    weight = P(dp, "tensor")
    return jax.shard_map(
        make_shards(outer),
        mesh=fine,
        in_specs=(
            every,
            P(dp, None),
            weight,
            weight,
            weight,
            weight,
            P(),
            weight,
            weight,
            weight,
            P(),
            every,
        ),
        out_specs=(every, every, weight, weight, weight, weight, P(), weight, weight, weight, P()),
        check_vma=False,
    )
```

```python
import functools

import jax
import jax.numpy as jnp
from jax import lax
from jax.experimental import pallas as pl
from jax.experimental.pallas import tpu as pltpu
from jax.sharding import Mesh, PartitionSpec as P

HEAD_DIM = 64
SWAP = ((0, 1), (1, 0))
QUERIES = 256
CHUNKS = 4
BLOCK = 256
ROW_STEPS = 3
COST = 10**10
SHORT = 0.01
VMEM = 48 * 2**20
epsilon = 1e-05
rope_base = 10000.0
bf16 = jnp.bfloat16
f32 = jnp.float32


def dot_plain(left, right):
    return jnp.dot(left, right, preferred_element_type=f32)


def dot_trans(left, right):
    return lax.dot_general(left, right, (((1,), (1,)), ((), ())), preferred_element_type=f32)


def dot_inner(left, right):
    return lax.dot_general(left, right, (((0,), (0,)), ((), ())), preferred_element_type=f32)


def rotary_tables(segment_row):
    length = segment_row.shape[0]
    before = jnp.sum((segment_row[None, :] < segment_row[:, None]).astype(jnp.int32), axis=1)
    places = (jnp.arange(length, dtype=jnp.int32) - before).astype(f32)
    half_dim = HEAD_DIM // 2
    frequency = rope_base ** (-2.0 * jnp.arange(half_dim).astype(f32) / HEAD_DIM)
    angles = places[:, None] * frequency[None, :]
    cosine, sine = jnp.cos(angles), jnp.sin(angles)
    return (jnp.concatenate([cosine] * 4, axis=1), jnp.concatenate([-sine, sine] * 2, axis=1))


def first_blocks(segment_row):
    starts, ends = segment_row[::QUERIES], segment_row[QUERIES - 1 :: QUERIES]
    return jnp.sum((ends[None, :] < starts[:, None]).astype(jnp.int32), axis=1)


def lanes_of(shape):
    return lax.broadcasted_iota(jnp.int32, shape, len(shape) - 1)


def turn(block, cosine, sine):
    low_half = lanes_of(block.shape) % HEAD_DIM < HEAD_DIM // 2
    other = jnp.where(low_half, pltpu.roll(block, 96, 1), pltpu.roll(block, 32, 1))
    return block * cosine + other * sine


def widen(pair_ref, wide_ref, group):
    pair = pair_ref[...]
    keep = (lanes_of(pair.shape) < HEAD_DIM) == (group == 0)
    half = jnp.where(keep, pair, pltpu.roll(pair.astype(f32), HEAD_DIM, 1).astype(bf16))
    wide_ref[:, :128] = half
    wide_ref[:, 128:] = half


def seen_bias(col_ref, row_ref, start, keys, step):
    queries = col_ref.shape[0]
    same = col_ref[...] == row_ref[:, pl.ds(start, keys)]
    q_at = lax.broadcasted_iota(jnp.int32, (queries, keys), 0) + step * queries
    k_at = lax.broadcasted_iota(jnp.int32, (queries, keys), 1) + start
    return jnp.where(same & (q_at >= k_at), 0.0, -1e30).astype(f32)


def forward_kernel(scale, low_ref, q_ref, k_ref, v_ref, col_ref, row_ref, o_ref, lse_ref, kw_ref, vw_ref):
    group, step = pl.program_id(0), pl.program_id(1)
    queries = q_ref.shape[0]

    @pl.when(step == 0)
    def _():
        widen(k_ref, kw_ref, group)
        widen(v_ref, vw_ref, group)

    def run(blocks):
        keys = blocks * queries
        start = pl.multiple_of(low_ref[step] * queries, queries)
        bias = seen_bias(col_ref, row_ref, start, keys, step)
        key = kw_ref[pl.ds(start, keys), :]
        value = vw_ref[pl.ds(start, keys), :]
        head_of = lanes_of((queries, 256)) // HEAD_DIM
        lse = jnp.zeros((queries, 128), f32)
        for quad in range(q_ref.shape[1] // 256):
            wide = q_ref[:, quad * 256 : quad * 256 + 256]
            out = jnp.zeros((queries, 256), f32)
            for j in range(4):
                one = jnp.where(head_of == j, wide, jnp.zeros_like(wide))
                scores = dot_trans(one, key) * scale + bias
                top = jnp.max(scores, axis=1, keepdims=True)
                powers = jnp.exp(scores - top)
                sums = jnp.sum(powers, axis=1, keepdims=True)
                prob = (powers * (1.0 / sums)).astype(bf16)
                out = jnp.where(head_of == j, dot_plain(prob, value), out)
                lse = jnp.where(lanes_of(lse.shape) == quad * 4 + j, top + jnp.log(sums), lse)
            o_ref[:, quad * 256 : quad * 256 + 256] = out.astype(bf16)
        lse_ref[...] = lse

    for blocks in range(1, row_ref.shape[1] // queries + 1):
        pl.when(step + 1 - low_ref[step] == blocks)(functools.partial(run, blocks))


def backward_kernel(
    scale, low_ref, q_ref, k_ref, v_ref, g_ref, lse_ref, col_ref, row_ref, cos_ref, sin_ref, kcos_ref, ksin_ref,
    dq_ref, dk_ref, dv_ref, kw_ref, vw_ref, dkw_ref, dvw_ref,
):
    group, step = pl.program_id(0), pl.program_id(1)
    queries = q_ref.shape[0]

    @pl.when(step == 0)
    def _():
        widen(k_ref, kw_ref, group)
        widen(v_ref, vw_ref, group)
        dkw_ref[...] = jnp.zeros_like(dkw_ref)
        dvw_ref[...] = jnp.zeros_like(dvw_ref)

    def run(blocks):
        keys = blocks * queries
        start = pl.multiple_of(low_ref[step] * queries, queries)
        bias = seen_bias(col_ref, row_ref, start, keys, step)
        key = kw_ref[pl.ds(start, keys), :]
        value = vw_ref[pl.ds(start, keys), :]
        head_of = lanes_of((queries, 256)) // HEAD_DIM
        cosine, sine = cos_ref[...], sin_ref[...]
        for quad in range(q_ref.shape[1] // 256):
            wide = q_ref[:, quad * 256 : quad * 256 + 256]
            grads = g_ref[:, quad * 256 : quad * 256 + 256]
            out = jnp.zeros((queries, 256), f32)
            for j in range(4):
                at = quad * 4 + j
                one = jnp.where(head_of == j, wide, jnp.zeros_like(wide))
                grad = jnp.where(head_of == j, grads, jnp.zeros_like(grads))
                prob = jnp.exp(dot_trans(one, key) * scale + bias - lse_ref[:, at : at + 1])
                prob_grad = dot_trans(grad, value)
                centre = jnp.sum(prob * prob_grad, axis=1, keepdims=True)
                score_grad = (prob * (prob_grad - centre) * scale).astype(bf16)
                dvw_ref[pl.ds(start, keys), :] += dot_inner(prob.astype(bf16), grad)
                dkw_ref[pl.ds(start, keys), :] += dot_inner(score_grad, one)
                out = jnp.where(head_of == j, dot_plain(score_grad, key), out)
            for half in range(2):
                piece = turn(out[:, half * 128 : half * 128 + 128], cosine, -sine)
                dq_ref[:, quad * 256 + half * 128 : quad * 256 + half * 128 + 128] = piece.astype(bf16)

    for blocks in range(1, row_ref.shape[1] // queries + 1):
        pl.when(step + 1 - low_ref[step] == blocks)(functools.partial(run, blocks))

    @pl.when(step == pl.num_programs(1) - 1)
    def _():
        mine = (lanes_of(dk_ref.shape) < HEAD_DIM) == (group == 0)

        def fold(ref):
            pair = ref[:, :128] + ref[:, 128:]
            return pair + pltpu.roll(pair, HEAD_DIM, 1)

        dk = turn(fold(dkw_ref), kcos_ref[...], -ksin_ref[...]).astype(bf16)
        dk_ref[...] = jnp.where(mine, dk, dk_ref[...])
        dv_ref[...] = jnp.where(mine, fold(dvw_ref).astype(bf16), dv_ref[...])


def launch(kernel, scalars, operands, deps, grid, in_specs, out_specs, out_shape, scratch=(), aliases=(), us=3):
    count = len(scalars) + len(operands)

    def body(*refs):
        kernel(*refs[:count], *refs[count + len(deps) :])

    return pl.pallas_call(
        body,
        grid_spec=pltpu.PrefetchScalarGridSpec(
            num_scalar_prefetch=len(scalars),
            grid=grid,
            in_specs=[*in_specs, *([pl.BlockSpec(memory_space=pl.ANY)] * len(deps))],
            out_specs=out_specs,
            scratch_shapes=scratch,
        ),
        out_shape=out_shape,
        compiler_params=pltpu.CompilerParams(vmem_limit_bytes=VMEM),
        cost_estimate=pl.CostEstimate(flops=int(COST * us), bytes_accessed=1024, transcendentals=0),
        input_output_aliases=dict(aliases),
    )(*scalars, *operands, *deps)


def whole_block(array):
    return pl.BlockSpec(array.shape, lambda *at: (0,) * array.ndim)


def weight_columns(weight, column):
    both, across, across_core = weight
    depth = across.shape[0]
    specs = [
        pl.BlockSpec((depth, BLOCK), lambda j, s: (s[1], column(j))),
        pl.BlockSpec((depth, BLOCK), lambda j, s: (0, column(j))),
        pl.BlockSpec((depth, BLOCK), lambda j, s: (1 - s[1], column(j))),
        pl.BlockSpec((depth, BLOCK), lambda j, s: (0, column(j))),
    ]
    return specs, [both, across, both, across_core]


def weight_rows(weight, block, units, at):
    both, across, across_core = weight
    per = across.shape[0] // block

    def spec(quarter):
        def index(j, s):
            row = jnp.clip(j - quarter * per, 0, per - 1)
            if quarter % 2 == 0:
                row = row + per * (s[1] if quarter == 0 else 1 - s[1])
            return row, at

        return pl.BlockSpec((block, units), index)

    return [spec(quarter) for quarter in range(4)], [both, across, both, across_core]


def stack_kernel(*refs):
    first = 0
    for ref in refs[:-1]:
        refs[-1][:, first : first + ref.shape[1]] = ref[...]
        first += ref.shape[1]


def stack(parts, deps):
    shape = (parts[0].shape[0], sum(p.shape[1] for p in parts))
    return launch(
        stack_kernel,
        [],
        parts,
        deps,
        (1,),
        [whole_block(p) for p in parts],
        pl.BlockSpec(shape, lambda j: (0, 0)),
        jax.ShapeDtypeStruct(shape, bf16),
        us=1.5,
    )


def own_kernel(spot_ref, both_ref, out_ref):
    out_ref[...] = both_ref[...]


def own_rows(spot, both, deps):
    rows, width = both.shape
    steps = 4
    block = rows // 2 // steps
    return launch(
        own_kernel,
        [spot],
        [both],
        deps,
        (steps,),
        [pl.BlockSpec((block, width), lambda j, s: (s[1] * steps + j, 0))],
        pl.BlockSpec((block, width), lambda j, s: (j, 0)),
        jax.ShapeDtypeStruct((rows // 2, width), bf16),
        us=4,
    )


def gate_kernel(in_ref, out_ref):
    pass


def gate(array, deps):
    anywhere = pl.BlockSpec(memory_space=pl.ANY)
    return launch(
        gate_kernel,
        [],
        [array],
        deps,
        (1,),
        [anywhere],
        anywhere,
        jax.ShapeDtypeStruct(array.shape, array.dtype),
        aliases=((0, 0),),
        us=1,
    )


def product(act_ref, parts):
    depth = parts[0].shape[0]
    return sum(
        dot_plain(act_ref[:, i * depth : i * depth + depth], part[...]) for i, part in enumerate(parts)
    )


def feed_kernel(spot_ref, x_ref, g_ref, *refs):
    pieces, (h_ref, gg_ref, ug_ref) = refs[:12], refs[12:]
    gate = product(x_ref, pieces[:4])
    up = product(x_ref, pieces[4:8])
    sigmoid = jax.nn.sigmoid(gate)
    silu = gate * sigmoid
    h_ref[...] = (silu * up).astype(bf16)
    grad = product(g_ref, pieces[8:])
    gg_ref[...] = (grad * up * (sigmoid * (1.0 + gate * (1.0 - sigmoid)))).astype(bf16)
    ug_ref[...] = (grad * silu).astype(bf16)


def feed(spot, normed, grads, weight, deps):
    rows, width = normed.shape
    units = weight[0].shape[1] // 3
    blocks = units // BLOCK
    specs, operands = [whole_block(normed), whole_block(grads)], [normed, grads]
    for at in range(3):
        more = weight_columns(weight, lambda j, at=at: j + at * blocks)
        specs += more[0]
        operands += more[1]
    return launch(
        feed_kernel,
        [spot],
        operands,
        deps,
        (blocks,),
        specs,
        [pl.BlockSpec((rows, BLOCK), lambda j, s: (0, j))] * 3,
        [jax.ShapeDtypeStruct((rows, units), bf16)] * 3,
        us=rows * width * units / 10**8,
    )


def project_kernel(rotated, spot_ref, own_ref, other_ref, *refs):
    parts, out_ref = refs[:4], refs[-1]
    rows = own_ref.shape[0]
    for act_ref, place in ((own_ref, spot_ref[0]), (other_ref, 1 - spot_ref[0])):
        at = pl.ds(pl.multiple_of(place * rows, rows), rows)
        total = product(act_ref, parts)
        if rotated is None:
            out_ref[at, :] = total.astype(bf16)
        else:
            cosine, sine = refs[4][at, :], refs[5][at, :]
            for half in range(2):
                piece = total[:, half * 128 : half * 128 + 128]
                keep = 2 * pl.program_id(0) + half >= rotated
                piece = jnp.where(keep, piece, turn(piece, cosine, sine))
                out_ref[at, half * 128 : half * 128 + 128] = piece.astype(bf16)


def project(spot, own, other, weight, deps, tables=(), rotated=None):
    rows, width = own.shape
    units = weight[0].shape[1]
    specs, operands = weight_columns(weight, lambda j: j)
    return launch(
        functools.partial(project_kernel, rotated),
        [spot],
        [own, other, *operands, *tables],
        deps,
        (units // BLOCK,),
        [whole_block(own), whole_block(other), *specs, *(whole_block(t) for t in tables)],
        pl.BlockSpec((2 * rows, BLOCK), lambda j, s: (0, j)),
        jax.ShapeDtypeStruct((2 * rows, units), bf16),
        us=rows * width * units / 10**8,
    )


def back_kernel(count, started, placed, spot_ref, *refs):
    step = pl.program_id(0)
    acts = refs[:count]
    weights = refs[count : 5 * count]
    starts = refs[5 * count : 5 * count + 2] if started else None
    mine_ref, theirs_ref = refs[-2:]
    rows = mine_ref.shape[0]

    def run(part):
        total = sum(dot_trans(a[...], weights[4 * i + part][...]) for i, a in enumerate(acts))
        mine, theirs = total[:rows], total[rows:]
        if placed:
            first = spot_ref[0] == 0
            mine, theirs = jnp.where(first, mine, theirs), jnp.where(first, theirs, mine)
        if started:
            mine = mine + starts[0][...].astype(f32)
            theirs = theirs + starts[1][...].astype(f32)
        mine_ref[...] = mine.astype(mine_ref.dtype)
        theirs_ref[...] = theirs.astype(theirs_ref.dtype)

    for part in range(4):
        pl.when(step // (pl.num_programs(0) // 4) == part)(functools.partial(run, part))


def back(spot, acts, weights, deps, placed=False, starts=(), kinds=(f32, bf16)):
    rows = acts[0].shape[0]
    depth = weights[0][0][1].shape[0]
    width = 4 * depth
    block = min(BLOCK, depth)
    half = pl.BlockSpec((rows // 2, block), lambda j, s: (0, j))
    specs, operands = [whole_block(a) for a in acts], list(acts)
    for act, (weight, at) in zip(acts, weights):
        more = weight_rows(weight, block, act.shape[1], at)
        specs += more[0]
        operands += more[1]
    return launch(
        functools.partial(back_kernel, len(acts), len(starts) > 0, placed),
        [spot],
        [*operands, *starts],
        deps,
        (width // block,),
        [*specs, *([half] * len(starts))],
        [half, half],
        [jax.ShapeDtypeStruct((rows // 2, width), kind) for kind in kinds],
        us=rows * width * sum(a.shape[1] for a in acts) / 285000000,
    )


def grad_kernel(which, added, *refs):
    step, steps = pl.program_id(0), pl.num_programs(0)
    acts = refs[: max(which) + 1]
    count = len(which)
    grads = refs[len(acts) : len(acts) + count]
    first = 0
    for i in range(count):
        at = slice(first, first + grads[i].shape[1])
        first = at.stop
        total = dot_inner(acts[which[i]][...], grads[i][...])
        if not added:
            refs[-1][:, at] = total.astype(bf16)
            continue
        total = (total + refs[-3][:, at].astype(f32)).astype(bf16)

        @pl.when(step < steps // 2)
        def _():
            refs[-2][:, at] = total

        @pl.when(step >= steps // 2)
        def _():
            refs[-1][:, at] = total


def grad(acts, which, grads, deps, added=None, us=None):
    tokens, width = acts[0].shape
    block = min(BLOCK, width // 4)
    steps = width // 2 // block
    half = steps // 2
    units = sum(g.shape[1] for g in grads)
    if added is None:
        row = lambda j: j + steps
        outs = pl.BlockSpec((block, units), lambda j: (j, 0))
        shapes = jax.ShapeDtypeStruct((width // 2, units), bf16)
    else:
        row = lambda j: (j + half) % steps
        outs = [
            pl.BlockSpec((block, units), lambda j: (jnp.minimum(j, half - 1), 0)),
            pl.BlockSpec((block, units), lambda j: (jnp.maximum(j - half, 0), 0)),
        ]
        shapes = [jax.ShapeDtypeStruct((width // 4, units), bf16)] * 2
    specs = [pl.BlockSpec((tokens, block), lambda j: (0, row(j))) for _ in acts]
    specs += [whole_block(g) for g in grads]
    operands = [*acts, *grads]
    if added is not None:
        specs.append(pl.BlockSpec((block, units), lambda j: (row(j), 0)))
        operands.append(added)
    return launch(
        functools.partial(grad_kernel, which, added is not None),
        [],
        operands,
        deps,
        (steps,),
        specs,
        outs,
        shapes,
        us=us or tokens * width * units / 480000000,
    )


def attention_specs(length, queries, wide):
    pair = lambda first: pl.BlockSpec((length, 128), lambda g, i, low: (0, first))
    col = pl.BlockSpec((queries, 1), lambda g, i, low: (i, 0))
    row = pl.BlockSpec((1, length), lambda g, i, low: (0, 0))
    return pl.BlockSpec((queries, wide), lambda g, i, low: (i, g)), pair, col, row


def attend(rotated, query_width, first_seen, segment_row, scale, deps):
    length = rotated.shape[0]
    queries = length // first_seen.shape[0]
    groups = 2
    heads, pair, col, row = attention_specs(length, queries, query_width // groups)
    first = query_width // 128
    return launch(
        functools.partial(forward_kernel, scale),
        [first_seen],
        [rotated, rotated, rotated, segment_row.reshape(length, 1), segment_row.reshape(1, length)],
        deps,
        (groups, length // queries),
        [heads, pair(first), pair(first + 1), col, row],
        [heads, pl.BlockSpec((queries, 128), lambda g, i, low: (i, g))],
        [
            jax.ShapeDtypeStruct((length, query_width), bf16),
            jax.ShapeDtypeStruct((length, groups * 128), f32),
        ],
        [pltpu.VMEM((length, 256), bf16)] * 2,
        us=16,
    )


def attend_back(rotated, grads, lse, query_width, first_seen, segment_row, cosine, sine, scale, deps):
    length = rotated.shape[0]
    queries = length // first_seen.shape[0]
    groups = 2
    heads, pair, col, row = attention_specs(length, queries, query_width // groups)
    first = query_width // 128
    table = pl.BlockSpec((queries, 128), lambda g, i, low: (i, 0))
    return launch(
        functools.partial(backward_kernel, scale),
        [first_seen],
        [
            rotated, rotated, rotated, grads, lse, segment_row.reshape(length, 1),
            segment_row.reshape(1, length), cosine, sine, cosine, sine,
        ],
        deps,
        (groups, length // queries),
        [
            heads, pair(first), pair(first + 1), heads,
            pl.BlockSpec((queries, 128), lambda g, i, low: (i, g)), col, row, table, table, pair(0), pair(0),
        ],
        [heads, pair(0), pair(0)],
        [
            jax.ShapeDtypeStruct((length, query_width), bf16),
            jax.ShapeDtypeStruct((length, 128), bf16),
            jax.ShapeDtypeStruct((length, 128), bf16),
        ],
        [pltpu.VMEM((length, 256), bf16)] * 2 + [pltpu.VMEM((length, 256), f32)] * 2,
        us=35,
    )


def join_kernel(spot_ref, own_ref, other_ref, out_ref):
    rows = own_ref.shape[0]
    for ref, place in ((own_ref, spot_ref[0]), (other_ref, 1 - spot_ref[0])):
        out_ref[pl.ds(pl.multiple_of(place * rows, rows), rows), :] = ref[...]


def join(spot, own, other, deps):
    rows, width = own.shape
    block = width // 4
    half = pl.BlockSpec((rows, block), lambda j, s: (0, j))
    return launch(
        join_kernel,
        [spot],
        [own, other],
        deps,
        (4,),
        [half, half],
        pl.BlockSpec((2 * rows, block), lambda j, s: (0, j)),
        jax.ShapeDtypeStruct((2 * rows, width), bf16),
        us=4,
    )


def add_kernel(a_ref, b_ref, out_ref):
    out_ref[...] = (a_ref[...].astype(f32) + b_ref[...].astype(f32)).astype(out_ref.dtype)


def add(a, b, deps, us=4, kind=bf16):
    rows, width = a.shape
    block = pl.BlockSpec((rows // 4, width), lambda j: (j, 0))
    return launch(
        add_kernel, [], [a, b], deps, (4,), [block, block], block, jax.ShapeDtypeStruct(a.shape, kind), us=us
    )


def natural_block(spot_ref, outer, core, x, z):
    x = 1 - spot_ref[2] if x else spot_ref[2]
    core = 1 - spot_ref[1] if core else spot_ref[1]
    return (z * 2 + x) * 2 + core


def reorder(spot_ref, outer, width):
    size = width // (4 * outer)
    for core in range(2):
        for x in range(2):
            for z in range(outer):
                at = ((core * 2 + x) * outer + z) * size
                there = natural_block(spot_ref, outer, core, x, z) * size
                yield slice(at, at + size), pl.ds(pl.multiple_of(there, size), size)


def inverse_rms(activity):
    return lax.rsqrt(jnp.mean(activity * activity, axis=-1, keepdims=True) + epsilon)


def norm_back(activity, inverse, gain_vec, incoming):
    scaled = incoming * gain_vec
    return inverse * scaled - activity * (inverse * inverse * inverse) * jnp.mean(
        scaled * activity, axis=-1, keepdims=True
    )


def enter_kernel(outer, spot_ref, tokens_ref, gain_ref, out_ref, normed_ref):
    if outer:
        for here, there in reorder(spot_ref, outer, tokens_ref.shape[1]):
            out_ref[:, here] = tokens_ref[:, there]
    else:
        out_ref[...] = tokens_ref[...]
    inputs = out_ref[...].astype(f32)
    normed_ref[...] = (inputs * inverse_rms(inputs) * gain_ref[...]).astype(bf16)


def turn_kernel(outer, spot_ref, array_ref, out_ref):
    for here, there in reorder(spot_ref, outer, array_ref.shape[1]):
        out_ref[:, here] = array_ref[:, there]


def rows_spec(rows, width):
    return pl.BlockSpec((rows // ROW_STEPS, width), lambda j, *s: (j, 0))


def enter(spot, outer, tokens, gain, deps):
    spec = rows_spec(*tokens.shape)
    return launch(
        functools.partial(enter_kernel, outer),
        [spot],
        [tokens, gain],
        deps,
        (ROW_STEPS,),
        [spec, whole_block(gain)],
        [spec, spec],
        [jax.ShapeDtypeStruct(tokens.shape, bf16)] * 2,
        us=3,
    )


def to_order(spot, outer, array, deps):
    spec = rows_spec(*array.shape)
    return launch(
        functools.partial(turn_kernel, outer),
        [spot],
        [array],
        deps,
        (ROW_STEPS,),
        [spec],
        spec,
        jax.ShapeDtypeStruct(array.shape, bf16),
        us=3,
    )


def middle_kernel(tokens_ref, own_ref, other_ref, gain_ref, normed_ref, middle_ref):
    middle = tokens_ref[...].astype(f32) + own_ref[...] + other_ref[...].astype(f32)
    middle_ref[...] = middle
    normed_ref[...] = (middle * inverse_rms(middle) * gain_ref[...]).astype(bf16)


def middle_forward(tokens, own, other, gain, deps):
    spec = rows_spec(*tokens.shape)
    return launch(
        middle_kernel,
        [],
        [tokens, own, other, gain],
        deps,
        (ROW_STEPS,),
        [spec, spec, spec, whole_block(gain)],
        [spec, spec],
        [jax.ShapeDtypeStruct(tokens.shape, bf16), jax.ShapeDtypeStruct(tokens.shape, f32)],
        us=5,
    )


def gain_part(part_ref, product):
    @pl.when(pl.program_id(0) == 0)
    def _():
        part_ref[...] = jnp.zeros_like(part_ref)

    part_ref[...] += jnp.sum(product, axis=0, keepdims=True)


def middle_back_kernel(own_ref, other_ref, middle_ref, grad_ref, gain_ref, low_ref, out_ref, part_ref):
    incoming = own_ref[...] + other_ref[...].astype(f32)
    middle = middle_ref[...]
    inverse = inverse_rms(middle)
    out = grad_ref[...].astype(f32) + norm_back(middle, inverse, gain_ref[...], incoming)
    out_ref[...] = out
    low_ref[...] = out.astype(bf16)
    gain_part(part_ref, incoming * middle * inverse)


def middle_backward(own, other, middle, out_grad, gain, deps):
    spec = rows_spec(*own.shape)
    part = jax.ShapeDtypeStruct(gain.shape, f32)
    return launch(
        middle_back_kernel,
        [],
        [own, other, middle, out_grad, gain],
        deps,
        (ROW_STEPS,),
        [spec, spec, spec, spec, whole_block(gain)],
        [spec, spec, whole_block(gain)],
        [jax.ShapeDtypeStruct(own.shape, bf16), jax.ShapeDtypeStruct(own.shape, f32), part],
        us=8,
    )


def leave(outer, spot_ref, out_ref, value):
    value = value.astype(bf16)
    if outer:
        for here, there in reorder(spot_ref, outer, value.shape[1]):
            out_ref[:, there] = value[:, here]
    else:
        out_ref[...] = value


def block_out_kernel(outer, spot_ref, middle_ref, own_ref, other_ref, out_ref):
    leave(outer, spot_ref, out_ref, middle_ref[...] + own_ref[...] + other_ref[...].astype(f32))


def block_result(spot, outer, middle, own, other, deps):
    spec = rows_spec(*own.shape)
    return launch(
        functools.partial(block_out_kernel, outer),
        [spot],
        [middle, own, other],
        deps,
        (ROW_STEPS,),
        [spec, spec, spec],
        spec,
        jax.ShapeDtypeStruct(own.shape, bf16),
        us=5,
    )


def input_back_kernel(outer, spot_ref, own_ref, other_ref, tokens_ref, grad_ref, gain_ref, out_ref, part_ref):
    incoming = own_ref[...] + other_ref[...].astype(f32)
    inputs = tokens_ref[...].astype(f32)
    inverse = inverse_rms(inputs)
    leave(outer, spot_ref, out_ref, grad_ref[...] + norm_back(inputs, inverse, gain_ref[...], incoming))
    gain_part(part_ref, incoming * inputs * inverse)


def input_backward(spot, outer, own, other, tokens, middle_grad, gain, deps):
    spec = rows_spec(*own.shape)
    return launch(
        functools.partial(input_back_kernel, outer),
        [spot],
        [own, other, tokens, middle_grad, gain],
        deps,
        (ROW_STEPS,),
        [spec, spec, spec, spec, whole_block(gain)],
        [spec, whole_block(gain)],
        [jax.ShapeDtypeStruct(own.shape, bf16), jax.ShapeDtypeStruct(gain.shape, f32)],
        us=7,
    )


class Order:
    def __init__(self):
        self.before = []

    def wait(self, *arrays):
        self.before += arrays

    def __call__(self, compute, *operands, **options):
        result = compute(*operands, deps=self.before, **options)
        self.before = [result[0] if isinstance(result, (tuple, list)) else result]
        return result


def chunk_edges(width):
    blocks = width // BLOCK
    return [BLOCK * (-(-blocks * i // CHUNKS)) for i in range(CHUNKS + 1)]


def make_shards(outer):
    def relative(array):
        rows, width = array.shape
        blocks = array.reshape(rows, outer, 2, 2, width // (4 * outer))
        blocks = jnp.where(lax.axis_index("x") == 0, blocks, blocks[:, :, ::-1])
        blocks = jnp.where(lax.axis_index("core") == 0, blocks, blocks[:, :, :, ::-1])
        return blocks.transpose(0, 3, 2, 1, 4).reshape(rows, width)

    def natural(array):
        rows, width = array.shape
        blocks = array.reshape(rows, 2, 2, outer, width // (4 * outer)).transpose(0, 3, 2, 1, 4)
        blocks = jnp.where(lax.axis_index("x") == 0, blocks, blocks[:, :, ::-1])
        blocks = jnp.where(lax.axis_index("core") == 0, blocks, blocks[:, :, :, ::-1])
        return blocks.reshape(rows, width)

    def over_x(array):
        return lax.ppermute(array, "x", SWAP)

    def over_core(array):
        return lax.ppermute(array, "core", SWAP)

    def gather(operand):
        return lax.all_gather(operand, ("core", "z"), axis=0, tiled=True)

    def scatter(operand):
        return lax.psum_scatter(operand, "z", scatter_dimension=0, tiled=True)

    def total(vector):
        for axis in ("core", "x", "tensor"):
            vector = vector + lax.ppermute(vector, axis, SWAP)
        step = 1
        while step < outer:
            vector = vector + lax.ppermute(vector, "z", [(i, i ^ step) for i in range(outer)])
            step *= 2
        return vector

    def swap(own):
        return lax.ppermute(own, "tensor", SWAP)

    def shards(
        tokens,
        segments,
        q_weight,
        k_weight,
        v_weight,
        o_weight,
        attention_gain,
        gate_weight,
        up_weight,
        down_weight,
        feed_gain,
        out_grad,
    ):
        query_width = q_weight.shape[1]
        key_width = k_weight.shape[1]
        score_scale = HEAD_DIM ** (-0.5)
        place, core, cross = (lax.axis_index(axis) for axis in ("tensor", "core", "x"))
        spot = jnp.stack([place, core, cross]).astype(jnp.int32)
        here = jnp.zeros_like(spot)
        edges = chunk_edges(gate_weight.shape[1])
        order = Order()
        along, full = {}, {}

        def spread(name):
            full[name] = over_x(order(lambda deps: own_rows(spot, along[name], deps)))

        def land(name):
            across = order(lambda deps: gate(full[name], deps))
            full[name] = (along[name], across, over_core(across))

        def chunk(i):
            columns = slice(edges[i], edges[i + 1])
            parts = [w[:, columns] for w in (gate_weight, up_weight, down_weight)]
            along[i] = gather(order(lambda deps: stack(parts, deps)))

        tiles = outer if tokens.shape[1] // (4 * outer) % 128 == 0 else 0
        along["o"] = gather(o_weight)
        along["qkv"] = gather(order(lambda deps: stack([q_weight, k_weight, v_weight], deps)))
        for i in range(CHUNKS):
            chunk(i)
        attention_gain = relative(attention_gain[None])
        feed_gain = relative(feed_gain[None])
        if not tiles:
            tokens, out_grad = relative(tokens), relative(out_grad)
        tokens, normed_first = order(lambda deps: enter(spot, tiles, tokens, attention_gain, deps))
        normed_other = swap(normed_first)
        if tiles:
            out_grad = order(lambda deps: to_order(spot, tiles, out_grad, deps))
        grad_other = swap(out_grad)
        segment_row = segments[0]
        cosine, sine = rotary_tables(segment_row)
        first_seen = first_blocks(segment_row)
        spread("o")
        spread("qkv")
        order.wait(cosine, sine, first_seen)
        land("o")
        grad_seq = order(lambda deps: join(here, out_grad, grad_other, deps))
        normed_seq = order(lambda deps: join(spot, normed_first, normed_other, deps))
        land("qkv")
        rotated = order(
            lambda deps: project(
                spot, normed_first, normed_other, full["qkv"], deps, (cosine, sine),
                (query_width + key_width) // 128,
            )
        )
        spread(0)
        mixed, log_totals = order(
            lambda deps: attend(rotated, query_width, first_seen, segment_row, score_scale, deps)
        )
        own, sent = order(lambda deps: back(spot, (mixed,), ((full["o"], 0),), deps, True))
        other = swap(sent)
        spread(1)
        land(0)
        normed_second, middle = order(lambda deps: middle_forward(tokens, own, other, feed_gain, deps))
        normed_third = swap(normed_second)
        spread(2)
        normed_feed = order(lambda deps: join(here, normed_second, normed_third, deps))
        land(1)
        hidden, gate_grad, up_grad = {}, {}, {}
        from_core, to_x, from_x, kept, summed = {}, {}, {}, {}, {}

        def run_feed(i):
            hidden[i], gate_grad[i], up_grad[i] = order(
                lambda deps: feed(spot, normed_feed, grad_seq, full[i], deps)
            )

        def core_part(i):
            grads = (gate_grad[i], up_grad[i], hidden[i])
            part = order(lambda deps: grad((normed_feed, grad_seq), (0, 0, 1), grads, deps))
            from_core[i] = over_core(part)

        def x_part(i):
            grads = (gate_grad[i], up_grad[i], hidden[i])
            to_x[i], kept[i] = order(
                lambda deps: grad((normed_feed, grad_seq), (0, 0, 1), grads, deps, from_core[i])
            )

        def send_x(i):
            from_x[i] = over_x(to_x[i])

        def finish(i, us=4):
            summed[i] = scatter(order(lambda deps: add(kept[i], from_x[i], deps, us)))

        def feed_back(chunks):
            acts = [a[i] for i in chunks for a in (gate_grad, up_grad)]
            weights = [(full[i], at) for i in chunks for at in (0, 1)]
            return order(lambda deps: back(spot, acts, weights, deps))

        run_feed(0)
        core_part(0)
        run_feed(1)
        spread(3)
        x_part(0)
        sent_along, kept_along = scatter(to_x[0]), scatter(kept[0])
        core_part(1)
        land(2)
        run_feed(2)
        x_part(1)
        send_x(1)
        from_along = over_x(order(lambda deps: gate(sent_along, deps)))
        land(3)
        core_part(2)
        run_feed(3)
        own, sent = feed_back(range(CHUNKS))
        other = swap(sent)
        order.wait(kept_along)
        x_part(2)
        send_x(2)
        core_part(3)
        order.wait(from_along)
        finish(1)
        attn_out_grad, middle_grad, feed_gain_part = order(
            lambda deps: middle_backward(own, other, middle, out_grad, feed_gain, deps)
        )
        attn_other = swap(attn_out_grad)
        x_part(3)
        send_x(3)
        block_own, block_sent = order(
            lambda deps: back(
                spot, [hidden[i] for i in range(CHUNKS)], [(full[i], 2) for i in range(CHUNKS)], deps
            )
        )
        block_other = swap(block_sent)
        finish(2)
        attn_grad_seq = order(lambda deps: join(spot, attn_out_grad, attn_other, deps))
        from_core["o"] = over_core(order(lambda deps: grad((attn_grad_seq,), (0,), (mixed,), deps)))
        mixed_grad = order(lambda deps: project(spot, attn_out_grad, attn_other, full["o"], deps))
        to_x["o"], kept["o"] = order(
            lambda deps: grad((attn_grad_seq,), (0,), (mixed,), deps, from_core["o"])
        )
        send_x("o")
        finish(3)
        qkv_grad = order(
            lambda deps: attend_back(
                rotated, mixed_grad, log_totals, query_width, first_seen, segment_row, cosine, sine,
                score_scale, deps,
            )
        )
        from_core["qkv"] = over_core(
            order(lambda deps: grad((normed_seq,), (0,) * 3, qkv_grad, deps, us=SHORT))
        )
        order.wait(summed[3])
        finish("o")
        to_x["qkv"], kept["qkv"] = order(
            lambda deps: grad((normed_seq,), (0,) * 3, qkv_grad, deps, from_core["qkv"])
        )
        send_x("qkv")
        places = (0, query_width // key_width, query_width // key_width + 1)
        own, sent = order(
            lambda deps: back(spot, qkv_grad, [(full["qkv"], at) for at in places], deps, True)
        )
        other = swap(sent)
        summed[0] = order(lambda deps: add(kept_along, from_along, deps, kind=f32))
        block_out = order(lambda deps: block_result(spot, tiles, middle, block_own, block_other, deps))
        order.wait(summed["o"])
        finish("qkv")
        input_grad, attention_gain_part = order(
            lambda deps: input_backward(spot, tiles, own, other, tokens, middle_grad, attention_gain, deps)
        )
        gains = total(natural(jnp.concatenate([attention_gain_part, feed_gain_part], axis=0)))
        if not tiles:
            block_out, input_grad = natural(block_out), natural(input_grad)
        qkv_weight_grad = summed["qkv"].astype(f32)

        def whole(at):
            parts = []
            for i in range(CHUNKS):
                units = edges[i + 1] - edges[i]
                parts.append(summed[i][:, at * units : at * units + units].astype(f32))
            return jnp.concatenate(parts, axis=1)

        return (
            block_out,
            input_grad,
            qkv_weight_grad[:, :query_width],
            qkv_weight_grad[:, query_width : query_width + key_width],
            qkv_weight_grad[:, query_width + key_width :],
            summed["o"].astype(f32),
            gains[0],
            whole(0),
            whole(1),
            whole(2),
            gains[1],
        )

    return shards


def solution(mesh):
    outer = mesh.shape["dp"] // 4
    fine = Mesh(
        mesh.devices.reshape(outer, 2, 2, mesh.shape["tensor"]), ("z", "x", "core", "tensor")
    )
    dp = ("z", "x", "core")
    every = P(dp + ("tensor",), None)
    weight = P(dp, "tensor")
    return jax.shard_map(
        make_shards(outer),
        mesh=fine,
        in_specs=(
            every,
            P(dp, None),
            weight,
            weight,
            weight,
            weight,
            P(),
            weight,
            weight,
            weight,
            P(),
            every,
        ),
        out_specs=(every, every, weight, weight, weight, weight, P(), weight, weight, weight, P()),
        check_vma=False,
    )
```

```python
import functools

import jax
import jax.numpy as jnp
from jax import lax
from jax.experimental import pallas as pl
from jax.experimental.pallas import tpu as pltpu
from jax.sharding import Mesh, PartitionSpec as P

HEAD_DIM = 64
SWAP = ((0, 1), (1, 0))
QUERIES = 256
CHUNKS = 4
BLOCK = 256
ROW_STEPS = 3
COST = 10**10
SHORT = 0.01
VMEM = 48 * 2**20
epsilon = 1e-05
rope_base = 10000.0
bf16 = jnp.bfloat16
f32 = jnp.float32


def dot_plain(left, right):
    return jnp.dot(left, right, preferred_element_type=f32)


def dot_trans(left, right):
    return lax.dot_general(left, right, (((1,), (1,)), ((), ())), preferred_element_type=f32)


def dot_inner(left, right):
    return lax.dot_general(left, right, (((0,), (0,)), ((), ())), preferred_element_type=f32)


def rotary_tables(segment_row):
    length = segment_row.shape[0]
    before = jnp.sum((segment_row[None, :] < segment_row[:, None]).astype(jnp.int32), axis=1)
    places = (jnp.arange(length, dtype=jnp.int32) - before).astype(f32)
    half_dim = HEAD_DIM // 2
    frequency = rope_base ** (-2.0 * jnp.arange(half_dim).astype(f32) / HEAD_DIM)
    angles = places[:, None] * frequency[None, :]
    cosine, sine = jnp.cos(angles), jnp.sin(angles)
    return (jnp.concatenate([cosine] * 4, axis=1), jnp.concatenate([-sine, sine] * 2, axis=1))


def first_blocks(segment_row):
    starts, ends = segment_row[::QUERIES], segment_row[QUERIES - 1 :: QUERIES]
    return jnp.sum((ends[None, :] < starts[:, None]).astype(jnp.int32), axis=1)


def lanes_of(shape):
    return lax.broadcasted_iota(jnp.int32, shape, len(shape) - 1)


def turn(block, cosine, sine):
    low_half = lanes_of(block.shape) % HEAD_DIM < HEAD_DIM // 2
    other = jnp.where(low_half, pltpu.roll(block, 96, 1), pltpu.roll(block, 32, 1))
    return block * cosine + other * sine


def widen(pair_ref, wide_ref, group):
    pair = pair_ref[...]
    keep = (lanes_of(pair.shape) < HEAD_DIM) == (group == 0)
    half = jnp.where(keep, pair, pltpu.roll(pair.astype(f32), HEAD_DIM, 1).astype(bf16))
    wide_ref[:, :128] = half
    wide_ref[:, 128:] = half


def seen_bias(col_ref, row_ref, start, keys, step):
    queries = col_ref.shape[0]
    same = col_ref[...] == row_ref[:, pl.ds(start, keys)]
    q_at = lax.broadcasted_iota(jnp.int32, (queries, keys), 0) + step * queries
    k_at = lax.broadcasted_iota(jnp.int32, (queries, keys), 1) + start
    return jnp.where(same & (q_at >= k_at), 0.0, -1e30).astype(f32)


def forward_kernel(scale, low_ref, q_ref, k_ref, v_ref, col_ref, row_ref, o_ref, lse_ref, kw_ref, vw_ref):
    group, step = pl.program_id(0), pl.program_id(1)
    queries = q_ref.shape[0]

    @pl.when(step == 0)
    def _():
        widen(k_ref, kw_ref, group)
        widen(v_ref, vw_ref, group)

    def run(blocks):
        keys = blocks * queries
        start = pl.multiple_of(low_ref[step] * queries, queries)
        bias = seen_bias(col_ref, row_ref, start, keys, step)
        key = kw_ref[pl.ds(start, keys), :]
        value = vw_ref[pl.ds(start, keys), :]
        head_of = lanes_of((queries, 256)) // HEAD_DIM
        lse = jnp.zeros((queries, 128), f32)
        for quad in range(q_ref.shape[1] // 256):
            wide = q_ref[:, quad * 256 : quad * 256 + 256]
            out = jnp.zeros((queries, 256), f32)
            for j in range(4):
                one = jnp.where(head_of == j, wide, jnp.zeros_like(wide))
                scores = dot_trans(one, key) * scale + bias
                top = jnp.max(scores, axis=1, keepdims=True)
                powers = jnp.exp(scores - top)
                sums = jnp.sum(powers, axis=1, keepdims=True)
                prob = (powers * (1.0 / sums)).astype(bf16)
                out = jnp.where(head_of == j, dot_plain(prob, value), out)
                lse = jnp.where(lanes_of(lse.shape) == quad * 4 + j, top + jnp.log(sums), lse)
            o_ref[:, quad * 256 : quad * 256 + 256] = out.astype(bf16)
        lse_ref[...] = lse

    for blocks in range(1, row_ref.shape[1] // queries + 1):
        pl.when(step + 1 - low_ref[step] == blocks)(functools.partial(run, blocks))


def backward_kernel(
    scale, low_ref, q_ref, k_ref, v_ref, g_ref, lse_ref, col_ref, row_ref, cos_ref, sin_ref, kcos_ref, ksin_ref,
    dq_ref, dk_ref, dv_ref, kw_ref, vw_ref, dkw_ref, dvw_ref,
):
    group, step = pl.program_id(0), pl.program_id(1)
    queries = q_ref.shape[0]

    @pl.when(step == 0)
    def _():
        widen(k_ref, kw_ref, group)
        widen(v_ref, vw_ref, group)
        dkw_ref[...] = jnp.zeros_like(dkw_ref)
        dvw_ref[...] = jnp.zeros_like(dvw_ref)

    def run(blocks):
        keys = blocks * queries
        start = pl.multiple_of(low_ref[step] * queries, queries)
        bias = seen_bias(col_ref, row_ref, start, keys, step)
        key = kw_ref[pl.ds(start, keys), :]
        value = vw_ref[pl.ds(start, keys), :]
        head_of = lanes_of((queries, 256)) // HEAD_DIM
        cosine, sine = cos_ref[...], sin_ref[...]
        for quad in range(q_ref.shape[1] // 256):
            wide = q_ref[:, quad * 256 : quad * 256 + 256]
            grads = g_ref[:, quad * 256 : quad * 256 + 256]
            out = jnp.zeros((queries, 256), f32)
            for j in range(4):
                at = quad * 4 + j
                one = jnp.where(head_of == j, wide, jnp.zeros_like(wide))
                grad = jnp.where(head_of == j, grads, jnp.zeros_like(grads))
                prob = jnp.exp(dot_trans(one, key) * scale + bias - lse_ref[:, at : at + 1])
                prob_grad = dot_trans(grad, value)
                centre = jnp.sum(prob * prob_grad, axis=1, keepdims=True)
                score_grad = (prob * (prob_grad - centre) * scale).astype(bf16)
                dvw_ref[pl.ds(start, keys), :] += dot_inner(prob.astype(bf16), grad)
                dkw_ref[pl.ds(start, keys), :] += dot_inner(score_grad, one)
                out = jnp.where(head_of == j, dot_plain(score_grad, key), out)
            for half in range(2):
                piece = turn(out[:, half * 128 : half * 128 + 128], cosine, -sine)
                dq_ref[:, quad * 256 + half * 128 : quad * 256 + half * 128 + 128] = piece.astype(bf16)

    for blocks in range(1, row_ref.shape[1] // queries + 1):
        pl.when(step + 1 - low_ref[step] == blocks)(functools.partial(run, blocks))

    @pl.when(step == pl.num_programs(1) - 1)
    def _():
        mine = (lanes_of(dk_ref.shape) < HEAD_DIM) == (group == 0)

        def fold(ref):
            pair = ref[:, :128] + ref[:, 128:]
            return pair + pltpu.roll(pair, HEAD_DIM, 1)

        dk = turn(fold(dkw_ref), kcos_ref[...], -ksin_ref[...]).astype(bf16)
        dk_ref[...] = jnp.where(mine, dk, dk_ref[...])
        dv_ref[...] = jnp.where(mine, fold(dvw_ref).astype(bf16), dv_ref[...])


def launch(kernel, scalars, operands, deps, grid, in_specs, out_specs, out_shape, scratch=(), aliases=(), us=3):
    count = len(scalars) + len(operands)

    def body(*refs):
        kernel(*refs[:count], *refs[count + len(deps) :])

    return pl.pallas_call(
        body,
        grid_spec=pltpu.PrefetchScalarGridSpec(
            num_scalar_prefetch=len(scalars),
            grid=grid,
            in_specs=[*in_specs, *([pl.BlockSpec(memory_space=pl.ANY)] * len(deps))],
            out_specs=out_specs,
            scratch_shapes=scratch,
        ),
        out_shape=out_shape,
        compiler_params=pltpu.CompilerParams(vmem_limit_bytes=VMEM),
        cost_estimate=pl.CostEstimate(flops=int(COST * us), bytes_accessed=1024, transcendentals=0),
        input_output_aliases=dict(aliases),
    )(*scalars, *operands, *deps)


def whole_block(array):
    return pl.BlockSpec(array.shape, lambda *at: (0,) * array.ndim)


def weight_columns(weight, column):
    both, across, across_core = weight
    depth = across.shape[0]
    specs = [
        pl.BlockSpec((depth, BLOCK), lambda j, s: (s[1], column(j))),
        pl.BlockSpec((depth, BLOCK), lambda j, s: (0, column(j))),
        pl.BlockSpec((depth, BLOCK), lambda j, s: (1 - s[1], column(j))),
        pl.BlockSpec((depth, BLOCK), lambda j, s: (0, column(j))),
    ]
    return specs, [both, across, both, across_core]


def weight_rows(weight, block, units, at):
    both, across, across_core = weight
    per = across.shape[0] // block

    def spec(quarter):
        def index(j, s):
            row = jnp.clip(j - quarter * per, 0, per - 1)
            if quarter % 2 == 0:
                row = row + per * (s[1] if quarter == 0 else 1 - s[1])
            return row, at

        return pl.BlockSpec((block, units), index)

    return [spec(quarter) for quarter in range(4)], [both, across, both, across_core]


def stack_kernel(*refs):
    first = 0
    for ref in refs[:-1]:
        refs[-1][:, first : first + ref.shape[1]] = ref[...]
        first += ref.shape[1]


def stack(parts, deps):
    shape = (parts[0].shape[0], sum(p.shape[1] for p in parts))
    return launch(
        stack_kernel,
        [],
        parts,
        deps,
        (1,),
        [whole_block(p) for p in parts],
        pl.BlockSpec(shape, lambda j: (0, 0)),
        jax.ShapeDtypeStruct(shape, bf16),
        us=1.5,
    )


def own_kernel(spot_ref, both_ref, out_ref):
    out_ref[...] = both_ref[...]


def own_rows(spot, both, deps):
    rows, width = both.shape
    steps = 4
    block = rows // 2 // steps
    return launch(
        own_kernel,
        [spot],
        [both],
        deps,
        (steps,),
        [pl.BlockSpec((block, width), lambda j, s: (s[1] * steps + j, 0))],
        pl.BlockSpec((block, width), lambda j, s: (j, 0)),
        jax.ShapeDtypeStruct((rows // 2, width), bf16),
        us=4,
    )


def gate_kernel(in_ref, out_ref):
    pass


def gate(array, deps):
    anywhere = pl.BlockSpec(memory_space=pl.ANY)
    return launch(
        gate_kernel,
        [],
        [array],
        deps,
        (1,),
        [anywhere],
        anywhere,
        jax.ShapeDtypeStruct(array.shape, array.dtype),
        aliases=((0, 0),),
        us=1,
    )


def product(act_ref, parts):
    depth = parts[0].shape[0]
    return sum(
        dot_plain(act_ref[:, i * depth : i * depth + depth], part[...]) for i, part in enumerate(parts)
    )


def feed_kernel(spot_ref, x_ref, g_ref, *refs):
    pieces, (h_ref, gg_ref, ug_ref) = refs[:12], refs[12:]
    gate = product(x_ref, pieces[:4])
    up = product(x_ref, pieces[4:8])
    sigmoid = jax.nn.sigmoid(gate)
    silu = gate * sigmoid
    h_ref[...] = (silu * up).astype(bf16)
    grad = product(g_ref, pieces[8:])
    gg_ref[...] = (grad * up * (sigmoid * (1.0 + gate * (1.0 - sigmoid)))).astype(bf16)
    ug_ref[...] = (grad * silu).astype(bf16)


def feed(spot, normed, grads, weight, deps):
    rows, width = normed.shape
    units = weight[0].shape[1] // 3
    blocks = units // BLOCK
    specs, operands = [whole_block(normed), whole_block(grads)], [normed, grads]
    for at in range(3):
        more = weight_columns(weight, lambda j, at=at: j + at * blocks)
        specs += more[0]
        operands += more[1]
    return launch(
        feed_kernel,
        [spot],
        operands,
        deps,
        (blocks,),
        specs,
        [pl.BlockSpec((rows, BLOCK), lambda j, s: (0, j))] * 3,
        [jax.ShapeDtypeStruct((rows, units), bf16)] * 3,
        us=rows * width * units / 10**8,
    )


def project_kernel(rotated, spot_ref, own_ref, other_ref, *refs):
    parts, out_ref = refs[:4], refs[-1]
    rows = own_ref.shape[0]
    for act_ref, place in ((own_ref, spot_ref[0]), (other_ref, 1 - spot_ref[0])):
        at = pl.ds(pl.multiple_of(place * rows, rows), rows)
        total = product(act_ref, parts)
        if rotated is None:
            out_ref[at, :] = total.astype(bf16)
        else:
            cosine, sine = refs[4][at, :], refs[5][at, :]
            for half in range(2):
                piece = total[:, half * 128 : half * 128 + 128]
                keep = 2 * pl.program_id(0) + half >= rotated
                piece = jnp.where(keep, piece, turn(piece, cosine, sine))
                out_ref[at, half * 128 : half * 128 + 128] = piece.astype(bf16)


def project(spot, own, other, weight, deps, tables=(), rotated=None):
    rows, width = own.shape
    units = weight[0].shape[1]
    specs, operands = weight_columns(weight, lambda j: j)
    return launch(
        functools.partial(project_kernel, rotated),
        [spot],
        [own, other, *operands, *tables],
        deps,
        (units // BLOCK,),
        [whole_block(own), whole_block(other), *specs, *(whole_block(t) for t in tables)],
        pl.BlockSpec((2 * rows, BLOCK), lambda j, s: (0, j)),
        jax.ShapeDtypeStruct((2 * rows, units), bf16),
        us=rows * width * units / 10**8,
    )


def back_kernel(count, started, placed, spot_ref, *refs):
    step = pl.program_id(0)
    acts = refs[:count]
    weights = refs[count : 5 * count]
    starts = refs[5 * count : 5 * count + 2] if started else None
    mine_ref, theirs_ref = refs[-2:]
    rows = mine_ref.shape[0]

    def run(part):
        total = sum(dot_trans(a[...], weights[4 * i + part][...]) for i, a in enumerate(acts))
        mine, theirs = total[:rows], total[rows:]
        if placed:
            first = spot_ref[0] == 0
            mine, theirs = jnp.where(first, mine, theirs), jnp.where(first, theirs, mine)
        if started:
            mine = mine + starts[0][...].astype(f32)
            theirs = theirs + starts[1][...].astype(f32)
        mine_ref[...] = mine.astype(mine_ref.dtype)
        theirs_ref[...] = theirs.astype(theirs_ref.dtype)

    for part in range(4):
        pl.when(step // (pl.num_programs(0) // 4) == part)(functools.partial(run, part))


def back(spot, acts, weights, deps, placed=False, starts=(), kinds=(f32, bf16)):
    rows = acts[0].shape[0]
    depth = weights[0][0][1].shape[0]
    width = 4 * depth
    block = min(BLOCK, depth)
    half = pl.BlockSpec((rows // 2, block), lambda j, s: (0, j))
    specs, operands = [whole_block(a) for a in acts], list(acts)
    for act, (weight, at) in zip(acts, weights):
        more = weight_rows(weight, block, act.shape[1], at)
        specs += more[0]
        operands += more[1]
    return launch(
        functools.partial(back_kernel, len(acts), len(starts) > 0, placed),
        [spot],
        [*operands, *starts],
        deps,
        (width // block,),
        [*specs, *([half] * len(starts))],
        [half, half],
        [jax.ShapeDtypeStruct((rows // 2, width), kind) for kind in kinds],
        us=rows * width * sum(a.shape[1] for a in acts) / 285000000,
    )


def grad_kernel(which, added, *refs):
    step, steps = pl.program_id(0), pl.num_programs(0)
    acts = refs[: max(which) + 1]
    count = len(which)
    grads = refs[len(acts) : len(acts) + count]
    first = 0
    for i in range(count):
        at = slice(first, first + grads[i].shape[1])
        first = at.stop
        total = dot_inner(acts[which[i]][...], grads[i][...])
        if not added:
            refs[-1][:, at] = total.astype(bf16)
            continue
        total = (total + refs[-3][:, at].astype(f32)).astype(bf16)

        @pl.when(step < steps // 2)
        def _():
            refs[-2][:, at] = total

        @pl.when(step >= steps // 2)
        def _():
            refs[-1][:, at] = total


def grad(acts, which, grads, deps, added=None, us=None):
    tokens, width = acts[0].shape
    block = min(BLOCK, width // 4)
    steps = width // 2 // block
    half = steps // 2
    units = sum(g.shape[1] for g in grads)
    if added is None:
        row = lambda j: j + steps
        outs = pl.BlockSpec((block, units), lambda j: (j, 0))
        shapes = jax.ShapeDtypeStruct((width // 2, units), bf16)
    else:
        row = lambda j: (j + half) % steps
        outs = [
            pl.BlockSpec((block, units), lambda j: (jnp.minimum(j, half - 1), 0)),
            pl.BlockSpec((block, units), lambda j: (jnp.maximum(j - half, 0), 0)),
        ]
        shapes = [jax.ShapeDtypeStruct((width // 4, units), bf16)] * 2
    specs = [pl.BlockSpec((tokens, block), lambda j: (0, row(j))) for _ in acts]
    specs += [whole_block(g) for g in grads]
    operands = [*acts, *grads]
    if added is not None:
        specs.append(pl.BlockSpec((block, units), lambda j: (row(j), 0)))
        operands.append(added)
    return launch(
        functools.partial(grad_kernel, which, added is not None),
        [],
        operands,
        deps,
        (steps,),
        specs,
        outs,
        shapes,
        us=us or tokens * width * units / 480000000,
    )


def attention_specs(length, queries, wide):
    pair = lambda first: pl.BlockSpec((length, 128), lambda g, i, low: (0, first))
    col = pl.BlockSpec((queries, 1), lambda g, i, low: (i, 0))
    row = pl.BlockSpec((1, length), lambda g, i, low: (0, 0))
    return pl.BlockSpec((queries, wide), lambda g, i, low: (i, g)), pair, col, row


def attend(rotated, query_width, first_seen, segment_row, scale, deps):
    length = rotated.shape[0]
    queries = length // first_seen.shape[0]
    groups = 2
    heads, pair, col, row = attention_specs(length, queries, query_width // groups)
    first = query_width // 128
    return launch(
        functools.partial(forward_kernel, scale),
        [first_seen],
        [rotated, rotated, rotated, segment_row.reshape(length, 1), segment_row.reshape(1, length)],
        deps,
        (groups, length // queries),
        [heads, pair(first), pair(first + 1), col, row],
        [heads, pl.BlockSpec((queries, 128), lambda g, i, low: (i, g))],
        [
            jax.ShapeDtypeStruct((length, query_width), bf16),
            jax.ShapeDtypeStruct((length, groups * 128), f32),
        ],
        [pltpu.VMEM((length, 256), bf16)] * 2,
        us=16,
    )


def attend_back(rotated, grads, lse, query_width, first_seen, segment_row, cosine, sine, scale, deps):
    length = rotated.shape[0]
    queries = length // first_seen.shape[0]
    groups = 2
    heads, pair, col, row = attention_specs(length, queries, query_width // groups)
    first = query_width // 128
    table = pl.BlockSpec((queries, 128), lambda g, i, low: (i, 0))
    return launch(
        functools.partial(backward_kernel, scale),
        [first_seen],
        [
            rotated, rotated, rotated, grads, lse, segment_row.reshape(length, 1),
            segment_row.reshape(1, length), cosine, sine, cosine, sine,
        ],
        deps,
        (groups, length // queries),
        [
            heads, pair(first), pair(first + 1), heads,
            pl.BlockSpec((queries, 128), lambda g, i, low: (i, g)), col, row, table, table, pair(0), pair(0),
        ],
        [heads, pair(0), pair(0)],
        [
            jax.ShapeDtypeStruct((length, query_width), bf16),
            jax.ShapeDtypeStruct((length, 128), bf16),
            jax.ShapeDtypeStruct((length, 128), bf16),
        ],
        [pltpu.VMEM((length, 256), bf16)] * 2 + [pltpu.VMEM((length, 256), f32)] * 2,
        us=35,
    )


def join_kernel(spot_ref, own_ref, other_ref, out_ref):
    rows = own_ref.shape[0]
    for ref, place in ((own_ref, spot_ref[0]), (other_ref, 1 - spot_ref[0])):
        out_ref[pl.ds(pl.multiple_of(place * rows, rows), rows), :] = ref[...]


def join(spot, own, other, deps):
    rows, width = own.shape
    block = width // 4
    half = pl.BlockSpec((rows, block), lambda j, s: (0, j))
    return launch(
        join_kernel,
        [spot],
        [own, other],
        deps,
        (4,),
        [half, half],
        pl.BlockSpec((2 * rows, block), lambda j, s: (0, j)),
        jax.ShapeDtypeStruct((2 * rows, width), bf16),
        us=4,
    )


def add_kernel(a_ref, b_ref, out_ref):
    out_ref[...] = (a_ref[...].astype(f32) + b_ref[...].astype(f32)).astype(out_ref.dtype)


def add(a, b, deps, us=4, kind=bf16):
    rows, width = a.shape
    block = pl.BlockSpec((rows // 4, width), lambda j: (j, 0))
    return launch(
        add_kernel, [], [a, b], deps, (4,), [block, block], block, jax.ShapeDtypeStruct(a.shape, kind), us=us
    )


def natural_block(spot_ref, outer, core, x, z):
    x = 1 - spot_ref[2] if x else spot_ref[2]
    core = 1 - spot_ref[1] if core else spot_ref[1]
    return (z * 2 + x) * 2 + core


def reorder(spot_ref, outer, width):
    size = width // (4 * outer)
    for core in range(2):
        for x in range(2):
            for z in range(outer):
                at = ((core * 2 + x) * outer + z) * size
                there = natural_block(spot_ref, outer, core, x, z) * size
                yield slice(at, at + size), pl.ds(pl.multiple_of(there, size), size)


def inverse_rms(activity):
    return lax.rsqrt(jnp.mean(activity * activity, axis=-1, keepdims=True) + epsilon)


def norm_back(activity, inverse, gain_vec, incoming):
    scaled = incoming * gain_vec
    return inverse * scaled - activity * (inverse * inverse * inverse) * jnp.mean(
        scaled * activity, axis=-1, keepdims=True
    )


def enter_kernel(outer, spot_ref, tokens_ref, gain_ref, out_ref, normed_ref):
    if outer:
        for here, there in reorder(spot_ref, outer, tokens_ref.shape[1]):
            out_ref[:, here] = tokens_ref[:, there]
    else:
        out_ref[...] = tokens_ref[...]
    inputs = out_ref[...].astype(f32)
    normed_ref[...] = (inputs * inverse_rms(inputs) * gain_ref[...]).astype(bf16)


def turn_kernel(outer, spot_ref, array_ref, out_ref):
    for here, there in reorder(spot_ref, outer, array_ref.shape[1]):
        out_ref[:, here] = array_ref[:, there]


def rows_spec(rows, width):
    return pl.BlockSpec((rows // ROW_STEPS, width), lambda j, *s: (j, 0))


def enter(spot, outer, tokens, gain, deps):
    spec = rows_spec(*tokens.shape)
    return launch(
        functools.partial(enter_kernel, outer),
        [spot],
        [tokens, gain],
        deps,
        (ROW_STEPS,),
        [spec, whole_block(gain)],
        [spec, spec],
        [jax.ShapeDtypeStruct(tokens.shape, bf16)] * 2,
        us=3,
    )


def to_order(spot, outer, array, deps):
    spec = rows_spec(*array.shape)
    return launch(
        functools.partial(turn_kernel, outer),
        [spot],
        [array],
        deps,
        (ROW_STEPS,),
        [spec],
        spec,
        jax.ShapeDtypeStruct(array.shape, bf16),
        us=3,
    )


def middle_kernel(tokens_ref, own_ref, other_ref, gain_ref, normed_ref, middle_ref):
    middle = tokens_ref[...].astype(f32) + own_ref[...] + other_ref[...].astype(f32)
    middle_ref[...] = middle
    normed_ref[...] = (middle * inverse_rms(middle) * gain_ref[...]).astype(bf16)


def middle_forward(tokens, own, other, gain, deps):
    spec = rows_spec(*tokens.shape)
    return launch(
        middle_kernel,
        [],
        [tokens, own, other, gain],
        deps,
        (ROW_STEPS,),
        [spec, spec, spec, whole_block(gain)],
        [spec, spec],
        [jax.ShapeDtypeStruct(tokens.shape, bf16), jax.ShapeDtypeStruct(tokens.shape, f32)],
        us=5,
    )


def gain_part(part_ref, product):
    @pl.when(pl.program_id(0) == 0)
    def _():
        part_ref[...] = jnp.zeros_like(part_ref)

    part_ref[...] += jnp.sum(product, axis=0, keepdims=True)


def middle_back_kernel(own_ref, other_ref, middle_ref, grad_ref, gain_ref, low_ref, out_ref, part_ref):
    incoming = own_ref[...] + other_ref[...].astype(f32)
    middle = middle_ref[...]
    inverse = inverse_rms(middle)
    out = grad_ref[...].astype(f32) + norm_back(middle, inverse, gain_ref[...], incoming)
    out_ref[...] = out
    low_ref[...] = out.astype(bf16)
    gain_part(part_ref, incoming * middle * inverse)


def middle_backward(own, other, middle, out_grad, gain, deps):
    spec = rows_spec(*own.shape)
    part = jax.ShapeDtypeStruct(gain.shape, f32)
    return launch(
        middle_back_kernel,
        [],
        [own, other, middle, out_grad, gain],
        deps,
        (ROW_STEPS,),
        [spec, spec, spec, spec, whole_block(gain)],
        [spec, spec, whole_block(gain)],
        [jax.ShapeDtypeStruct(own.shape, bf16), jax.ShapeDtypeStruct(own.shape, f32), part],
        us=8,
    )


def leave(outer, spot_ref, out_ref, value):
    value = value.astype(bf16)
    if outer:
        for here, there in reorder(spot_ref, outer, value.shape[1]):
            out_ref[:, there] = value[:, here]
    else:
        out_ref[...] = value


def block_out_kernel(outer, spot_ref, middle_ref, own_ref, other_ref, out_ref):
    leave(outer, spot_ref, out_ref, middle_ref[...] + own_ref[...] + other_ref[...].astype(f32))


def block_result(spot, outer, middle, own, other, deps):
    spec = rows_spec(*own.shape)
    return launch(
        functools.partial(block_out_kernel, outer),
        [spot],
        [middle, own, other],
        deps,
        (ROW_STEPS,),
        [spec, spec, spec],
        spec,
        jax.ShapeDtypeStruct(own.shape, bf16),
        us=5,
    )


def input_back_kernel(outer, spot_ref, own_ref, other_ref, tokens_ref, grad_ref, gain_ref, out_ref, part_ref):
    incoming = own_ref[...] + other_ref[...].astype(f32)
    inputs = tokens_ref[...].astype(f32)
    inverse = inverse_rms(inputs)
    leave(outer, spot_ref, out_ref, grad_ref[...] + norm_back(inputs, inverse, gain_ref[...], incoming))
    gain_part(part_ref, incoming * inputs * inverse)


def input_backward(spot, outer, own, other, tokens, middle_grad, gain, deps):
    spec = rows_spec(*own.shape)
    return launch(
        functools.partial(input_back_kernel, outer),
        [spot],
        [own, other, tokens, middle_grad, gain],
        deps,
        (ROW_STEPS,),
        [spec, spec, spec, spec, whole_block(gain)],
        [spec, whole_block(gain)],
        [jax.ShapeDtypeStruct(own.shape, bf16), jax.ShapeDtypeStruct(gain.shape, f32)],
        us=7,
    )


class Order:
    def __init__(self):
        self.before = []

    def wait(self, *arrays):
        self.before += arrays

    def __call__(self, compute, *operands, **options):
        result = compute(*operands, deps=self.before, **options)
        self.before = [result[0] if isinstance(result, (tuple, list)) else result]
        return result


def chunk_edges(width):
    blocks = width // BLOCK
    return [BLOCK * (-(-blocks * i // CHUNKS)) for i in range(CHUNKS + 1)]


def make_shards(outer):
    def relative(array):
        rows, width = array.shape
        blocks = array.reshape(rows, outer, 2, 2, width // (4 * outer))
        blocks = jnp.where(lax.axis_index("x") == 0, blocks, blocks[:, :, ::-1])
        blocks = jnp.where(lax.axis_index("core") == 0, blocks, blocks[:, :, :, ::-1])
        return blocks.transpose(0, 3, 2, 1, 4).reshape(rows, width)

    def natural(array):
        rows, width = array.shape
        blocks = array.reshape(rows, 2, 2, outer, width // (4 * outer)).transpose(0, 3, 2, 1, 4)
        blocks = jnp.where(lax.axis_index("x") == 0, blocks, blocks[:, :, ::-1])
        blocks = jnp.where(lax.axis_index("core") == 0, blocks, blocks[:, :, :, ::-1])
        return blocks.reshape(rows, width)

    def over_x(array):
        return lax.ppermute(array, "x", SWAP)

    def over_core(array):
        return lax.ppermute(array, "core", SWAP)

    def gather(operand):
        return lax.all_gather(operand, ("core", "z"), axis=0, tiled=True)

    def scatter(operand):
        return lax.psum_scatter(operand, "z", scatter_dimension=0, tiled=True)

    def total(vector):
        for axis in ("core", "x", "tensor"):
            vector = vector + lax.ppermute(vector, axis, SWAP)
        step = 1
        while step < outer:
            vector = vector + lax.ppermute(vector, "z", [(i, i ^ step) for i in range(outer)])
            step *= 2
        return vector

    def swap(own):
        return lax.ppermute(own, "tensor", SWAP)

    def shards(
        tokens,
        segments,
        q_weight,
        k_weight,
        v_weight,
        o_weight,
        attention_gain,
        gate_weight,
        up_weight,
        down_weight,
        feed_gain,
        out_grad,
    ):
        query_width = q_weight.shape[1]
        key_width = k_weight.shape[1]
        score_scale = HEAD_DIM ** (-0.5)
        place, core, cross = (lax.axis_index(axis) for axis in ("tensor", "core", "x"))
        spot = jnp.stack([place, core, cross]).astype(jnp.int32)
        here = jnp.zeros_like(spot)
        edges = chunk_edges(gate_weight.shape[1])
        order = Order()
        along, full = {}, {}

        def spread(name):
            full[name] = over_x(order(lambda deps: own_rows(spot, along[name], deps)))

        def land(name):
            across = order(lambda deps: gate(full[name], deps))
            full[name] = (along[name], across, over_core(across))

        def chunk(i):
            columns = slice(edges[i], edges[i + 1])
            parts = [w[:, columns] for w in (gate_weight, up_weight, down_weight)]
            along[i] = gather(order(lambda deps: stack(parts, deps)))

        tiles = outer if tokens.shape[1] // (4 * outer) % 128 == 0 else 0
        along["qkv"] = gather(order(lambda deps: stack([q_weight, k_weight, v_weight], deps)))
        along["o"] = gather(order(lambda deps: stack([o_weight], deps)))
        for i in range(CHUNKS):
            chunk(i)
        attention_gain = relative(attention_gain[None])
        feed_gain = relative(feed_gain[None])
        if not tiles:
            tokens, out_grad = relative(tokens), relative(out_grad)
        tokens, normed_first = order(lambda deps: enter(spot, tiles, tokens, attention_gain, deps))
        normed_other = swap(normed_first)
        segment_row = segments[0]
        cosine, sine = rotary_tables(segment_row)
        first_seen = first_blocks(segment_row)
        spread("qkv")
        if tiles:
            out_grad = order(lambda deps: to_order(spot, tiles, out_grad, deps))
        grad_other = swap(out_grad)
        order.wait(cosine, sine, first_seen)
        normed_seq = order(lambda deps: join(spot, normed_first, normed_other, deps))
        land("qkv")
        spread("o")
        rotated = order(
            lambda deps: project(
                spot, normed_first, normed_other, full["qkv"], deps, (cosine, sine),
                (query_width + key_width) // 128,
            )
        )
        mixed, log_totals = order(
            lambda deps: attend(rotated, query_width, first_seen, segment_row, score_scale, deps)
        )
        land("o")
        grad_seq = order(lambda deps: join(here, out_grad, grad_other, deps))
        own, sent = order(lambda deps: back(spot, (mixed,), ((full["o"], 0),), deps, True))
        other = swap(sent)
        spread(0)
        normed_second, middle = order(lambda deps: middle_forward(tokens, own, other, feed_gain, deps))
        normed_third = swap(normed_second)
        spread(1)
        land(0)
        normed_feed = order(lambda deps: join(here, normed_second, normed_third, deps))
        hidden, gate_grad, up_grad = {}, {}, {}
        from_core, to_x, from_x, kept, summed = {}, {}, {}, {}, {}

        def run_feed(i):
            hidden[i], gate_grad[i], up_grad[i] = order(
                lambda deps: feed(spot, normed_feed, grad_seq, full[i], deps)
            )

        def core_part(i):
            grads = (gate_grad[i], up_grad[i], hidden[i])
            part = order(lambda deps: grad((normed_feed, grad_seq), (0, 0, 1), grads, deps))
            from_core[i] = over_core(part)

        def x_part(i):
            grads = (gate_grad[i], up_grad[i], hidden[i])
            to_x[i], kept[i] = order(
                lambda deps: grad((normed_feed, grad_seq), (0, 0, 1), grads, deps, from_core[i])
            )

        def send_x(i):
            from_x[i] = over_x(to_x[i])

        def finish(i, us=4):
            summed[i] = scatter(order(lambda deps: add(kept[i], from_x[i], deps, us)))

        def feed_back(chunks):
            acts = [a[i] for i in chunks for a in (gate_grad, up_grad)]
            weights = [(full[i], at) for i in chunks for at in (0, 1)]
            return order(lambda deps: back(spot, acts, weights, deps))

        run_feed(0)
        core_part(0)
        spread(2)
        land(1)
        run_feed(1)
        core_part(1)
        spread(3)
        x_part(0)
        sent_along, kept_along = scatter(to_x[0]), scatter(kept[0])
        land(2)
        run_feed(2)
        x_part(1)
        send_x(1)
        core_part(2)
        land(3)
        run_feed(3)
        from_along = over_x(order(lambda deps: gate(sent_along, deps)))
        own, sent = feed_back(range(CHUNKS))
        other = swap(sent)
        x_part(2)
        send_x(2)
        core_part(3)
        order.wait(from_along, kept_along)
        finish(1)
        attn_out_grad, middle_grad, feed_gain_part = order(
            lambda deps: middle_backward(own, other, middle, out_grad, feed_gain, deps)
        )
        attn_other = swap(attn_out_grad)
        x_part(3)
        send_x(3)
        block_own, block_sent = order(
            lambda deps: back(
                spot, [hidden[i] for i in range(CHUNKS)], [(full[i], 2) for i in range(CHUNKS)], deps
            )
        )
        block_other = swap(block_sent)
        finish(2)
        attn_grad_seq = order(lambda deps: join(spot, attn_out_grad, attn_other, deps))
        from_core["o"] = over_core(order(lambda deps: grad((attn_grad_seq,), (0,), (mixed,), deps)))
        mixed_grad = order(lambda deps: project(spot, attn_out_grad, attn_other, full["o"], deps))
        to_x["o"], kept["o"] = order(
            lambda deps: grad((attn_grad_seq,), (0,), (mixed,), deps, from_core["o"])
        )
        send_x("o")
        finish(3)
        qkv_grad = order(
            lambda deps: attend_back(
                rotated, mixed_grad, log_totals, query_width, first_seen, segment_row, cosine, sine,
                score_scale, deps,
            )
        )
        from_core["qkv"] = over_core(
            order(lambda deps: grad((normed_seq,), (0,) * 3, qkv_grad, deps, us=SHORT))
        )
        order.wait(summed[3])
        finish("o")
        to_x["qkv"], kept["qkv"] = order(
            lambda deps: grad((normed_seq,), (0,) * 3, qkv_grad, deps, from_core["qkv"])
        )
        send_x("qkv")
        places = (0, query_width // key_width, query_width // key_width + 1)
        own, sent = order(
            lambda deps: back(spot, qkv_grad, [(full["qkv"], at) for at in places], deps, True)
        )
        other = swap(sent)
        summed[0] = order(lambda deps: add(kept_along, from_along, deps, kind=f32))
        block_out = order(lambda deps: block_result(spot, tiles, middle, block_own, block_other, deps))
        order.wait(summed["o"])
        finish("qkv")
        input_grad, attention_gain_part = order(
            lambda deps: input_backward(spot, tiles, own, other, tokens, middle_grad, attention_gain, deps)
        )
        gains = total(natural(jnp.concatenate([attention_gain_part, feed_gain_part], axis=0)))
        if not tiles:
            block_out, input_grad = natural(block_out), natural(input_grad)
        qkv_weight_grad = summed["qkv"].astype(f32)

        def whole(at):
            parts = []
            for i in range(CHUNKS):
                units = edges[i + 1] - edges[i]
                parts.append(summed[i][:, at * units : at * units + units].astype(f32))
            return jnp.concatenate(parts, axis=1)

        return (
            block_out,
            input_grad,
            qkv_weight_grad[:, :query_width],
            qkv_weight_grad[:, query_width : query_width + key_width],
            qkv_weight_grad[:, query_width + key_width :],
            summed["o"].astype(f32),
            gains[0],
            whole(0),
            whole(1),
            whole(2),
            gains[1],
        )

    return shards


def solution(mesh):
    outer = mesh.shape["dp"] // 4
    fine = Mesh(
        mesh.devices.reshape(outer, 2, 2, mesh.shape["tensor"]), ("z", "x", "core", "tensor")
    )
    dp = ("z", "x", "core")
    every = P(dp + ("tensor",), None)
    weight = P(dp, "tensor")
    return jax.shard_map(
        make_shards(outer),
        mesh=fine,
        in_specs=(
            every,
            P(dp, None),
            weight,
            weight,
            weight,
            weight,
            P(),
            weight,
            weight,
            weight,
            P(),
            every,
        ),
        out_specs=(every, every, weight, weight, weight, weight, P(), weight, weight, weight, P()),
        check_vma=False,
    )
```

```python
import functools

import jax
import jax.numpy as jnp
from jax import lax
from jax.experimental import pallas as pl
from jax.experimental.pallas import tpu as pltpu
from jax.sharding import Mesh, PartitionSpec as P

HEAD_DIM = 64
SWAP = ((0, 1), (1, 0))
QUERIES = 256
CHUNKS = 4
BLOCK = 256
ROW_STEPS = 3
COST = 10**10
SHORT = 0.01
VMEM = 48 * 2**20
epsilon = 1e-05
rope_base = 10000.0
bf16 = jnp.bfloat16
f32 = jnp.float32


def dot_plain(left, right):
    return jnp.dot(left, right, preferred_element_type=f32)


def dot_trans(left, right):
    return lax.dot_general(left, right, (((1,), (1,)), ((), ())), preferred_element_type=f32)


def dot_inner(left, right):
    return lax.dot_general(left, right, (((0,), (0,)), ((), ())), preferred_element_type=f32)


def rotary_tables(segment_row):
    length = segment_row.shape[0]
    before = jnp.sum((segment_row[None, :] < segment_row[:, None]).astype(jnp.int32), axis=1)
    places = (jnp.arange(length, dtype=jnp.int32) - before).astype(f32)
    half_dim = HEAD_DIM // 2
    frequency = rope_base ** (-2.0 * jnp.arange(half_dim).astype(f32) / HEAD_DIM)
    angles = places[:, None] * frequency[None, :]
    cosine, sine = jnp.cos(angles), jnp.sin(angles)
    return (jnp.concatenate([cosine] * 4, axis=1), jnp.concatenate([-sine, sine] * 2, axis=1))


def first_blocks(segment_row):
    starts, ends = segment_row[::QUERIES], segment_row[QUERIES - 1 :: QUERIES]
    return jnp.sum((ends[None, :] < starts[:, None]).astype(jnp.int32), axis=1)


def lanes_of(shape):
    return lax.broadcasted_iota(jnp.int32, shape, len(shape) - 1)


def turn(block, cosine, sine):
    low_half = lanes_of(block.shape) % HEAD_DIM < HEAD_DIM // 2
    other = jnp.where(low_half, pltpu.roll(block, 96, 1), pltpu.roll(block, 32, 1))
    return block * cosine + other * sine


def widen(pair_ref, wide_ref, group):
    pair = pair_ref[...]
    keep = (lanes_of(pair.shape) < HEAD_DIM) == (group == 0)
    half = jnp.where(keep, pair, pltpu.roll(pair.astype(f32), HEAD_DIM, 1).astype(bf16))
    wide_ref[:, :128] = half
    wide_ref[:, 128:] = half


def seen_bias(col_ref, row_ref, start, keys, step):
    queries = col_ref.shape[0]
    same = col_ref[...] == row_ref[:, pl.ds(start, keys)]
    q_at = lax.broadcasted_iota(jnp.int32, (queries, keys), 0) + step * queries
    k_at = lax.broadcasted_iota(jnp.int32, (queries, keys), 1) + start
    return jnp.where(same & (q_at >= k_at), 0.0, -1e30).astype(f32)


def forward_kernel(scale, low_ref, q_ref, k_ref, v_ref, col_ref, row_ref, o_ref, lse_ref, kw_ref, vw_ref):
    group, step = pl.program_id(0), pl.program_id(1)
    queries = q_ref.shape[0]

    @pl.when(step == 0)
    def _():
        widen(k_ref, kw_ref, group)
        widen(v_ref, vw_ref, group)

    def run(blocks):
        keys = blocks * queries
        start = pl.multiple_of(low_ref[step] * queries, queries)
        bias = seen_bias(col_ref, row_ref, start, keys, step)
        key = kw_ref[pl.ds(start, keys), :]
        value = vw_ref[pl.ds(start, keys), :]
        head_of = lanes_of((queries, 256)) // HEAD_DIM
        lse = jnp.zeros((queries, 128), f32)
        for quad in range(q_ref.shape[1] // 256):
            wide = q_ref[:, quad * 256 : quad * 256 + 256]
            out = jnp.zeros((queries, 256), f32)
            for j in range(4):
                one = jnp.where(head_of == j, wide, jnp.zeros_like(wide))
                scores = dot_trans(one, key) * scale + bias
                top = jnp.max(scores, axis=1, keepdims=True)
                powers = jnp.exp(scores - top)
                sums = jnp.sum(powers, axis=1, keepdims=True)
                prob = (powers * (1.0 / sums)).astype(bf16)
                out = jnp.where(head_of == j, dot_plain(prob, value), out)
                lse = jnp.where(lanes_of(lse.shape) == quad * 4 + j, top + jnp.log(sums), lse)
            o_ref[:, quad * 256 : quad * 256 + 256] = out.astype(bf16)
        lse_ref[...] = lse

    for blocks in range(1, row_ref.shape[1] // queries + 1):
        pl.when(step + 1 - low_ref[step] == blocks)(functools.partial(run, blocks))


def backward_kernel(
    scale, low_ref, q_ref, k_ref, v_ref, g_ref, lse_ref, col_ref, row_ref, cos_ref, sin_ref, kcos_ref, ksin_ref,
    dq_ref, dk_ref, dv_ref, kw_ref, vw_ref, dkw_ref, dvw_ref,
):
    group, step = pl.program_id(0), pl.program_id(1)
    queries = q_ref.shape[0]

    @pl.when(step == 0)
    def _():
        widen(k_ref, kw_ref, group)
        widen(v_ref, vw_ref, group)
        dkw_ref[...] = jnp.zeros_like(dkw_ref)
        dvw_ref[...] = jnp.zeros_like(dvw_ref)

    def run(blocks):
        keys = blocks * queries
        start = pl.multiple_of(low_ref[step] * queries, queries)
        bias = seen_bias(col_ref, row_ref, start, keys, step)
        key = kw_ref[pl.ds(start, keys), :]
        value = vw_ref[pl.ds(start, keys), :]
        head_of = lanes_of((queries, 256)) // HEAD_DIM
        cosine, sine = cos_ref[...], sin_ref[...]
        for quad in range(q_ref.shape[1] // 256):
            wide = q_ref[:, quad * 256 : quad * 256 + 256]
            grads = g_ref[:, quad * 256 : quad * 256 + 256]
            out = jnp.zeros((queries, 256), f32)
            for j in range(4):
                at = quad * 4 + j
                one = jnp.where(head_of == j, wide, jnp.zeros_like(wide))
                grad = jnp.where(head_of == j, grads, jnp.zeros_like(grads))
                prob = jnp.exp(dot_trans(one, key) * scale + bias - lse_ref[:, at : at + 1])
                prob_grad = dot_trans(grad, value)
                centre = jnp.sum(prob * prob_grad, axis=1, keepdims=True)
                score_grad = (prob * (prob_grad - centre) * scale).astype(bf16)
                dvw_ref[pl.ds(start, keys), :] += dot_inner(prob.astype(bf16), grad)
                dkw_ref[pl.ds(start, keys), :] += dot_inner(score_grad, one)
                out = jnp.where(head_of == j, dot_plain(score_grad, key), out)
            for half in range(2):
                piece = turn(out[:, half * 128 : half * 128 + 128], cosine, -sine)
                dq_ref[:, quad * 256 + half * 128 : quad * 256 + half * 128 + 128] = piece.astype(bf16)

    for blocks in range(1, row_ref.shape[1] // queries + 1):
        pl.when(step + 1 - low_ref[step] == blocks)(functools.partial(run, blocks))

    @pl.when(step == pl.num_programs(1) - 1)
    def _():
        mine = (lanes_of(dk_ref.shape) < HEAD_DIM) == (group == 0)

        def fold(ref):
            pair = ref[:, :128] + ref[:, 128:]
            return pair + pltpu.roll(pair, HEAD_DIM, 1)

        dk = turn(fold(dkw_ref), kcos_ref[...], -ksin_ref[...]).astype(bf16)
        dk_ref[...] = jnp.where(mine, dk, dk_ref[...])
        dv_ref[...] = jnp.where(mine, fold(dvw_ref).astype(bf16), dv_ref[...])


def launch(kernel, scalars, operands, deps, grid, in_specs, out_specs, out_shape, scratch=(), aliases=(), us=3):
    count = len(scalars) + len(operands)

    def body(*refs):
        kernel(*refs[:count], *refs[count + len(deps) :])

    return pl.pallas_call(
        body,
        grid_spec=pltpu.PrefetchScalarGridSpec(
            num_scalar_prefetch=len(scalars),
            grid=grid,
            in_specs=[*in_specs, *([pl.BlockSpec(memory_space=pl.ANY)] * len(deps))],
            out_specs=out_specs,
            scratch_shapes=scratch,
        ),
        out_shape=out_shape,
        compiler_params=pltpu.CompilerParams(vmem_limit_bytes=VMEM),
        cost_estimate=pl.CostEstimate(flops=int(COST * us), bytes_accessed=1024, transcendentals=0),
        input_output_aliases=dict(aliases),
    )(*scalars, *operands, *deps)


def whole_block(array):
    return pl.BlockSpec(array.shape, lambda *at: (0,) * array.ndim)


def weight_columns(weight, column):
    both, across, across_core = weight
    depth = across.shape[0]
    specs = [
        pl.BlockSpec((depth, BLOCK), lambda j, s: (s[1], column(j))),
        pl.BlockSpec((depth, BLOCK), lambda j, s: (0, column(j))),
        pl.BlockSpec((depth, BLOCK), lambda j, s: (1 - s[1], column(j))),
        pl.BlockSpec((depth, BLOCK), lambda j, s: (0, column(j))),
    ]
    return specs, [both, across, both, across_core]


def weight_rows(weight, block, units, at, quarters):
    both, across, across_core = weight
    per = across.shape[0] // block

    def spec(quarter):
        def index(j, s):
            row = jnp.clip(j - (quarter - quarters[0]) * per, 0, per - 1)
            if quarter % 2 == 0:
                row = row + per * (s[1] if quarter == 0 else 1 - s[1])
            return row, at

        return pl.BlockSpec((block, units), index)

    pieces = [both, across, both, across_core]
    return [spec(quarter) for quarter in quarters], [pieces[quarter] for quarter in quarters]


def stack_kernel(*refs):
    first = 0
    for ref in refs[:-1]:
        refs[-1][:, first : first + ref.shape[1]] = ref[...]
        first += ref.shape[1]


def stack(parts, deps):
    shape = (parts[0].shape[0], sum(p.shape[1] for p in parts))
    return launch(
        stack_kernel,
        [],
        parts,
        deps,
        (1,),
        [whole_block(p) for p in parts],
        pl.BlockSpec(shape, lambda j: (0, 0)),
        jax.ShapeDtypeStruct(shape, bf16),
        us=1.5,
    )


def own_kernel(spot_ref, both_ref, out_ref):
    out_ref[...] = both_ref[...]


def own_rows(spot, both, deps):
    rows, width = both.shape
    steps = 4
    block = rows // 2 // steps
    return launch(
        own_kernel,
        [spot],
        [both],
        deps,
        (steps,),
        [pl.BlockSpec((block, width), lambda j, s: (s[1] * steps + j, 0))],
        pl.BlockSpec((block, width), lambda j, s: (j, 0)),
        jax.ShapeDtypeStruct((rows // 2, width), bf16),
        us=4,
    )


def gate_kernel(in_ref, out_ref):
    pass


def gate(array, deps):
    anywhere = pl.BlockSpec(memory_space=pl.ANY)
    return launch(
        gate_kernel,
        [],
        [array],
        deps,
        (1,),
        [anywhere],
        anywhere,
        jax.ShapeDtypeStruct(array.shape, array.dtype),
        aliases=((0, 0),),
        us=1,
    )


def product(act_ref, parts):
    depth = parts[0].shape[0]
    return sum(
        dot_plain(act_ref[:, i * depth : i * depth + depth], part[...]) for i, part in enumerate(parts)
    )


def feed_kernel(spot_ref, x_ref, g_ref, *refs):
    pieces, (h_ref, gg_ref, ug_ref) = refs[:12], refs[12:]
    gate = product(x_ref, pieces[:4])
    up = product(x_ref, pieces[4:8])
    sigmoid = jax.nn.sigmoid(gate)
    silu = gate * sigmoid
    h_ref[...] = (silu * up).astype(bf16)
    grad = product(g_ref, pieces[8:])
    gg_ref[...] = (grad * up * (sigmoid * (1.0 + gate * (1.0 - sigmoid)))).astype(bf16)
    ug_ref[...] = (grad * silu).astype(bf16)


def feed(spot, normed, grads, weight, deps):
    rows, width = normed.shape
    units = weight[0].shape[1] // 3
    blocks = units // BLOCK
    specs, operands = [whole_block(normed), whole_block(grads)], [normed, grads]
    for at in range(3):
        more = weight_columns(weight, lambda j, at=at: j + at * blocks)
        specs += more[0]
        operands += more[1]
    return launch(
        feed_kernel,
        [spot],
        operands,
        deps,
        (blocks,),
        specs,
        [pl.BlockSpec((rows, BLOCK), lambda j, s: (0, j))] * 3,
        [jax.ShapeDtypeStruct((rows, units), bf16)] * 3,
        us=rows * width * units / 10**8,
    )


def project_kernel(rotated, spot_ref, own_ref, other_ref, *refs):
    parts, out_ref = refs[:4], refs[-1]
    rows = own_ref.shape[0]
    for act_ref, place in ((own_ref, spot_ref[0]), (other_ref, 1 - spot_ref[0])):
        at = pl.ds(pl.multiple_of(place * rows, rows), rows)
        total = product(act_ref, parts)
        if rotated is None:
            out_ref[at, :] = total.astype(bf16)
        else:
            cosine, sine = refs[4][at, :], refs[5][at, :]
            for half in range(2):
                piece = total[:, half * 128 : half * 128 + 128]
                keep = 2 * pl.program_id(0) + half >= rotated
                piece = jnp.where(keep, piece, turn(piece, cosine, sine))
                out_ref[at, half * 128 : half * 128 + 128] = piece.astype(bf16)


def project(spot, own, other, weight, deps, tables=(), rotated=None):
    rows, width = own.shape
    units = weight[0].shape[1]
    specs, operands = weight_columns(weight, lambda j: j)
    return launch(
        functools.partial(project_kernel, rotated),
        [spot],
        [own, other, *operands, *tables],
        deps,
        (units // BLOCK,),
        [whole_block(own), whole_block(other), *specs, *(whole_block(t) for t in tables)],
        pl.BlockSpec((2 * rows, BLOCK), lambda j, s: (0, j)),
        jax.ShapeDtypeStruct((2 * rows, units), bf16),
        us=rows * width * units / 10**8,
    )


def back_kernel(count, parts, placed, spot_ref, *refs):
    step = pl.program_id(0)
    acts = refs[:count]
    weights = refs[count : count + parts * count]
    mine_ref, theirs_ref = refs[-2:]
    rows = mine_ref.shape[0]

    def run(part):
        total = sum(dot_trans(a[...], weights[parts * i + part][...]) for i, a in enumerate(acts))
        mine, theirs = total[:rows], total[rows:]
        if placed:
            first = spot_ref[0] == 0
            mine, theirs = jnp.where(first, mine, theirs), jnp.where(first, theirs, mine)
        mine_ref[...] = mine.astype(mine_ref.dtype)
        theirs_ref[...] = theirs.astype(theirs_ref.dtype)

    for part in range(parts):
        pl.when(step // (pl.num_programs(0) // parts) == part)(functools.partial(run, part))


def back(spot, acts, weights, deps, placed=False, quarters=(0, 1, 2, 3)):
    rows = acts[0].shape[0]
    depth = weights[0][0][1].shape[0]
    width = len(quarters) * depth
    block = min(BLOCK, depth)
    half = pl.BlockSpec((rows // 2, block), lambda j, s: (0, j))
    specs, operands = [whole_block(a) for a in acts], list(acts)
    for act, (weight, at) in zip(acts, weights):
        more = weight_rows(weight, block, act.shape[1], at, quarters)
        specs += more[0]
        operands += more[1]
    return launch(
        functools.partial(back_kernel, len(acts), len(quarters), placed),
        [spot],
        operands,
        deps,
        (width // block,),
        specs,
        [half, half],
        [jax.ShapeDtypeStruct((rows // 2, width), kind) for kind in (f32, bf16)],
        us=rows * width * sum(a.shape[1] for a in acts) / 285000000,
    )


def grad_kernel(which, added, placed, *refs):
    if placed:
        spot_ref, *refs = refs
    step, steps = pl.program_id(0), pl.num_programs(0)
    acts = refs[: 2 if placed else max(which) + 1]
    count = len(which)
    grads = refs[len(acts) : len(acts) + count]
    first = 0
    for i in range(count):
        at = slice(first, first + grads[i].shape[1])
        first = at.stop
        if placed:
            rows = acts[0].shape[0]
            total = 0.0
            for act, place in ((acts[0], spot_ref[0]), (acts[1], 1 - spot_ref[0])):
                here = pl.ds(pl.multiple_of(place * rows, rows), rows)
                total = total + dot_inner(act[...], grads[i][here, :])
        else:
            total = dot_inner(acts[which[i]][...], grads[i][...])
        if not added:
            refs[-1][:, at] = total.astype(bf16)
            continue
        total = (total + refs[-3][:, at].astype(f32)).astype(bf16)

        @pl.when(step < steps // 2)
        def _():
            refs[-2][:, at] = total

        @pl.when(step >= steps // 2)
        def _():
            refs[-1][:, at] = total


def grad(acts, which, grads, deps, added=None, us=None, spot=None):
    tokens, width = acts[0].shape
    block = min(BLOCK, width // 4)
    steps = width // 2 // block
    half = steps // 2
    units = sum(g.shape[1] for g in grads)
    if added is None:
        row = lambda j: j + steps
        outs = pl.BlockSpec((block, units), lambda j, *s: (j, 0))
        shapes = jax.ShapeDtypeStruct((width // 2, units), bf16)
    else:
        row = lambda j: (j + half) % steps
        outs = [
            pl.BlockSpec((block, units), lambda j, *s: (jnp.minimum(j, half - 1), 0)),
            pl.BlockSpec((block, units), lambda j, *s: (jnp.maximum(j - half, 0), 0)),
        ]
        shapes = [jax.ShapeDtypeStruct((width // 4, units), bf16)] * 2
    specs = [pl.BlockSpec((tokens, block), lambda j, *s: (0, row(j))) for _ in acts]
    specs += [whole_block(g) for g in grads]
    operands = [*acts, *grads]
    if added is not None:
        specs.append(pl.BlockSpec((block, units), lambda j, *s: (row(j), 0)))
        operands.append(added)
    return launch(
        functools.partial(grad_kernel, which, added is not None, spot is not None),
        [] if spot is None else [spot],
        operands,
        deps,
        (steps,),
        specs,
        outs,
        shapes,
        us=us or tokens * width * units / 480000000,
    )


def attention_specs(length, queries, wide):
    pair = lambda first: pl.BlockSpec((length, 128), lambda g, i, low: (0, first))
    col = pl.BlockSpec((queries, 1), lambda g, i, low: (i, 0))
    row = pl.BlockSpec((1, length), lambda g, i, low: (0, 0))
    return pl.BlockSpec((queries, wide), lambda g, i, low: (i, g)), pair, col, row


def attend(rotated, query_width, first_seen, segment_row, scale, deps):
    length = rotated.shape[0]
    queries = length // first_seen.shape[0]
    groups = 2
    heads, pair, col, row = attention_specs(length, queries, query_width // groups)
    first = query_width // 128
    return launch(
        functools.partial(forward_kernel, scale),
        [first_seen],
        [rotated, rotated, rotated, segment_row.reshape(length, 1), segment_row.reshape(1, length)],
        deps,
        (groups, length // queries),
        [heads, pair(first), pair(first + 1), col, row],
        [heads, pl.BlockSpec((queries, 128), lambda g, i, low: (i, g))],
        [
            jax.ShapeDtypeStruct((length, query_width), bf16),
            jax.ShapeDtypeStruct((length, groups * 128), f32),
        ],
        [pltpu.VMEM((length, 256), bf16)] * 2,
        us=16,
    )


def attend_back(rotated, grads, lse, query_width, first_seen, segment_row, cosine, sine, scale, deps):
    length = rotated.shape[0]
    queries = length // first_seen.shape[0]
    groups = 2
    heads, pair, col, row = attention_specs(length, queries, query_width // groups)
    first = query_width // 128
    table = pl.BlockSpec((queries, 128), lambda g, i, low: (i, 0))
    return launch(
        functools.partial(backward_kernel, scale),
        [first_seen],
        [
            rotated, rotated, rotated, grads, lse, segment_row.reshape(length, 1),
            segment_row.reshape(1, length), cosine, sine, cosine, sine,
        ],
        deps,
        (groups, length // queries),
        [
            heads, pair(first), pair(first + 1), heads,
            pl.BlockSpec((queries, 128), lambda g, i, low: (i, g)), col, row, table, table, pair(0), pair(0),
        ],
        [heads, pair(0), pair(0)],
        [
            jax.ShapeDtypeStruct((length, query_width), bf16),
            jax.ShapeDtypeStruct((length, 128), bf16),
            jax.ShapeDtypeStruct((length, 128), bf16),
        ],
        [pltpu.VMEM((length, 256), bf16)] * 2 + [pltpu.VMEM((length, 256), f32)] * 2,
        us=35,
    )


def join_kernel(spot_ref, own_ref, other_ref, out_ref):
    rows = own_ref.shape[0]
    for ref, place in ((own_ref, spot_ref[0]), (other_ref, 1 - spot_ref[0])):
        out_ref[pl.ds(pl.multiple_of(place * rows, rows), rows), :] = ref[...]


def join(spot, own, other, deps):
    rows, width = own.shape
    block = width // 4
    half = pl.BlockSpec((rows, block), lambda j, s: (0, j))
    return launch(
        join_kernel,
        [spot],
        [own, other],
        deps,
        (4,),
        [half, half],
        pl.BlockSpec((2 * rows, block), lambda j, s: (0, j)),
        jax.ShapeDtypeStruct((2 * rows, width), bf16),
        us=4,
    )


def add_kernel(a_ref, b_ref, out_ref):
    out_ref[...] = (a_ref[...].astype(f32) + b_ref[...].astype(f32)).astype(out_ref.dtype)


def add(a, b, deps, us=4, kind=bf16):
    rows, width = a.shape
    block = pl.BlockSpec((rows // 4, width), lambda j: (j, 0))
    return launch(
        add_kernel, [], [a, b], deps, (4,), [block, block], block, jax.ShapeDtypeStruct(a.shape, kind), us=us
    )


def natural_block(spot_ref, outer, core, x, z):
    x = 1 - spot_ref[2] if x else spot_ref[2]
    core = 1 - spot_ref[1] if core else spot_ref[1]
    return (z * 2 + x) * 2 + core


def reorder(spot_ref, outer, width):
    size = width // (4 * outer)
    for core in range(2):
        for x in range(2):
            for z in range(outer):
                at = ((core * 2 + x) * outer + z) * size
                there = natural_block(spot_ref, outer, core, x, z) * size
                yield slice(at, at + size), pl.ds(pl.multiple_of(there, size), size)


def inverse_rms(activity):
    return lax.rsqrt(jnp.mean(activity * activity, axis=-1, keepdims=True) + epsilon)


def norm_back(activity, inverse, gain_vec, incoming):
    scaled = incoming * gain_vec
    return inverse * scaled - activity * (inverse * inverse * inverse) * jnp.mean(
        scaled * activity, axis=-1, keepdims=True
    )


def enter_kernel(outer, spot_ref, tokens_ref, gain_ref, out_ref, normed_ref):
    if outer:
        for here, there in reorder(spot_ref, outer, tokens_ref.shape[1]):
            out_ref[:, here] = tokens_ref[:, there]
    else:
        out_ref[...] = tokens_ref[...]
    inputs = out_ref[...].astype(f32)
    normed_ref[...] = (inputs * inverse_rms(inputs) * gain_ref[...]).astype(bf16)


def turn_kernel(outer, spot_ref, array_ref, out_ref):
    for here, there in reorder(spot_ref, outer, array_ref.shape[1]):
        out_ref[:, here] = array_ref[:, there]


def rows_spec(rows, width):
    return pl.BlockSpec((rows // ROW_STEPS, width), lambda j, *s: (j, 0))


def enter(spot, outer, tokens, gain, deps):
    spec = rows_spec(*tokens.shape)
    return launch(
        functools.partial(enter_kernel, outer),
        [spot],
        [tokens, gain],
        deps,
        (ROW_STEPS,),
        [spec, whole_block(gain)],
        [spec, spec],
        [jax.ShapeDtypeStruct(tokens.shape, bf16)] * 2,
        us=3,
    )


def to_order(spot, outer, array, deps):
    spec = rows_spec(*array.shape)
    return launch(
        functools.partial(turn_kernel, outer),
        [spot],
        [array],
        deps,
        (ROW_STEPS,),
        [spec],
        spec,
        jax.ShapeDtypeStruct(array.shape, bf16),
        us=3,
    )


def middle_kernel(tokens_ref, own_ref, other_ref, gain_ref, normed_ref, middle_ref):
    middle = tokens_ref[...].astype(f32) + own_ref[...] + other_ref[...].astype(f32)
    middle_ref[...] = middle
    normed_ref[...] = (middle * inverse_rms(middle) * gain_ref[...]).astype(bf16)


def middle_forward(tokens, own, other, gain, deps):
    spec = rows_spec(*tokens.shape)
    return launch(
        middle_kernel,
        [],
        [tokens, own, other, gain],
        deps,
        (ROW_STEPS,),
        [spec, spec, spec, whole_block(gain)],
        [spec, spec],
        [jax.ShapeDtypeStruct(tokens.shape, bf16), jax.ShapeDtypeStruct(tokens.shape, f32)],
        us=5,
    )


def gain_part(part_ref, product):
    @pl.when(pl.program_id(0) == 0)
    def _():
        part_ref[...] = jnp.zeros_like(part_ref)

    part_ref[...] += jnp.sum(product, axis=0, keepdims=True)


def middle_back_kernel(own_ref, other_ref, middle_ref, grad_ref, gain_ref, low_ref, out_ref, part_ref):
    incoming = own_ref[...] + other_ref[...].astype(f32)
    middle = middle_ref[...]
    inverse = inverse_rms(middle)
    out = grad_ref[...].astype(f32) + norm_back(middle, inverse, gain_ref[...], incoming)
    out_ref[...] = out
    low_ref[...] = out.astype(bf16)
    gain_part(part_ref, incoming * middle * inverse)


def middle_backward(own, other, middle, out_grad, gain, deps):
    spec = rows_spec(*own.shape)
    part = jax.ShapeDtypeStruct(gain.shape, f32)
    return launch(
        middle_back_kernel,
        [],
        [own, other, middle, out_grad, gain],
        deps,
        (ROW_STEPS,),
        [spec, spec, spec, spec, whole_block(gain)],
        [spec, spec, whole_block(gain)],
        [jax.ShapeDtypeStruct(own.shape, bf16), jax.ShapeDtypeStruct(own.shape, f32), part],
        us=8,
    )


def leave(outer, spot_ref, out_ref, value):
    value = value.astype(bf16)
    if outer:
        for here, there in reorder(spot_ref, outer, value.shape[1]):
            out_ref[:, there] = value[:, here]
    else:
        out_ref[...] = value


def block_out_kernel(outer, spot_ref, middle_ref, own_ref, other_ref, out_ref):
    leave(outer, spot_ref, out_ref, middle_ref[...] + own_ref[...] + other_ref[...].astype(f32))


def block_result(spot, outer, middle, own, other, deps):
    spec = rows_spec(*own.shape)
    return launch(
        functools.partial(block_out_kernel, outer),
        [spot],
        [middle, own, other],
        deps,
        (ROW_STEPS,),
        [spec, spec, spec],
        spec,
        jax.ShapeDtypeStruct(own.shape, bf16),
        us=5,
    )


def gain_kernel(own_ref, sent_ref, tokens_ref, other_ref, gain_ref, part_ref):
    inputs = tokens_ref[...].astype(f32)
    mine = own_ref[...] * inputs * inverse_rms(inputs)
    theirs = sent_ref[...].astype(f32) * other_ref[...].astype(f32) / gain_ref[...]
    gain_part(part_ref, mine + theirs)


def gain_sum(own, sent, tokens, normed_other, gain, deps):
    spec = rows_spec(*own.shape)
    return launch(
        gain_kernel,
        [],
        [own, sent, tokens, normed_other, gain],
        deps,
        (ROW_STEPS,),
        [spec, spec, spec, spec, whole_block(gain)],
        whole_block(gain),
        jax.ShapeDtypeStruct(gain.shape, f32),
        us=30,
    )


def input_back_kernel(outer, spot_ref, own_ref, other_ref, tokens_ref, grad_ref, gain_ref, out_ref):
    incoming = own_ref[...] + other_ref[...].astype(f32)
    inputs = tokens_ref[...].astype(f32)
    inverse = inverse_rms(inputs)
    leave(outer, spot_ref, out_ref, grad_ref[...] + norm_back(inputs, inverse, gain_ref[...], incoming))


def input_backward(spot, outer, own, other, tokens, middle_grad, gain, deps):
    spec = rows_spec(*own.shape)
    return launch(
        functools.partial(input_back_kernel, outer),
        [spot],
        [own, other, tokens, middle_grad, gain],
        deps,
        (ROW_STEPS,),
        [spec, spec, spec, spec, whole_block(gain)],
        spec,
        jax.ShapeDtypeStruct(own.shape, bf16),
        us=SHORT,
    )


class Order:
    def __init__(self):
        self.before = []

    def wait(self, *arrays):
        self.before += arrays

    def __call__(self, compute, *operands, **options):
        result = compute(*operands, deps=self.before, **options)
        self.before = [result[0] if isinstance(result, (tuple, list)) else result]
        return result


def chunk_edges(width):
    blocks = width // BLOCK
    return [BLOCK * (-(-blocks * i // CHUNKS)) for i in range(CHUNKS + 1)]


def make_shards(outer):
    def relative(array):
        rows, width = array.shape
        blocks = array.reshape(rows, outer, 2, 2, width // (4 * outer))
        blocks = jnp.where(lax.axis_index("x") == 0, blocks, blocks[:, :, ::-1])
        blocks = jnp.where(lax.axis_index("core") == 0, blocks, blocks[:, :, :, ::-1])
        return blocks.transpose(0, 3, 2, 1, 4).reshape(rows, width)

    def natural(array):
        rows, width = array.shape
        blocks = array.reshape(rows, 2, 2, outer, width // (4 * outer)).transpose(0, 3, 2, 1, 4)
        blocks = jnp.where(lax.axis_index("x") == 0, blocks, blocks[:, :, ::-1])
        blocks = jnp.where(lax.axis_index("core") == 0, blocks, blocks[:, :, :, ::-1])
        return blocks.reshape(rows, width)

    def over_x(array):
        return lax.ppermute(array, "x", SWAP)

    def over_core(array):
        return lax.ppermute(array, "core", SWAP)

    def gather(operand):
        return lax.all_gather(operand, ("core", "z"), axis=0, tiled=True)

    def scatter(operand):
        return lax.psum_scatter(operand, "z", scatter_dimension=0, tiled=True)

    def total(vector):
        for axis in ("core", "x", "tensor"):
            vector = vector + lax.ppermute(vector, axis, SWAP)
        step = 1
        while step < outer:
            vector = vector + lax.ppermute(vector, "z", [(i, i ^ step) for i in range(outer)])
            step *= 2
        return vector

    def swap(own):
        return lax.ppermute(own, "tensor", SWAP)

    def shards(
        tokens,
        segments,
        q_weight,
        k_weight,
        v_weight,
        o_weight,
        attention_gain,
        gate_weight,
        up_weight,
        down_weight,
        feed_gain,
        out_grad,
    ):
        query_width = q_weight.shape[1]
        key_width = k_weight.shape[1]
        score_scale = HEAD_DIM ** (-0.5)
        place, core, cross = (lax.axis_index(axis) for axis in ("tensor", "core", "x"))
        spot = jnp.stack([place, core, cross]).astype(jnp.int32)
        here = jnp.zeros_like(spot)
        edges = chunk_edges(gate_weight.shape[1])
        order = Order()
        along, full = {}, {}

        def spread(name):
            full[name] = over_x(order(lambda deps: own_rows(spot, along[name], deps)))

        def land(name):
            across = order(lambda deps: gate(full[name], deps))
            full[name] = (along[name], across, over_core(across))

        def chunk(i):
            columns = slice(edges[i], edges[i + 1])
            parts = [w[:, columns] for w in (gate_weight, up_weight, down_weight)]
            along[i] = gather(order(lambda deps: stack(parts, deps)))

        tiles = outer if tokens.shape[1] // (4 * outer) % 128 == 0 else 0
        along["qkv"] = gather(order(lambda deps: stack([q_weight, k_weight, v_weight], deps)))
        along["o"] = gather(order(lambda deps: stack([o_weight], deps)))
        for i in range(CHUNKS):
            chunk(i)
        attention_gain = relative(attention_gain[None])
        feed_gain = relative(feed_gain[None])
        if not tiles:
            tokens, out_grad = relative(tokens), relative(out_grad)
        tokens, normed_first = order(lambda deps: enter(spot, tiles, tokens, attention_gain, deps))
        normed_other = swap(normed_first)
        segment_row = segments[0]
        cosine, sine = rotary_tables(segment_row)
        first_seen = first_blocks(segment_row)
        spread("qkv")
        if tiles:
            out_grad = order(lambda deps: to_order(spot, tiles, out_grad, deps))
        grad_other = swap(out_grad)
        order.wait(cosine, sine, first_seen)
        normed_seq = order(lambda deps: join(spot, normed_first, normed_other, deps))
        land("qkv")
        spread("o")
        rotated = order(
            lambda deps: project(
                spot, normed_first, normed_other, full["qkv"], deps, (cosine, sine),
                (query_width + key_width) // 128,
            )
        )
        mixed, log_totals = order(
            lambda deps: attend(rotated, query_width, first_seen, segment_row, score_scale, deps)
        )
        land("o")
        grad_seq = order(lambda deps: join(here, out_grad, grad_other, deps))
        own, sent = order(lambda deps: back(spot, (mixed,), ((full["o"], 0),), deps, True))
        other = swap(sent)
        spread(0)
        normed_second, middle = order(lambda deps: middle_forward(tokens, own, other, feed_gain, deps))
        normed_third = swap(normed_second)
        spread(1)
        land(0)
        normed_feed = order(lambda deps: join(here, normed_second, normed_third, deps))
        hidden, gate_grad, up_grad = {}, {}, {}
        from_core, to_x, from_x, kept, summed = {}, {}, {}, {}, {}

        def run_feed(i):
            hidden[i], gate_grad[i], up_grad[i] = order(
                lambda deps: feed(spot, normed_feed, grad_seq, full[i], deps)
            )

        def core_part(i):
            grads = (gate_grad[i], up_grad[i], hidden[i])
            part = order(lambda deps: grad((normed_feed, grad_seq), (0, 0, 1), grads, deps))
            from_core[i] = over_core(part)

        def x_part(i):
            grads = (gate_grad[i], up_grad[i], hidden[i])
            to_x[i], kept[i] = order(
                lambda deps: grad((normed_feed, grad_seq), (0, 0, 1), grads, deps, from_core[i])
            )

        def send_x(i):
            from_x[i] = over_x(to_x[i])

        def finish(i, us=4):
            summed[i] = scatter(order(lambda deps: add(kept[i], from_x[i], deps, us)))

        def feed_back(chunks):
            acts = [a[i] for i in chunks for a in (gate_grad, up_grad)]
            weights = [(full[i], at) for i in chunks for at in (0, 1)]
            return order(lambda deps: back(spot, acts, weights, deps))

        run_feed(0)
        core_part(0)
        spread(2)
        land(1)
        run_feed(1)
        core_part(1)
        spread(3)
        x_part(0)
        sent_along, kept_along = scatter(to_x[0]), scatter(kept[0])
        land(2)
        run_feed(2)
        x_part(1)
        send_x(1)
        core_part(2)
        land(3)
        run_feed(3)
        from_along = over_x(order(lambda deps: gate(sent_along, deps)))
        own, sent = feed_back(range(CHUNKS))
        other = swap(sent)
        x_part(2)
        send_x(2)
        core_part(3)
        order.wait(from_along, kept_along)
        finish(1)
        attn_out_grad, middle_grad, feed_gain_part = order(
            lambda deps: middle_backward(own, other, middle, out_grad, feed_gain, deps)
        )
        attn_other = swap(attn_out_grad)
        x_part(3)
        send_x(3)
        block_own, block_sent = order(
            lambda deps: back(
                spot, [hidden[i] for i in range(CHUNKS)], [(full[i], 2) for i in range(CHUNKS)], deps
            )
        )
        block_other = swap(block_sent)
        finish(2)
        both = (attn_out_grad, attn_other)
        from_core["o"] = over_core(order(lambda deps: grad(both, (0,), (mixed,), deps, spot=spot)))
        mixed_grad = order(lambda deps: project(spot, attn_out_grad, attn_other, full["o"], deps))
        to_x["o"], kept["o"] = order(
            lambda deps: grad(both, (0,), (mixed,), deps, from_core["o"], spot=spot)
        )
        send_x("o")
        finish(3)
        qkv_grad = order(
            lambda deps: attend_back(
                rotated, mixed_grad, log_totals, query_width, first_seen, segment_row, cosine, sine,
                score_scale, deps,
            )
        )
        order.wait(from_x["o"], block_other)
        from_core["qkv"] = over_core(
            order(lambda deps: grad((normed_seq,), (0,) * 3, qkv_grad, deps, us=SHORT))
        )
        to_x["qkv"], kept["qkv"] = order(
            lambda deps: grad((normed_seq,), (0,) * 3, qkv_grad, deps, from_core["qkv"], us=SHORT)
        )
        send_x("qkv")
        order.wait(summed[3])
        finish("o")
        places = (0, query_width // key_width, query_width // key_width + 1)
        own, sent = order(
            lambda deps: back(spot, qkv_grad, [(full["qkv"], at) for at in places], deps, True)
        )
        other = swap(sent)
        summed[0] = order(lambda deps: add(kept_along, from_along, deps, kind=f32))
        block_out = order(lambda deps: block_result(spot, tiles, middle, block_own, block_other, deps))
        order.wait(summed["o"])
        finish("qkv")
        attention_gain_part = order(
            lambda deps: gain_sum(own, sent, tokens, normed_other, attention_gain, deps)
        )
        input_grad = order(
            lambda deps: input_backward(spot, tiles, own, other, tokens, middle_grad, attention_gain, deps)
        )
        gains = total(natural(jnp.concatenate([attention_gain_part, feed_gain_part], axis=0)))
        if not tiles:
            block_out, input_grad = natural(block_out), natural(input_grad)
        qkv_weight_grad = summed["qkv"].astype(f32)

        def whole(at):
            parts = []
            for i in range(CHUNKS):
                units = edges[i + 1] - edges[i]
                parts.append(summed[i][:, at * units : at * units + units].astype(f32))
            return jnp.concatenate(parts, axis=1)

        return (
            block_out,
            input_grad,
            qkv_weight_grad[:, :query_width],
            qkv_weight_grad[:, query_width : query_width + key_width],
            qkv_weight_grad[:, query_width + key_width :],
            summed["o"].astype(f32),
            gains[0],
            whole(0),
            whole(1),
            whole(2),
            gains[1],
        )

    return shards


def solution(mesh):
    outer = mesh.shape["dp"] // 4
    fine = Mesh(
        mesh.devices.reshape(outer, 2, 2, mesh.shape["tensor"]), ("z", "x", "core", "tensor")
    )
    dp = ("z", "x", "core")
    every = P(dp + ("tensor",), None)
    weight = P(dp, "tensor")
    return jax.shard_map(
        make_shards(outer),
        mesh=fine,
        in_specs=(
            every,
            P(dp, None),
            weight,
            weight,
            weight,
            weight,
            P(),
            weight,
            weight,
            weight,
            P(),
            every,
        ),
        out_specs=(every, every, weight, weight, weight, weight, P(), weight, weight, weight, P()),
        check_vma=False,
    )
```

```python
import functools

import jax
import jax.numpy as jnp
from jax import lax
from jax.experimental import pallas as pl
from jax.experimental.pallas import tpu as pltpu
from jax.sharding import Mesh, PartitionSpec as P

HEAD_DIM = 64
SWAP = ((0, 1), (1, 0))
QUERIES = 256
CHUNKS = 4
BLOCK = 256
ROW_STEPS = 3
COST = 10**10
SHORT = 0.01
VMEM = 48 * 2**20
epsilon = 1e-05
rope_base = 10000.0
bf16 = jnp.bfloat16
f32 = jnp.float32


def dot_plain(left, right):
    return jnp.dot(left, right, preferred_element_type=f32)


def dot_trans(left, right):
    return lax.dot_general(left, right, (((1,), (1,)), ((), ())), preferred_element_type=f32)


def dot_inner(left, right):
    return lax.dot_general(left, right, (((0,), (0,)), ((), ())), preferred_element_type=f32)


def rotary_tables(segment_row):
    length = segment_row.shape[0]
    before = jnp.sum((segment_row[None, :] < segment_row[:, None]).astype(jnp.int32), axis=1)
    places = (jnp.arange(length, dtype=jnp.int32) - before).astype(f32)
    half_dim = HEAD_DIM // 2
    frequency = rope_base ** (-2.0 * jnp.arange(half_dim).astype(f32) / HEAD_DIM)
    angles = places[:, None] * frequency[None, :]
    cosine, sine = jnp.cos(angles), jnp.sin(angles)
    return (jnp.concatenate([cosine] * 4, axis=1), jnp.concatenate([-sine, sine] * 2, axis=1))


def first_blocks(segment_row):
    starts, ends = segment_row[::QUERIES], segment_row[QUERIES - 1 :: QUERIES]
    return jnp.sum((ends[None, :] < starts[:, None]).astype(jnp.int32), axis=1)


def lanes_of(shape):
    return lax.broadcasted_iota(jnp.int32, shape, len(shape) - 1)


def turn(block, cosine, sine):
    low_half = lanes_of(block.shape) % HEAD_DIM < HEAD_DIM // 2
    other = jnp.where(low_half, pltpu.roll(block, 96, 1), pltpu.roll(block, 32, 1))
    return block * cosine + other * sine


def widen(pair_ref, wide_ref, group):
    pair = pair_ref[...]
    keep = (lanes_of(pair.shape) < HEAD_DIM) == (group == 0)
    half = jnp.where(keep, pair, pltpu.roll(pair.astype(f32), HEAD_DIM, 1).astype(bf16))
    wide_ref[:, :128] = half
    wide_ref[:, 128:] = half


def seen_bias(col_ref, row_ref, start, keys, step):
    queries = col_ref.shape[0]
    same = col_ref[...] == row_ref[:, pl.ds(start, keys)]
    q_at = lax.broadcasted_iota(jnp.int32, (queries, keys), 0) + step * queries
    k_at = lax.broadcasted_iota(jnp.int32, (queries, keys), 1) + start
    return jnp.where(same & (q_at >= k_at), 0.0, -1e30).astype(f32)


def forward_kernel(scale, low_ref, q_ref, k_ref, v_ref, col_ref, row_ref, o_ref, lse_ref, kw_ref, vw_ref):
    group, step = pl.program_id(0), pl.program_id(1)
    queries = q_ref.shape[0]

    @pl.when(step == 0)
    def _():
        widen(k_ref, kw_ref, group)
        widen(v_ref, vw_ref, group)

    def run(blocks):
        keys = blocks * queries
        start = pl.multiple_of(low_ref[step] * queries, queries)
        bias = seen_bias(col_ref, row_ref, start, keys, step)
        key = kw_ref[pl.ds(start, keys), :]
        value = vw_ref[pl.ds(start, keys), :]
        head_of = lanes_of((queries, 256)) // HEAD_DIM
        lse = jnp.zeros((queries, 128), f32)
        for quad in range(q_ref.shape[1] // 256):
            wide = q_ref[:, quad * 256 : quad * 256 + 256] * scale
            out = jnp.zeros((queries, 256), f32)
            for j in range(4):
                one = jnp.where(head_of == j, wide, jnp.zeros_like(wide))
                scores = dot_trans(one, key) + bias
                top = jnp.max(scores, axis=1, keepdims=True)
                powers = jnp.exp(scores - top)
                sums = jnp.sum(powers, axis=1, keepdims=True)
                prob = (powers * (1.0 / sums)).astype(bf16)
                out = jnp.where(head_of == j, dot_plain(prob, value), out)
                lse = jnp.where(lanes_of(lse.shape) == quad * 4 + j, top + jnp.log(sums), lse)
            o_ref[:, quad * 256 : quad * 256 + 256] = out.astype(bf16)
        lse_ref[...] = lse

    for blocks in range(1, row_ref.shape[1] // queries + 1):
        pl.when(step + 1 - low_ref[step] == blocks)(functools.partial(run, blocks))


def backward_kernel(
    scale, low_ref, q_ref, k_ref, v_ref, g_ref, lse_ref, col_ref, row_ref, cos_ref, sin_ref, kcos_ref, ksin_ref,
    dq_ref, dk_ref, dv_ref, kw_ref, vw_ref, dkw_ref, dvw_ref,
):
    group, step = pl.program_id(0), pl.program_id(1)
    queries = q_ref.shape[0]

    @pl.when(step == 0)
    def _():
        widen(k_ref, kw_ref, group)
        widen(v_ref, vw_ref, group)
        dkw_ref[...] = jnp.zeros_like(dkw_ref)
        dvw_ref[...] = jnp.zeros_like(dvw_ref)

    def run(blocks):
        keys = blocks * queries
        start = pl.multiple_of(low_ref[step] * queries, queries)
        bias = seen_bias(col_ref, row_ref, start, keys, step)
        key = kw_ref[pl.ds(start, keys), :]
        value = vw_ref[pl.ds(start, keys), :]
        head_of = lanes_of((queries, 256)) // HEAD_DIM
        cosine, sine = cos_ref[...], sin_ref[...]
        for quad in range(q_ref.shape[1] // 256):
            wide = q_ref[:, quad * 256 : quad * 256 + 256] * scale
            grads = g_ref[:, quad * 256 : quad * 256 + 256]
            out = jnp.zeros((queries, 256), f32)
            for j in range(4):
                at = quad * 4 + j
                one = jnp.where(head_of == j, wide, jnp.zeros_like(wide))
                grad = jnp.where(head_of == j, grads, jnp.zeros_like(grads))
                prob = jnp.exp(dot_trans(one, key) + bias - lse_ref[:, at : at + 1])
                prob_grad = dot_trans(grad, value)
                centre = jnp.sum(prob * prob_grad, axis=1, keepdims=True)
                score_grad = (prob * (prob_grad - centre)).astype(bf16)
                dvw_ref[pl.ds(start, keys), :] += dot_inner(prob.astype(bf16), grad)
                dkw_ref[pl.ds(start, keys), :] += dot_inner(score_grad, one)
                out = jnp.where(head_of == j, dot_plain(score_grad, key), out)
            for half in range(2):
                piece = turn(out[:, half * 128 : half * 128 + 128] * scale, cosine, -sine)
                dq_ref[:, quad * 256 + half * 128 : quad * 256 + half * 128 + 128] = piece.astype(bf16)

    for blocks in range(1, row_ref.shape[1] // queries + 1):
        pl.when(step + 1 - low_ref[step] == blocks)(functools.partial(run, blocks))

    @pl.when(step == pl.num_programs(1) - 1)
    def _():
        mine = (lanes_of(dk_ref.shape) < HEAD_DIM) == (group == 0)

        def fold(ref):
            pair = ref[:, :128] + ref[:, 128:]
            return pair + pltpu.roll(pair, HEAD_DIM, 1)

        dk = turn(fold(dkw_ref), kcos_ref[...], -ksin_ref[...]).astype(bf16)
        dk_ref[...] = jnp.where(mine, dk, dk_ref[...])
        dv_ref[...] = jnp.where(mine, fold(dvw_ref).astype(bf16), dv_ref[...])


def launch(kernel, scalars, operands, deps, grid, in_specs, out_specs, out_shape, scratch=(), aliases=(), us=3):
    count = len(scalars) + len(operands)

    def body(*refs):
        kernel(*refs[:count], *refs[count + len(deps) :])

    return pl.pallas_call(
        body,
        grid_spec=pltpu.PrefetchScalarGridSpec(
            num_scalar_prefetch=len(scalars),
            grid=grid,
            in_specs=[*in_specs, *([pl.BlockSpec(memory_space=pl.ANY)] * len(deps))],
            out_specs=out_specs,
            scratch_shapes=scratch,
        ),
        out_shape=out_shape,
        compiler_params=pltpu.CompilerParams(vmem_limit_bytes=VMEM),
        cost_estimate=pl.CostEstimate(flops=int(COST * us), bytes_accessed=1024, transcendentals=0),
        input_output_aliases=dict(aliases),
    )(*scalars, *operands, *deps)


def whole_block(array):
    return pl.BlockSpec(array.shape, lambda *at: (0,) * array.ndim)


def weight_columns(weight, column):
    both, across, across_core = weight
    depth = across.shape[0]
    specs = [
        pl.BlockSpec((depth, BLOCK), lambda j, s: (s[1], column(j))),
        pl.BlockSpec((depth, BLOCK), lambda j, s: (0, column(j))),
        pl.BlockSpec((depth, BLOCK), lambda j, s: (1 - s[1], column(j))),
        pl.BlockSpec((depth, BLOCK), lambda j, s: (0, column(j))),
    ]
    return specs, [both, across, both, across_core]


def weight_rows(weight, block, units, at):
    both, across, across_core = weight
    per = across.shape[0] // block

    def spec(quarter):
        def index(j, s):
            row = jnp.clip(j - quarter * per, 0, per - 1)
            if quarter % 2 == 0:
                row = row + per * (s[1] if quarter == 0 else 1 - s[1])
            return row, at

        return pl.BlockSpec((block, units), index)

    return [spec(quarter) for quarter in range(4)], [both, across, both, across_core]


def stack_kernel(*refs):
    first = 0
    for ref in refs[:-1]:
        refs[-1][:, first : first + ref.shape[1]] = ref[...]
        first += ref.shape[1]


def stack(parts, deps):
    shape = (parts[0].shape[0], sum(p.shape[1] for p in parts))
    return launch(
        stack_kernel,
        [],
        parts,
        deps,
        (1,),
        [whole_block(p) for p in parts],
        pl.BlockSpec(shape, lambda j: (0, 0)),
        jax.ShapeDtypeStruct(shape, bf16),
        us=1.5,
    )


def own_kernel(spot_ref, both_ref, out_ref):
    out_ref[...] = both_ref[...]


def own_rows(spot, both, deps):
    rows, width = both.shape
    steps = 4
    block = rows // 2 // steps
    return launch(
        own_kernel,
        [spot],
        [both],
        deps,
        (steps,),
        [pl.BlockSpec((block, width), lambda j, s: (s[1] * steps + j, 0))],
        pl.BlockSpec((block, width), lambda j, s: (j, 0)),
        jax.ShapeDtypeStruct((rows // 2, width), bf16),
        us=4,
    )


def gate_kernel(in_ref, out_ref):
    pass


def gate(array, deps):
    anywhere = pl.BlockSpec(memory_space=pl.ANY)
    return launch(
        gate_kernel,
        [],
        [array],
        deps,
        (1,),
        [anywhere],
        anywhere,
        jax.ShapeDtypeStruct(array.shape, array.dtype),
        aliases=((0, 0),),
        us=1,
    )


def product(act_ref, parts):
    depth = parts[0].shape[0]
    return sum(
        dot_plain(act_ref[:, i * depth : i * depth + depth], part[...]) for i, part in enumerate(parts)
    )


def feed_kernel(spot_ref, x_ref, g_ref, *refs):
    pieces, (h_ref, gg_ref, ug_ref) = refs[:12], refs[12:]
    gate = product(x_ref, pieces[:4])
    up = product(x_ref, pieces[4:8])
    sigmoid = jax.nn.sigmoid(gate)
    silu = gate * sigmoid
    h_ref[...] = (silu * up).astype(bf16)
    grad = product(g_ref, pieces[8:])
    gg_ref[...] = (grad * up * (sigmoid * (1.0 + gate * (1.0 - sigmoid)))).astype(bf16)
    ug_ref[...] = (grad * silu).astype(bf16)


def feed(spot, normed, grads, weight, deps):
    rows, width = normed.shape
    units = weight[0].shape[1] // 3
    blocks = units // BLOCK
    specs, operands = [whole_block(normed), whole_block(grads)], [normed, grads]
    for at in range(3):
        more = weight_columns(weight, lambda j, at=at: j + at * blocks)
        specs += more[0]
        operands += more[1]
    return launch(
        feed_kernel,
        [spot],
        operands,
        deps,
        (blocks,),
        specs,
        [pl.BlockSpec((rows, BLOCK), lambda j, s: (0, j))] * 3,
        [jax.ShapeDtypeStruct((rows, units), bf16)] * 3,
        us=rows * width * units / 10**8,
    )


def project_kernel(rotated, spot_ref, own_ref, other_ref, *refs):
    parts, out_ref = refs[:4], refs[-1]
    rows = own_ref.shape[0]
    for act_ref, place in ((own_ref, spot_ref[0]), (other_ref, 1 - spot_ref[0])):
        at = pl.ds(pl.multiple_of(place * rows, rows), rows)
        total = product(act_ref, parts)
        if rotated is None:
            out_ref[at, :] = total.astype(bf16)
        else:
            cosine, sine = refs[4][at, :], refs[5][at, :]
            for half in range(2):
                piece = total[:, half * 128 : half * 128 + 128]
                keep = 2 * pl.program_id(0) + half >= rotated
                piece = jnp.where(keep, piece, turn(piece, cosine, sine))
                out_ref[at, half * 128 : half * 128 + 128] = piece.astype(bf16)


def project(spot, own, other, weight, deps, tables=(), rotated=None):
    rows, width = own.shape
    units = weight[0].shape[1]
    specs, operands = weight_columns(weight, lambda j: j)
    return launch(
        functools.partial(project_kernel, rotated),
        [spot],
        [own, other, *operands, *tables],
        deps,
        (units // BLOCK,),
        [whole_block(own), whole_block(other), *specs, *(whole_block(t) for t in tables)],
        pl.BlockSpec((2 * rows, BLOCK), lambda j, s: (0, j)),
        jax.ShapeDtypeStruct((2 * rows, units), bf16),
        us=rows * width * units / 10**8,
    )


def back_kernel(count, started, placed, spot_ref, *refs):
    step = pl.program_id(0)
    acts = refs[:count]
    weights = refs[count : 5 * count]
    starts = refs[5 * count : 5 * count + 2] if started else None
    mine_ref, theirs_ref = refs[-2:]
    rows = mine_ref.shape[0]

    def run(part):
        total = sum(dot_trans(a[...], weights[4 * i + part][...]) for i, a in enumerate(acts))
        mine, theirs = total[:rows], total[rows:]
        if placed:
            first = spot_ref[0] == 0
            mine, theirs = jnp.where(first, mine, theirs), jnp.where(first, theirs, mine)
        if started:
            mine = mine + starts[0][...].astype(f32)
            theirs = theirs + starts[1][...].astype(f32)
        mine_ref[...] = mine.astype(mine_ref.dtype)
        theirs_ref[...] = theirs.astype(theirs_ref.dtype)

    for part in range(4):
        pl.when(step // (pl.num_programs(0) // 4) == part)(functools.partial(run, part))


def back(spot, acts, weights, deps, placed=False, starts=(), kinds=(f32, bf16)):
    rows = acts[0].shape[0]
    depth = weights[0][0][1].shape[0]
    width = 4 * depth
    block = min(BLOCK, depth)
    half = pl.BlockSpec((rows // 2, block), lambda j, s: (0, j))
    specs, operands = [whole_block(a) for a in acts], list(acts)
    for act, (weight, at) in zip(acts, weights):
        more = weight_rows(weight, block, act.shape[1], at)
        specs += more[0]
        operands += more[1]
    return launch(
        functools.partial(back_kernel, len(acts), len(starts) > 0, placed),
        [spot],
        [*operands, *starts],
        deps,
        (width // block,),
        [*specs, *([half] * len(starts))],
        [half, half],
        [jax.ShapeDtypeStruct((rows // 2, width), kind) for kind in kinds],
        us=rows * width * sum(a.shape[1] for a in acts) / 285000000,
    )


def grad_kernel(which, added, *refs):
    step, steps = pl.program_id(0), pl.num_programs(0)
    acts = refs[: max(which) + 1]
    count = len(which)
    grads = refs[len(acts) : len(acts) + count]
    first = 0
    for i in range(count):
        at = slice(first, first + grads[i].shape[1])
        first = at.stop
        total = dot_inner(acts[which[i]][...], grads[i][...])
        if not added:
            refs[-1][:, at] = total.astype(bf16)
            continue
        total = (total + refs[-3][:, at].astype(f32)).astype(bf16)

        @pl.when(step < steps // 2)
        def _():
            refs[-2][:, at] = total

        @pl.when(step >= steps // 2)
        def _():
            refs[-1][:, at] = total


def grad(acts, which, grads, deps, added=None, us=None):
    tokens, width = acts[0].shape
    block = min(BLOCK, width // 4)
    steps = width // 2 // block
    half = steps // 2
    units = sum(g.shape[1] for g in grads)
    if added is None:
        row = lambda j: j + steps
        outs = pl.BlockSpec((block, units), lambda j: (j, 0))
        shapes = jax.ShapeDtypeStruct((width // 2, units), bf16)
    else:
        row = lambda j: (j + half) % steps
        outs = [
            pl.BlockSpec((block, units), lambda j: (jnp.minimum(j, half - 1), 0)),
            pl.BlockSpec((block, units), lambda j: (jnp.maximum(j - half, 0), 0)),
        ]
        shapes = [jax.ShapeDtypeStruct((width // 4, units), bf16)] * 2
    specs = [pl.BlockSpec((tokens, block), lambda j: (0, row(j))) for _ in acts]
    specs += [whole_block(g) for g in grads]
    operands = [*acts, *grads]
    if added is not None:
        specs.append(pl.BlockSpec((block, units), lambda j: (row(j), 0)))
        operands.append(added)
    return launch(
        functools.partial(grad_kernel, which, added is not None),
        [],
        operands,
        deps,
        (steps,),
        specs,
        outs,
        shapes,
        us=us or tokens * width * units / 480000000,
    )


def attention_specs(length, queries, wide):
    pair = lambda first: pl.BlockSpec((length, 128), lambda g, i, low: (0, first))
    col = pl.BlockSpec((queries, 1), lambda g, i, low: (i, 0))
    row = pl.BlockSpec((1, length), lambda g, i, low: (0, 0))
    return pl.BlockSpec((queries, wide), lambda g, i, low: (i, g)), pair, col, row


def attend(rotated, query_width, first_seen, segment_row, scale, deps):
    length = rotated.shape[0]
    queries = length // first_seen.shape[0]
    groups = 2
    heads, pair, col, row = attention_specs(length, queries, query_width // groups)
    first = query_width // 128
    return launch(
        functools.partial(forward_kernel, scale),
        [first_seen],
        [rotated, rotated, rotated, segment_row.reshape(length, 1), segment_row.reshape(1, length)],
        deps,
        (groups, length // queries),
        [heads, pair(first), pair(first + 1), col, row],
        [heads, pl.BlockSpec((queries, 128), lambda g, i, low: (i, g))],
        [
            jax.ShapeDtypeStruct((length, query_width), bf16),
            jax.ShapeDtypeStruct((length, groups * 128), f32),
        ],
        [pltpu.VMEM((length, 256), bf16)] * 2,
        us=16,
    )


def attend_back(rotated, grads, lse, query_width, first_seen, segment_row, cosine, sine, scale, deps):
    length = rotated.shape[0]
    queries = length // first_seen.shape[0]
    groups = 2
    heads, pair, col, row = attention_specs(length, queries, query_width // groups)
    first = query_width // 128
    table = pl.BlockSpec((queries, 128), lambda g, i, low: (i, 0))
    return launch(
        functools.partial(backward_kernel, scale),
        [first_seen],
        [
            rotated, rotated, rotated, grads, lse, segment_row.reshape(length, 1),
            segment_row.reshape(1, length), cosine, sine, cosine, sine,
        ],
        deps,
        (groups, length // queries),
        [
            heads, pair(first), pair(first + 1), heads,
            pl.BlockSpec((queries, 128), lambda g, i, low: (i, g)), col, row, table, table, pair(0), pair(0),
        ],
        [heads, pair(0), pair(0)],
        [
            jax.ShapeDtypeStruct((length, query_width), bf16),
            jax.ShapeDtypeStruct((length, 128), bf16),
            jax.ShapeDtypeStruct((length, 128), bf16),
        ],
        [pltpu.VMEM((length, 256), bf16)] * 2 + [pltpu.VMEM((length, 256), f32)] * 2,
        us=35,
    )


def join_kernel(spot_ref, own_ref, other_ref, out_ref):
    rows = own_ref.shape[0]
    for ref, place in ((own_ref, spot_ref[0]), (other_ref, 1 - spot_ref[0])):
        out_ref[pl.ds(pl.multiple_of(place * rows, rows), rows), :] = ref[...]


def join(spot, own, other, deps):
    rows, width = own.shape
    block = width // 4
    half = pl.BlockSpec((rows, block), lambda j, s: (0, j))
    return launch(
        join_kernel,
        [spot],
        [own, other],
        deps,
        (4,),
        [half, half],
        pl.BlockSpec((2 * rows, block), lambda j, s: (0, j)),
        jax.ShapeDtypeStruct((2 * rows, width), bf16),
        us=4,
    )


def add_kernel(a_ref, b_ref, out_ref):
    out_ref[...] = (a_ref[...].astype(f32) + b_ref[...].astype(f32)).astype(out_ref.dtype)


def add(a, b, deps, us=4, kind=bf16):
    rows, width = a.shape
    block = pl.BlockSpec((rows // 4, width), lambda j: (j, 0))
    return launch(
        add_kernel, [], [a, b], deps, (4,), [block, block], block, jax.ShapeDtypeStruct(a.shape, kind), us=us
    )


def natural_block(spot_ref, outer, core, x, z):
    x = 1 - spot_ref[2] if x else spot_ref[2]
    core = 1 - spot_ref[1] if core else spot_ref[1]
    return (z * 2 + x) * 2 + core


def reorder(spot_ref, outer, width):
    size = width // (4 * outer)
    for core in range(2):
        for x in range(2):
            for z in range(outer):
                at = ((core * 2 + x) * outer + z) * size
                there = natural_block(spot_ref, outer, core, x, z) * size
                yield slice(at, at + size), pl.ds(pl.multiple_of(there, size), size)


def inverse_rms(activity):
    return lax.rsqrt(jnp.mean(activity * activity, axis=-1, keepdims=True) + epsilon)


def norm_back(activity, inverse, gain_vec, incoming):
    scaled = incoming * gain_vec
    return inverse * scaled - activity * (inverse * inverse * inverse) * jnp.mean(
        scaled * activity, axis=-1, keepdims=True
    )


def enter_kernel(outer, spot_ref, tokens_ref, gain_ref, out_ref, normed_ref):
    if outer:
        for here, there in reorder(spot_ref, outer, tokens_ref.shape[1]):
            out_ref[:, here] = tokens_ref[:, there]
    else:
        out_ref[...] = tokens_ref[...]
    inputs = out_ref[...].astype(f32)
    normed_ref[...] = (inputs * inverse_rms(inputs) * gain_ref[...]).astype(bf16)


def turn_kernel(outer, spot_ref, array_ref, out_ref):
    for here, there in reorder(spot_ref, outer, array_ref.shape[1]):
        out_ref[:, here] = array_ref[:, there]


def rows_spec(rows, width):
    return pl.BlockSpec((rows // ROW_STEPS, width), lambda j, *s: (j, 0))


def enter(spot, outer, tokens, gain, deps):
    spec = rows_spec(*tokens.shape)
    return launch(
        functools.partial(enter_kernel, outer),
        [spot],
        [tokens, gain],
        deps,
        (ROW_STEPS,),
        [spec, whole_block(gain)],
        [spec, spec],
        [jax.ShapeDtypeStruct(tokens.shape, bf16)] * 2,
        us=3,
    )


def to_order(spot, outer, array, deps):
    spec = rows_spec(*array.shape)
    return launch(
        functools.partial(turn_kernel, outer),
        [spot],
        [array],
        deps,
        (ROW_STEPS,),
        [spec],
        spec,
        jax.ShapeDtypeStruct(array.shape, bf16),
        us=3,
    )


def middle_kernel(tokens_ref, own_ref, other_ref, gain_ref, normed_ref, middle_ref):
    middle = tokens_ref[...].astype(f32) + own_ref[...] + other_ref[...].astype(f32)
    middle_ref[...] = middle
    normed_ref[...] = (middle * inverse_rms(middle) * gain_ref[...]).astype(bf16)


def middle_forward(tokens, own, other, gain, deps):
    spec = rows_spec(*tokens.shape)
    return launch(
        middle_kernel,
        [],
        [tokens, own, other, gain],
        deps,
        (ROW_STEPS,),
        [spec, spec, spec, whole_block(gain)],
        [spec, spec],
        [jax.ShapeDtypeStruct(tokens.shape, bf16), jax.ShapeDtypeStruct(tokens.shape, f32)],
        us=5,
    )


def gain_part(part_ref, product):
    @pl.when(pl.program_id(0) == 0)
    def _():
        part_ref[...] = jnp.zeros_like(part_ref)

    part_ref[...] += jnp.sum(product, axis=0, keepdims=True)


def middle_back_kernel(own_ref, other_ref, middle_ref, grad_ref, gain_ref, low_ref, out_ref, part_ref):
    incoming = own_ref[...] + other_ref[...].astype(f32)
    middle = middle_ref[...]
    inverse = inverse_rms(middle)
    out = grad_ref[...].astype(f32) + norm_back(middle, inverse, gain_ref[...], incoming)
    out_ref[...] = out
    low_ref[...] = out.astype(bf16)
    gain_part(part_ref, incoming * middle * inverse)


def middle_backward(own, other, middle, out_grad, gain, deps):
    spec = rows_spec(*own.shape)
    part = jax.ShapeDtypeStruct(gain.shape, f32)
    return launch(
        middle_back_kernel,
        [],
        [own, other, middle, out_grad, gain],
        deps,
        (ROW_STEPS,),
        [spec, spec, spec, spec, whole_block(gain)],
        [spec, spec, whole_block(gain)],
        [jax.ShapeDtypeStruct(own.shape, bf16), jax.ShapeDtypeStruct(own.shape, f32), part],
        us=8,
    )


def leave(outer, spot_ref, out_ref, value):
    value = value.astype(bf16)
    if outer:
        for here, there in reorder(spot_ref, outer, value.shape[1]):
            out_ref[:, there] = value[:, here]
    else:
        out_ref[...] = value


def block_out_kernel(outer, spot_ref, middle_ref, own_ref, other_ref, out_ref):
    leave(outer, spot_ref, out_ref, middle_ref[...] + own_ref[...] + other_ref[...].astype(f32))


def block_result(spot, outer, middle, own, other, deps):
    spec = rows_spec(*own.shape)
    return launch(
        functools.partial(block_out_kernel, outer),
        [spot],
        [middle, own, other],
        deps,
        (ROW_STEPS,),
        [spec, spec, spec],
        spec,
        jax.ShapeDtypeStruct(own.shape, bf16),
        us=5,
    )


def input_back_kernel(outer, spot_ref, own_ref, other_ref, tokens_ref, grad_ref, gain_ref, out_ref, part_ref):
    incoming = own_ref[...] + other_ref[...].astype(f32)
    inputs = tokens_ref[...].astype(f32)
    inverse = inverse_rms(inputs)
    leave(outer, spot_ref, out_ref, grad_ref[...] + norm_back(inputs, inverse, gain_ref[...], incoming))
    gain_part(part_ref, incoming * inputs * inverse)


def input_backward(spot, outer, own, other, tokens, middle_grad, gain, deps):
    spec = rows_spec(*own.shape)
    return launch(
        functools.partial(input_back_kernel, outer),
        [spot],
        [own, other, tokens, middle_grad, gain],
        deps,
        (ROW_STEPS,),
        [spec, spec, spec, spec, whole_block(gain)],
        [spec, whole_block(gain)],
        [jax.ShapeDtypeStruct(own.shape, bf16), jax.ShapeDtypeStruct(gain.shape, f32)],
        us=7,
    )


class Order:
    def __init__(self):
        self.before = []

    def wait(self, *arrays):
        self.before += arrays

    def __call__(self, compute, *operands, **options):
        result = compute(*operands, deps=self.before, **options)
        self.before = [result[0] if isinstance(result, (tuple, list)) else result]
        return result


def chunk_edges(width):
    blocks = width // BLOCK
    return [BLOCK * (-(-blocks * i // CHUNKS)) for i in range(CHUNKS + 1)]


def make_shards(outer):
    def relative(array):
        rows, width = array.shape
        blocks = array.reshape(rows, outer, 2, 2, width // (4 * outer))
        blocks = jnp.where(lax.axis_index("x") == 0, blocks, blocks[:, :, ::-1])
        blocks = jnp.where(lax.axis_index("core") == 0, blocks, blocks[:, :, :, ::-1])
        return blocks.transpose(0, 3, 2, 1, 4).reshape(rows, width)

    def natural(array):
        rows, width = array.shape
        blocks = array.reshape(rows, 2, 2, outer, width // (4 * outer)).transpose(0, 3, 2, 1, 4)
        blocks = jnp.where(lax.axis_index("x") == 0, blocks, blocks[:, :, ::-1])
        blocks = jnp.where(lax.axis_index("core") == 0, blocks, blocks[:, :, :, ::-1])
        return blocks.reshape(rows, width)

    def over_x(array):
        return lax.ppermute(array, "x", SWAP)

    def over_core(array):
        return lax.ppermute(array, "core", SWAP)

    def gather(operand):
        return lax.all_gather(operand, ("core", "z"), axis=0, tiled=True)

    def scatter(operand):
        return lax.psum_scatter(operand, "z", scatter_dimension=0, tiled=True)

    def total(vector):
        for axis in ("core", "x", "tensor"):
            vector = vector + lax.ppermute(vector, axis, SWAP)
        step = 1
        while step < outer:
            vector = vector + lax.ppermute(vector, "z", [(i, i ^ step) for i in range(outer)])
            step *= 2
        return vector

    def swap(own):
        return lax.ppermute(own, "tensor", SWAP)

    def shards(
        tokens,
        segments,
        q_weight,
        k_weight,
        v_weight,
        o_weight,
        attention_gain,
        gate_weight,
        up_weight,
        down_weight,
        feed_gain,
        out_grad,
    ):
        query_width = q_weight.shape[1]
        key_width = k_weight.shape[1]
        score_scale = HEAD_DIM ** (-0.5)
        place, core, cross = (lax.axis_index(axis) for axis in ("tensor", "core", "x"))
        spot = jnp.stack([place, core, cross]).astype(jnp.int32)
        here = jnp.zeros_like(spot)
        edges = chunk_edges(gate_weight.shape[1])
        order = Order()
        along, full = {}, {}

        def spread(name):
            full[name] = over_x(order(lambda deps: own_rows(spot, along[name], deps)))

        def land(name):
            across = order(lambda deps: gate(full[name], deps))
            full[name] = (along[name], across, over_core(across))

        def chunk(i):
            columns = slice(edges[i], edges[i + 1])
            parts = [w[:, columns] for w in (gate_weight, up_weight, down_weight)]
            along[i] = gather(order(lambda deps: stack(parts, deps)))

        tiles = outer if tokens.shape[1] // (4 * outer) % 128 == 0 else 0
        along["qkv"] = gather(order(lambda deps: stack([q_weight, k_weight, v_weight], deps)))
        along["o"] = gather(order(lambda deps: stack([o_weight], deps)))
        for i in range(CHUNKS):
            chunk(i)
        attention_gain = relative(attention_gain[None])
        feed_gain = relative(feed_gain[None])
        if not tiles:
            tokens, out_grad = relative(tokens), relative(out_grad)
        tokens, normed_first = order(lambda deps: enter(spot, tiles, tokens, attention_gain, deps))
        normed_other = swap(normed_first)
        segment_row = segments[0]
        cosine, sine = rotary_tables(segment_row)
        first_seen = first_blocks(segment_row)
        spread("qkv")
        if tiles:
            out_grad = order(lambda deps: to_order(spot, tiles, out_grad, deps))
        grad_other = swap(out_grad)
        order.wait(cosine, sine, first_seen)
        normed_seq = order(lambda deps: join(spot, normed_first, normed_other, deps))
        land("qkv")
        spread("o")
        rotated = order(
            lambda deps: project(
                spot, normed_first, normed_other, full["qkv"], deps, (cosine, sine),
                (query_width + key_width) // 128,
            )
        )
        mixed, log_totals = order(
            lambda deps: attend(rotated, query_width, first_seen, segment_row, score_scale, deps)
        )
        land("o")
        grad_seq = order(lambda deps: join(here, out_grad, grad_other, deps))
        own, sent = order(lambda deps: back(spot, (mixed,), ((full["o"], 0),), deps, True))
        other = swap(sent)
        spread(0)
        normed_second, middle = order(lambda deps: middle_forward(tokens, own, other, feed_gain, deps))
        normed_third = swap(normed_second)
        spread(1)
        land(0)
        normed_feed = order(lambda deps: join(here, normed_second, normed_third, deps))
        hidden, gate_grad, up_grad = {}, {}, {}
        from_core, to_x, from_x, kept, summed = {}, {}, {}, {}, {}

        def run_feed(i):
            hidden[i], gate_grad[i], up_grad[i] = order(
                lambda deps: feed(spot, normed_feed, grad_seq, full[i], deps)
            )

        def core_part(i):
            grads = (gate_grad[i], up_grad[i], hidden[i])
            part = order(lambda deps: grad((normed_feed, grad_seq), (0, 0, 1), grads, deps))
            from_core[i] = over_core(part)

        def x_part(i):
            grads = (gate_grad[i], up_grad[i], hidden[i])
            to_x[i], kept[i] = order(
                lambda deps: grad((normed_feed, grad_seq), (0, 0, 1), grads, deps, from_core[i])
            )

        def send_x(i):
            from_x[i] = over_x(to_x[i])

        def finish(i, us=4):
            summed[i] = scatter(order(lambda deps: add(kept[i], from_x[i], deps, us)))

        def feed_back(chunks):
            acts = [a[i] for i in chunks for a in (gate_grad, up_grad)]
            weights = [(full[i], at) for i in chunks for at in (0, 1)]
            return order(lambda deps: back(spot, acts, weights, deps))

        run_feed(0)
        core_part(0)
        spread(2)
        land(1)
        run_feed(1)
        core_part(1)
        spread(3)
        x_part(0)
        sent_along, kept_along = scatter(to_x[0]), scatter(kept[0])
        land(2)
        run_feed(2)
        x_part(1)
        send_x(1)
        core_part(2)
        land(3)
        run_feed(3)
        from_along = over_x(order(lambda deps: gate(sent_along, deps)))
        own, sent = feed_back(range(CHUNKS))
        other = swap(sent)
        x_part(2)
        send_x(2)
        core_part(3)
        order.wait(from_along, kept_along)
        finish(1)
        attn_out_grad, middle_grad, feed_gain_part = order(
            lambda deps: middle_backward(own, other, middle, out_grad, feed_gain, deps)
        )
        attn_other = swap(attn_out_grad)
        x_part(3)
        send_x(3)
        block_own, block_sent = order(
            lambda deps: back(
                spot, [hidden[i] for i in range(CHUNKS)], [(full[i], 2) for i in range(CHUNKS)], deps
            )
        )
        block_other = swap(block_sent)
        finish(2)
        attn_grad_seq = order(lambda deps: join(spot, attn_out_grad, attn_other, deps))
        from_core["o"] = over_core(order(lambda deps: grad((attn_grad_seq,), (0,), (mixed,), deps)))
        mixed_grad = order(lambda deps: project(spot, attn_out_grad, attn_other, full["o"], deps))
        to_x["o"], kept["o"] = order(
            lambda deps: grad((attn_grad_seq,), (0,), (mixed,), deps, from_core["o"])
        )
        send_x("o")
        finish(3)
        qkv_grad = order(
            lambda deps: attend_back(
                rotated, mixed_grad, log_totals, query_width, first_seen, segment_row, cosine, sine,
                score_scale, deps,
            )
        )
        from_core["qkv"] = over_core(
            order(lambda deps: grad((normed_seq,), (0,) * 3, qkv_grad, deps, us=SHORT))
        )
        order.wait(summed[3])
        finish("o")
        to_x["qkv"], kept["qkv"] = order(
            lambda deps: grad((normed_seq,), (0,) * 3, qkv_grad, deps, from_core["qkv"])
        )
        send_x("qkv")
        places = (0, query_width // key_width, query_width // key_width + 1)
        own, sent = order(
            lambda deps: back(spot, qkv_grad, [(full["qkv"], at) for at in places], deps, True)
        )
        other = swap(sent)
        summed[0] = order(lambda deps: add(kept_along, from_along, deps, kind=f32))
        block_out = order(lambda deps: block_result(spot, tiles, middle, block_own, block_other, deps))
        order.wait(summed["o"])
        finish("qkv")
        input_grad, attention_gain_part = order(
            lambda deps: input_backward(spot, tiles, own, other, tokens, middle_grad, attention_gain, deps)
        )
        gains = total(natural(jnp.concatenate([attention_gain_part, feed_gain_part], axis=0)))
        if not tiles:
            block_out, input_grad = natural(block_out), natural(input_grad)
        qkv_weight_grad = summed["qkv"].astype(f32)

        def whole(at):
            parts = []
            for i in range(CHUNKS):
                units = edges[i + 1] - edges[i]
                parts.append(summed[i][:, at * units : at * units + units].astype(f32))
            return jnp.concatenate(parts, axis=1)

        return (
            block_out,
            input_grad,
            qkv_weight_grad[:, :query_width],
            qkv_weight_grad[:, query_width : query_width + key_width],
            qkv_weight_grad[:, query_width + key_width :],
            summed["o"].astype(f32),
            gains[0],
            whole(0),
            whole(1),
            whole(2),
            gains[1],
        )

    return shards


def solution(mesh):
    outer = mesh.shape["dp"] // 4
    fine = Mesh(
        mesh.devices.reshape(outer, 2, 2, mesh.shape["tensor"]), ("z", "x", "core", "tensor")
    )
    dp = ("z", "x", "core")
    every = P(dp + ("tensor",), None)
    weight = P(dp, "tensor")
    return jax.shard_map(
        make_shards(outer),
        mesh=fine,
        in_specs=(
            every,
            P(dp, None),
            weight,
            weight,
            weight,
            weight,
            P(),
            weight,
            weight,
            weight,
            P(),
            every,
        ),
        out_specs=(every, every, weight, weight, weight, weight, P(), weight, weight, weight, P()),
        check_vma=False,
    )
```
